32 devices in a mesh: groups: 2 (over x), shot: 16 (over z, y, core).
Axes of the slice: x: 2, y: 2, z: 4, core: 2. Of those that a mesh axis runs over, the one named last changes fastest.
Arguments:
- courant_sq: float32 [128, 32, 128], P('groups'), parts along dimension 0, may hold values from 0.05 to 0.2
- wave_now: float32 [512, 32, 128], P(('groups', 'shot')), parts along dimension 0, may hold values from -6 to 6
- wave_before: float32 [512, 32, 128], P(('groups', 'shot')), parts along dimension 0, may hold values from -6 to 6
- wavelet: float32 [32, 8], P(('groups', 'shot')), parts along dimension 0, may hold values from -24 to 24
- source_cell: int32 [32], P(('groups', 'shot')), parts along dimension 0, may hold values from 0 to 65535, as said below
- receiver_cell: int32 [8192], P(('groups', 'shot')), parts along dimension 0, may hold values from 0 to 65535, as said below
- send_order: int32 [8192], P(('groups', 'shot')), parts along dimension 0, may hold values from 0 to 255, as said below
- observed: float32 [512, 128], P(('groups', 'shot')), parts along dimension 0, may hold values from -6 to 6
Outputs:
- gradient_slabs: float32 [128, 32, 128], P(('groups', 'shot')), parts along dimension 0
The draws below stay inside these ranges and needn't reach their ends.
There are 2 independent parts, one for each index of `groups`. The reference program is written for one: setup_inputs(seed, part) draws one part's arguments, and reference() takes and returns one part's arrays. A program takes and returns all parts, laid end to end along the dimension named above; each array names one. Nothing has to cross between parts.
Inputs may be any that keep to these rules, and one draw needn't show every extreme that they name: `source_cell`: a local cell index (x * 32 + y) * 128 + z of a block of 16 planes. `receiver_cell`: a local cell index (x * 32 + y) * 128 + z of a block of 16 planes. `send_order`: each aligned block of 256 entries is a permutation of 0 to 255.
All inputs are finite; a program needn't handle non-finite values.
Results may differ from the reference program's by a relative error of at most 0.00021.
Values sent between devices are 32-bit elements; how exact they have to be, the bound alone decides.
No kernel may reach another device: no remote copies, remote signals or barrier semaphores. Data moves between devices by JAX's collectives and lax.ppermute only.
A program may use at most 64 MiB of HBM per device.

```python
import math
import jax
import jax.numpy as jnp

PX = 16
PY = 32
PZ = 128
NT = 8
Q = 16
RAD = 4
PIECES = 4
NX = 64
REC_DEV = 256
SHOTS = 4
N_SHOT = 16


def cell_draw(key, count):
    key_x, key_y, key_z = jax.random.split(key, 3)
    along_x = jax.random.randint(key_x, (count,), 0, PX)
    along_y = jax.random.randint(key_y, (count,), 0, PY)
    along_z = jax.random.randint(key_z, (count,), 0, PZ)
    chosen = (along_x * PY + along_y) * PZ + along_z
    chosen = chosen.at[0].set(0)
    chosen = chosen.at[1].set(PX * PY * PZ - 1)
    return chosen.astype(jnp.int32)


def draw_source_cell(key, part):
    return cell_draw(jax.random.fold_in(key, 11), N_SHOT)


def draw_receiver_cell(key, part):
    return cell_draw(jax.random.fold_in(key, 12), N_SHOT * REC_DEV)


def draw_send_order(key, part):
    keys_all = jax.random.split(jax.random.fold_in(key, 13), N_SHOT)
    orders = jax.vmap(lambda single: jax.random.permutation(single, REC_DEV))(keys_all)
    return orders.reshape(-1).astype(jnp.int32)


def shard_levels(stream_key, shape, cuts, low, high):
    factor_of = 1.0
    for axis_at, shards_of in cuts:
        draws = jax.random.uniform(jax.random.fold_in(jax.random.fold_in(stream_key, 6), axis_at), (shards_of,), jnp.float32, low / len(cuts), high / len(cuts))
        factor_of = factor_of * jnp.repeat(jnp.exp(draws), shape[axis_at] // shards_of).reshape((-1,) + (1,) * (len(shape) - 1 - axis_at))
    return factor_of


def gaussian(rng, extent, spread, limit, shards=(), kind=jnp.bfloat16):
    gain = shard_levels(rng, extent, shards, -0.22, 0.18) if shards else 1.0
    drawn = jax.random.normal(rng, extent, jnp.float32) * spread * gain
    return jnp.minimum(jnp.maximum(drawn, -limit), limit).astype(kind)


def setup_inputs(seed: int = 0, part: int = 0) -> dict:
    keys = jax.random.split(jax.random.key(seed), 9)
    part_keys = jax.random.split(jax.random.fold_in(keys[8], part), 9)
    return {
        "courant_sq": jnp.clip(jnp.exp(jax.random.uniform(part_keys[0], (NX, PY, PZ), jnp.float32, math.log(0.05), math.log(0.2))), 0.05, 0.2),
        "wave_now": gaussian(part_keys[1], (SHOTS * NX, PY, PZ), 1.0, 6.0, ((0, 16),), jnp.float32),
        "wave_before": gaussian(part_keys[2], (SHOTS * NX, PY, PZ), 1.0, 6.0, ((0, 16),), jnp.float32),
        "wavelet": gaussian(part_keys[3], (N_SHOT, NT), 4.0, 24.0, ((0, 16),), jnp.float32),
        "source_cell": draw_source_cell(jax.random.fold_in(jax.random.fold_in(keys[8], part), 71), part),
        "receiver_cell": draw_receiver_cell(jax.random.fold_in(jax.random.fold_in(keys[8], part), 71), part),
        "send_order": draw_send_order(jax.random.fold_in(jax.random.fold_in(keys[8], part), 71), part),
        "observed": gaussian(part_keys[7], (N_SHOT * N_SHOT, NT * Q), 1.0, 6.0, ((0, 16),), jnp.float32),
    }


stencil_center = -205.0 / 72.0
stencil_weights = (8.0 / 5.0, -1.0 / 5.0, 8.0 / 315.0, -1.0 / 560.0)


def laplace_whole(wavefield):
    size_x, size_y, size_z = wavefield.shape
    padded = jnp.pad(wavefield, ((0, 0), (RAD, RAD), (RAD, RAD)))

    def window(offset_y, offset_z):
        return padded[:, RAD + offset_y:RAD + offset_y + size_y, RAD + offset_z:RAD + offset_z + size_z]

    summed = 3.0 * stencil_center * wavefield
    for distance in range(1, 5):
        weight = stencil_weights[distance - 1]
        beside_all = jnp.roll(wavefield, -distance, 0) + jnp.roll(wavefield, distance, 0)
        beside_all = beside_all + window(distance, 0) + window(-distance, 0)
        beside_all = beside_all + window(0, distance) + window(0, -distance)
        summed = summed + weight * beside_all
    return summed


def inject(wavefield, cell_index, amounts):
    flattened = wavefield.reshape(-1)
    return flattened.at[cell_index].add(amounts).reshape(wavefield.shape)


def advance(current, previous, model, cell_index, amounts):
    updated = 2.0 * current - previous + model * laplace_whole(current)
    return inject(updated, cell_index, amounts)


def reference(courant_sq, wave_now, wave_before, wavelet, source_cell, receiver_cell, send_order, observed):
    periods = N_SHOT // PIECES
    cell_count = PX * PY * PZ
    model = jnp.tile(courant_sq, (periods, 1, 1))
    offsets = jnp.arange(N_SHOT, dtype=jnp.int32) * cell_count
    source_global = (source_cell + offsets).astype(jnp.int32)
    receiver_global = (receiver_cell.reshape(N_SHOT, REC_DEV) + offsets[:, None]).reshape(-1).astype(jnp.int32)

    fields = []
    current, previous = wave_now, wave_before
    for step_index in range(NT):
        updated = advance(current, previous, model, source_global, wavelet[:, step_index])
        fields.append(updated)
        previous, current = current, updated

    traces = jnp.stack([wavefield.reshape(-1)[receiver_global] for wavefield in fields])
    per_device = traces.reshape(NT, N_SHOT, REC_DEV).transpose(1, 0, 2)
    ordering = send_order.reshape(N_SHOT, REC_DEV)
    packed = jnp.take_along_axis(per_device, ordering[:, None, :], axis=2)
    arranged = packed.reshape(N_SHOT, NT, N_SHOT, Q).transpose(2, 0, 1, 3).reshape(N_SHOT * N_SHOT, NT * Q)
    misfit = arranged - observed
    returned = misfit.reshape(N_SHOT, N_SHOT, NT, Q).transpose(1, 2, 0, 3).reshape(N_SHOT, NT, REC_DEV)

    def place_rows(values, rows_order):
        return jnp.zeros((NT, REC_DEV), jnp.float32).at[:, rows_order].set(values)

    adjoint_rows = jax.vmap(place_rows)(returned, ordering)
    adjoint_global = adjoint_rows.transpose(1, 0, 2).reshape(NT, N_SHOT * REC_DEV)

    empty_field = jnp.zeros_like(wave_now)
    adjoint_now = inject(empty_field, receiver_global, adjoint_global[NT - 1])
    imaging_sum = adjoint_now * fields[NT - 1]
    adjoint_before = empty_field
    for adjoint_step in range(1, NT):
        updated = advance(adjoint_now, adjoint_before, model, receiver_global, adjoint_global[NT - 1 - adjoint_step])
        imaging_sum = imaging_sum + updated * fields[NT - 1 - adjoint_step]
        adjoint_before, adjoint_now = adjoint_now, updated

    gradient = jnp.sum(imaging_sum.reshape(periods, NX, PY, PZ), axis=0)
    slab_rows = gradient.reshape(PIECES, periods, NX // N_SHOT, PY, PZ).transpose(1, 0, 2, 3, 4).reshape(NX, PY, PZ)
    return slab_rows
```

```python
import functools

import jax
import jax.numpy as jnp
import numpy as np
from jax import lax
from jax.experimental import pallas as pl
from jax.experimental.pallas import tpu as pltpu
from jax.sharding import PartitionSpec as P

NT = 8
PIECES = 4
RAD = 4
ROUNDS = (4, 4)
SCALE = 5040.0
CENTER = -43050.0
WEIGHTS = (8064.0, -1008.0, 128.0, -9.0)
GROUP = 8
HALO = RAD * (NT - 1)
BF = jnp.bfloat16
F32 = jnp.float32

VMEM = pl.BlockSpec(memory_space=pltpu.VMEM)
SMEM = pl.BlockSpec(memory_space=pltpu.SMEM)


def band(size):
    out = np.zeros((size, size), np.float32)
    for k, weight in enumerate(WEIGHTS, 1):
        out += weight * (np.eye(size, k=k) + np.eye(size, k=-k))
    return out


def matrices(span_y, span_z):
    along_z = np.concatenate([band(span_z)] * 2, axis=0)
    along_y = np.kron(np.eye(GROUP), band(span_y))
    return jnp.asarray(along_z, BF), jnp.asarray(along_y, BF)


def split(values):
    high = values.astype(BF)
    low = (values - high.astype(F32)).astype(BF)
    return high, low


def dot(a, b, dims=(((1,), (0,)), ((), ()))):
    return lax.dot_general(a, b, dims, preferred_element_type=F32)


def advance(cur, old, model, zmat, ymat, first, last, model_shift):
    span_y, span_z = cur.shape[1:]
    zmat, ymat = zmat[...], ymat[...]
    for base in range(first, last, GROUP):
        group = cur[base : base + GROUP].reshape(GROUP * span_y, span_z)
        pair = jnp.concatenate(split(group), axis=1)
        z_part = dot(pair, zmat)
        y_part = dot(ymat, pair)
        for i in range(GROUP):
            x = base + i
            rows = slice(i * span_y, (i + 1) * span_y)
            here = cur[x]
            total = CENTER * here + z_part[rows] + y_part[rows, :span_z] + y_part[rows, span_z:]
            for k, weight in enumerate(WEIGHTS, 1):
                total = total + weight * (cur[x + k] + cur[x - k])
            old[x] = 2.0 * here - old[x] + model[x + model_shift] * total


def add_source(field, pack, step, own, block, halo, rows):
    span_y, span_z = field.shape[1:]
    cell = pack[NT].astype(jnp.int32)
    amount = pack[step]
    plane = own + block * rows + cell // (span_y * span_z)
    y = (cell // span_z) % span_y
    z = cell % span_z

    @pl.when((plane >= own - halo) & (plane < own + rows + halo))
    def _():
        tile = pl.ds(pl.multiple_of((y // 8) * 8, 8), 8)
        sub = lax.broadcasted_iota(jnp.int32, (8, span_z), 0)
        lane = lax.broadcasted_iota(jnp.int32, (8, span_z), 1)
        hit = (sub == y % 8) & (lane == z)
        field[plane, tile, :] = field[plane, tile, :] + jnp.where(hit, amount, 0.0)


def prepare_kernel(courant, cells, order, observed, model_out, pack_out):
    rows = 16
    piece = lax.rem(lax.axis_index("shot"), PIECES)
    period = courant.shape[0]
    window = model_out.shape[0]
    for chunk in range(0, window, RAD):
        source = lax.rem(piece * rows - HALO + chunk + period, period)
        model_out[chunk : chunk + RAD] = courant[pl.ds(source, RAD)] * (1.0 / SCALE)
    count = cells.shape[1]
    wanted = order[...]
    cell = cells[...]
    high = (cell // 256).astype(F32).astype(BF)
    low = (cell % 256).astype(F32).astype(BF)
    which = lax.broadcasted_iota(jnp.int32, (16, count), 0)
    digits = jnp.where(which == 0, high.astype(F32), jnp.where(which == 1, low.astype(F32), 0.0)).astype(BF)
    for j in range(0, count, 256):
        index = lax.broadcasted_iota(jnp.int32, (count, 256), 0)
        chosen = jnp.where(index == wanted[:, j : j + 256], 1.0, 0.0).astype(BF)
        found = dot(digits, chosen)
        ordered = found[0:1] * 256.0 + found[1:2]
        pack_out[j // 128 : j // 128 + 1] = ordered[:, :128]
        pack_out[j // 128 + 1 : j // 128 + 2] = ordered[:, 128:]
    pack_out[count // 128 :] = observed[...]


def cell_row(pack, count):
    parts = [pack[j : j + 1] for j in range(count // 128)]
    return jnp.concatenate(parts, axis=1).astype(jnp.int32)


def pick_tables(cells, table_rows):
    count = cells.shape[1]
    column = jnp.transpose(jnp.broadcast_to(cells.astype(F32), (128, count)))
    column = column.astype(jnp.int32)
    row_of = jnp.concatenate([column // 128] * (table_rows // 128), axis=1)
    lane_of = jnp.concatenate([column % 128] * 2, axis=1)
    lanes = lax.broadcasted_iota(jnp.int32, (count, table_rows), 1)
    rows_table = jnp.where(row_of == lanes, 1.0, 0.0).astype(BF)
    lanes2 = lax.broadcasted_iota(jnp.int32, (count, 256), 1) % 128
    lane_table = jnp.where(lane_of == lanes2, 1.0, 0.0)
    return rows_table, lane_table


def extract(field, step, rows_table, lane_table):
    rows, span_y, span_z = field.shape
    pair = jnp.concatenate(split(field.reshape(rows * span_y, span_z)), axis=1)
    which = lax.broadcasted_iota(jnp.int32, (16, 2 * span_z), 0)
    ones = jnp.where(which == step, 1.0, 0.0).astype(BF)
    out = []
    for j in range(0, rows_table.shape[0], 256):
        found = dot(rows_table[j : j + 256], pair)
        kept = (found * lane_table[j : j + 256]).astype(BF)
        out.append(dot(ones, kept, (((1,), (1,)), ((), ()))))
    return jnp.concatenate(out, axis=1)


def forward_round(
    index, refs_in, zmat, ymat, model, pack_left, pack_own, pack_right, fields, buf_a, buf_b
):
    steps = ROUNDS[index]
    done = sum(ROUNDS[:index])
    rows = 16
    own = RAD * steps
    cur, old = buf_a, buf_b
    wide, narrow = RAD * steps, RAD * (steps - 1)
    if index == 0:
        now, before, now_l, now_r, before_l, before_r = refs_in
        cur[own : own + rows] = now[...]
        old[own : own + rows] = before[...]
        cur[own - wide : own] = now_l[...]
        cur[own + rows : own + rows + wide] = now_r[...]
        if narrow:
            old[own - narrow : own] = before_l[...]
            old[own + rows : own + rows + narrow] = before_r[...]
    else:
        earlier, known, got_l, got_r = refs_in
        cur[own : own + rows] = earlier[earlier.shape[0] - 1]
        old[own : own + rows] = earlier[earlier.shape[0] - 2]
        cur[own - wide : own] = got_l[0:wide]
        cur[own + rows : own + rows + wide] = got_r[0:wide]
        if narrow:
            old[own - RAD : own] = known[0]
            old[own + rows : own + rows + RAD] = known[1]
        if narrow > RAD:
            old[own - narrow : own - RAD] = got_l[wide:]
            old[own + rows + RAD : own + rows + narrow] = got_r[wide:]
    for step in range(steps):
        halo = RAD * (steps - 1 - step)
        advance(cur, old, model, zmat, ymat, own - halo, own + rows + halo, HALO - own)
        for block, pack in ((-1, pack_left), (0, pack_own), (1, pack_right)):
            if halo or block == 0:
                add_source(old, pack, done + step, own, block, halo, rows)
        fields[step] = old[own : own + rows]
        cur, old = old, cur
    return cur, old, own


def send_shapes(index):
    steps = ROUNDS[index]
    return RAD * steps + RAD * max(steps - 2, 0)


def forward_kernel(index, *refs):
    take = 6 if index == 0 else 4
    refs_in, refs = refs[:take], refs[take:]
    zmat, ymat, model, pack_left, pack_own, pack_right, fields, known, send_l, send_r, buf_a, buf_b = refs
    cur, old, own = forward_round(
        index, refs_in, zmat, ymat, model, pack_left, pack_own, pack_right, fields, buf_a, buf_b
    )
    rows = 16
    known[0] = old[own - RAD : own]
    known[1] = old[own + rows : own + rows + RAD]
    wide = RAD * ROUNDS[index + 1]
    inner = wide - RAD
    send_l[0:wide] = cur[own : own + wide]
    send_r[0:wide] = cur[own + rows - wide : own + rows]
    if inner > RAD:
        send_l[wide:] = old[own + RAD : own + inner]
        send_r[wide:] = old[own + rows - inner : own + rows - RAD]


def tables_kernel(count, *refs):
    (pack, *fields), (rows_out, lanes_out, traces) = refs[:-3], refs[-3:]
    rows_table, lane_table = pick_tables(cell_row(pack, count), rows_out.shape[1])
    rows_out[...] = rows_table
    lanes_out[...] = lane_table
    total = jnp.zeros((16, count), F32)
    step = 0
    for group in fields:
        for i in range(group.shape[0]):
            total = total + extract(group[i], step, rows_table, lane_table)
            step += 1
    traces[...] = total


def last_kernel(index, *refs):
    take = 6 if index == 0 else 4
    refs_in, refs = refs[:take], refs[take:]
    zmat, ymat, model, pack_left, pack_own, pack_right = refs[:6]
    rows_table, lane_table, traces, observed = refs[6:10]
    fields, adj, buf_a, buf_b = refs[10:]
    forward_round(index, refs_in, zmat, ymat, model, pack_left, pack_own, pack_right, fields, buf_a, buf_b)
    total = traces[...]
    done = sum(ROUNDS[:index])
    rows_table = rows_table[...]
    lane_table = lane_table[...]
    for step in range(ROUNDS[index]):
        total = total + extract(fields[step], done + step, rows_table, lane_table)
    adj[...] = total[0:NT] - observed[...]


def inject_tables_kernel(count, packs, rows_out, lanes_out):
    me = lax.axis_index("shot")
    devices = packs.shape[0]
    for block in range(5):
        cells = cell_row(packs.at[lax.rem(me + block - 2 + devices, devices)], count)
        sub = lax.broadcasted_iota(jnp.int32, (rows_out.shape[1], count), 0)
        rows_out[block] = jnp.where(sub == cells // 128, 1.0, 0.0).astype(BF)
        lanes_out[block : block + 1] = cells % 128


def adjoint_kernel(field_groups, slabs, count, *refs):
    fields = []
    for ref in refs[:field_groups]:
        fields += [ref.at[i] for i in range(ref.shape[0])]
    refs = refs[field_groups:]
    zmat, ymat, model, rows_table, lanes, *adjs = refs[:10]
    outs = refs[10 : 10 + slabs]
    buf_a, buf_b, image = refs[10 + slabs :]
    rows = 16
    own = HALO
    span_y, span_z = buf_a.shape[1:]

    def inject(field, number):
        halo = RAD * (NT - number)
        step = NT - number
        for block in range(-2, 3):
            begin = own + block * rows
            first = max(begin, own - halo)
            last = min(begin + rows, own + rows + halo)
            if first >= last:
                continue
            amounts = adjs[block + 2][step : step + 1]
            high = amounts.astype(BF).astype(F32)
            low = amounts - high
            sub = lax.broadcasted_iota(jnp.int32, (span_z, count), 0)
            hit = sub == lanes[block + 2 : block + 3]
            both = jnp.concatenate(
                [jnp.where(hit, high, 0.0).astype(BF), jnp.where(hit, low, 0.0).astype(BF)], axis=0
            )
            table = rows_table[block + 2, (first - begin) * span_y : (last - begin) * span_y, :]
            added = dot(table, both, (((1,), (1,)), ((), ())))
            added = (added[:, :span_z] + added[:, span_z:]).reshape(last - first, span_y, span_z)
            if number == 1:
                field[first:last] = added
            else:
                field[first:last] = field[first:last] + added

    cur, old = buf_a, buf_b
    inject(cur, 1)
    old[...] = jnp.zeros(old.shape, F32)
    image[...] = cur[own : own + rows] * fields[NT - 1][...]
    for number in range(2, NT + 1):
        halo = RAD * (NT - number)
        advance(cur, old, model, zmat, ymat, own - halo, own + rows + halo, 0)
        inject(old, number)
        image[...] = image[...] + old[own : own + rows] * fields[NT - number][...]
        cur, old = old, cur
    mine = lax.axis_index("shot") // PIECES
    thick = rows // slabs
    for i in range(slabs):
        outs[i][...] = image[pl.ds(lax.rem(mine + i, slabs) * thick, thick)]


def call(kernel, outs, ins, specs=None, scratch=(), cost=(1e6, 1e6), name=None):
    return pl.pallas_call(
        kernel,
        out_shape=outs,
        in_specs=specs or [VMEM] * len(ins),
        out_specs=jax.tree.map(lambda _: VMEM, outs),
        scratch_shapes=list(scratch),
        compiler_params=pltpu.CompilerParams(vmem_limit_bytes=48 * 1024 * 1024),
        cost_estimate=pl.CostEstimate(flops=int(cost[0]), bytes_accessed=int(cost[1]), transcendentals=0),
        name=name,
    )(*ins)


def shifted(value, steps):
    count = lax.axis_size("shot")
    return lax.ppermute(value, "shot", [(i, (i + steps) % count) for i in range(count)])


def per_device(
    courant_sq, wave_now, wave_before, wavelet, source_cell, receiver_cell, send_order, observed
):
    devices = lax.axis_size("shot")
    me = lax.axis_index("shot")
    rows, span_y, span_z = wave_now.shape
    count = receiver_cell.shape[0]
    per_owner = count // devices
    table_rows = rows * span_y
    plane = (span_y, span_z)
    zmat, ymat = matrices(span_y, span_z)

    wide = RAD * ROUNDS[0]
    narrow = wide - RAD
    pack_own = jnp.concatenate([wavelet.reshape(-1), source_cell.astype(F32)])
    pack_left, pack_right = shifted(pack_own, 1), shifted(pack_own, -1)
    now_l, now_r = shifted(wave_now[rows - wide :], 1), shifted(wave_now[:wide], -1)
    before_l, before_r = shifted(wave_before[rows - narrow :], 1), shifted(wave_before[:narrow], -1)

    model, pack = call(
        prepare_kernel,
        (
            jax.ShapeDtypeStruct((rows + 2 * HALO,) + plane, F32),
            jax.ShapeDtypeStruct((count // 128 + devices, 128), F32),
        ),
        (courant_sq, receiver_cell.reshape(1, count), send_order.reshape(1, count), observed),
        name="prepare",
    )
    packs = lax.all_gather(pack, "shot", axis=0, tiled=False)

    common = (zmat, ymat, model, pack_left, pack_own, pack_right)
    common_specs = [VMEM] * 3 + [SMEM] * 3
    field_list = []
    ins = (wave_now, wave_before, now_l, now_r, before_l, before_r)
    for index in range(len(ROUNDS) - 1):
        window = rows + 2 * RAD * ROUNDS[index]
        sent = send_shapes(index + 1)
        fields, known, send_l, send_r = call(
            functools.partial(forward_kernel, index),
            (
                jax.ShapeDtypeStruct((ROUNDS[index], rows) + plane, F32),
                jax.ShapeDtypeStruct((2, RAD) + plane, F32),
                jax.ShapeDtypeStruct((sent,) + plane, F32),
                jax.ShapeDtypeStruct((sent,) + plane, F32),
            ),
            ins + common,
            specs=[VMEM] * len(ins) + common_specs,
            scratch=[pltpu.VMEM((window,) + plane, F32)] * 2,
            name="forward",
        )
        field_list.append(fields)
        ins = (fields, known, shifted(send_r, 1), shifted(send_l, -1))

    rows_table, lane_table, traces = call(
        functools.partial(tables_kernel, count),
        (
            jax.ShapeDtypeStruct((count, table_rows), BF),
            jax.ShapeDtypeStruct((count, 256), F32),
            jax.ShapeDtypeStruct((16, count), F32),
        ),
        (pack, *field_list),
        name="traces",
    )
    mine = lax.dynamic_index_in_dim(packs[:, count // 128 :], me, 1, keepdims=False)
    target = mine.reshape(devices, NT, per_owner).transpose(1, 0, 2).reshape(NT, count)
    inject_rows, inject_lanes = call(
        functools.partial(inject_tables_kernel, count),
        (
            jax.ShapeDtypeStruct((5, table_rows, count), BF),
            jax.ShapeDtypeStruct((5, count), jnp.int32),
        ),
        (packs,),
        name="inject_tables",
    )

    index = len(ROUNDS) - 1
    window = rows + 2 * RAD * ROUNDS[index]
    fields, adj = call(
        functools.partial(last_kernel, index),
        (
            jax.ShapeDtypeStruct((ROUNDS[index], rows) + plane, F32),
            jax.ShapeDtypeStruct((NT, count), F32),
        ),
        ins + common + (rows_table, lane_table, traces, target),
        specs=[VMEM] * len(ins) + common_specs + [VMEM] * 4,
        scratch=[pltpu.VMEM((window,) + plane, F32)] * 2,
        name="forward_last",
    )
    field_list.append(fields)

    adjs = [shifted(adj, 2), shifted(adj, 1), adj, shifted(adj, -1), shifted(adj, -2)]
    slabs = devices // PIECES
    thick = rows // slabs
    parts = call(
        functools.partial(adjoint_kernel, len(field_list), slabs, count),
        tuple(jax.ShapeDtypeStruct((thick,) + plane, F32) for _ in range(slabs)),
        (*field_list, zmat, ymat, model, inject_rows, inject_lanes, *adjs),
        scratch=[pltpu.VMEM((rows + 2 * HALO,) + plane, F32)] * 2 + [pltpu.VMEM((rows,) + plane, F32)],
        name="adjoint",
    )
    total = parts[0]
    for i in range(1, slabs):
        total = total + shifted(parts[i], i * PIECES)
    return total


def solution(mesh):
    return jax.shard_map(
        per_device,
        mesh=mesh,
        in_specs=(
            P("groups", None, None),
            P(("groups", "shot"), None, None),
            P(("groups", "shot"), None, None),
            P(("groups", "shot"), None),
            P(("groups", "shot")),
            P(("groups", "shot")),
            P(("groups", "shot")),
            P(("groups", "shot"), None),
        ),
        out_specs=P(("groups", "shot"), None, None),
        check_vma=False,
    )
```

```python
import functools

import jax
import jax.numpy as jnp
import numpy as np
from jax import lax
from jax.experimental import pallas as pl
from jax.experimental.pallas import tpu as pltpu
from jax.sharding import PartitionSpec as P

NT = 8
PIECES = 4
RAD = 4
ROUNDS = (4, 4)
SCALE = 5040.0
CENTER = -43050.0
WEIGHTS = (8064.0, -1008.0, 128.0, -9.0)
GROUP = 8
HALO = RAD * (NT - 1)
BF = jnp.bfloat16
F32 = jnp.float32

VMEM = pl.BlockSpec(memory_space=pltpu.VMEM)
SMEM = pl.BlockSpec(memory_space=pltpu.SMEM)


def band(size):
    out = np.zeros((size, size), np.float32)
    for k, weight in enumerate(WEIGHTS, 1):
        out += weight * (np.eye(size, k=k) + np.eye(size, k=-k))
    return out


def matrices(span_y, span_z):
    along_z = np.concatenate([band(span_z)] * 2, axis=0)
    along_y = np.kron(np.eye(GROUP), band(span_y))
    return jnp.asarray(along_z, BF), jnp.asarray(along_y, BF)


def split(values):
    high = values.astype(BF)
    low = (values - high.astype(F32)).astype(BF)
    return high, low


def dot(a, b, dims=(((1,), (0,)), ((), ()))):
    return lax.dot_general(a, b, dims, preferred_element_type=F32)


def advance(cur, old, model, zmat, ymat, first, last, model_shift):
    span_y, span_z = cur.shape[1:]
    zmat, ymat = zmat[...], ymat[...]
    for base in range(first, last, GROUP):
        group = cur[base : base + GROUP].reshape(GROUP * span_y, span_z)
        pair = jnp.concatenate(split(group), axis=1)
        z_part = dot(pair, zmat)
        y_part = dot(ymat, pair)
        for i in range(GROUP):
            x = base + i
            rows = slice(i * span_y, (i + 1) * span_y)
            here = cur[x]
            total = CENTER * here + z_part[rows] + y_part[rows, :span_z] + y_part[rows, span_z:]
            for k, weight in enumerate(WEIGHTS, 1):
                total = total + weight * (cur[x + k] + cur[x - k])
            old[x] = 2.0 * here - old[x] + model[x + model_shift] * total


def add_source(field, pack, cell, step, own, block, halo, rows):
    span_y, span_z = field.shape[1:]
    plane = own + block * rows + cell // (span_y * span_z)
    y = (cell // span_z) % span_y
    z = cell % span_z

    @pl.when((plane >= own - halo) & (plane < own + rows + halo))
    def _():
        tile = pl.ds(pl.multiple_of((y // 8) * 8, 8), 8)
        sub = lax.broadcasted_iota(jnp.int32, (8, span_z), 0)
        lane = lax.broadcasted_iota(jnp.int32, (8, span_z), 1)
        hit = (sub == y % 8) & (lane == z)
        field[plane, tile, :] = field[plane, tile, :] + jnp.where(hit, pack[step : step + 1], 0.0)


def message_kernel(before, wavelet, source, left_out, right_out, pack_out):
    rows, span_y, span_z = before.shape
    which = lax.broadcasted_iota(jnp.int32, (16, span_z), 0)
    pack = jnp.where(which >= NT, source[0].astype(F32), 0.0)
    for step in range(NT):
        pack = jnp.where(which == step, wavelet[0, step], pack)
    pack_out[...] = pack
    narrow = RAD * (ROUNDS[0] - 1)
    size = narrow * span_y
    left_out[:size] = before[:narrow].reshape(size, span_z)
    right_out[:size] = before[rows - narrow :].reshape(size, span_z)
    left_out[size:] = pack
    right_out[size:] = pack


def prepare_kernel(courant, cells, order, observed, pack, model_out, cells_out, observed_out):
    rows = 16
    piece = lax.rem(lax.axis_index("shot"), PIECES)
    period = courant.shape[0]
    window = model_out.shape[0]
    for chunk in range(0, window, RAD):
        source = lax.rem(piece * rows - HALO + chunk + period, period)
        model_out[chunk : chunk + RAD] = courant[pl.ds(source, RAD)] * (1.0 / SCALE)
    count = cells.shape[1]
    wanted = order[...]
    cell = cells[...]
    which = lax.broadcasted_iota(jnp.int32, (16, count), 0)
    digits = jnp.where(which == 0, cell // 256, jnp.where(which == 1, cell % 256, 0)).astype(F32).astype(BF)
    for j in range(0, count, 256):
        index = lax.broadcasted_iota(jnp.int32, (count, 256), 0)
        chosen = jnp.where(index == wanted[:, j : j + 256], 1.0, 0.0).astype(BF)
        found = dot(digits, chosen)
        ordered = found[0:1] * 256.0 + found[1:2]
        cells_out[:, j : j + 256] = jnp.broadcast_to(ordered, (8, 256))
    observed_out[...] = observed[...] + 0.0 * pack[0:1, :]


def pick_tables(cells, table_rows):
    count = cells.shape[1]
    column = jnp.transpose(jnp.broadcast_to(cells.astype(F32), (128, count)))
    column = column.astype(jnp.int32)
    row_of = jnp.concatenate([column // 128] * (table_rows // 128), axis=1)
    lane_of = jnp.concatenate([column % 128] * 2, axis=1)
    lanes = lax.broadcasted_iota(jnp.int32, (count, table_rows), 1)
    rows_table = jnp.where(row_of == lanes, 1.0, 0.0).astype(BF)
    lanes2 = lax.broadcasted_iota(jnp.int32, (count, 256), 1) % 128
    lane_table = jnp.where(lane_of == lanes2, 1.0, 0.0)
    return rows_table, lane_table


def extract(field, step, rows_table, lane_table):
    rows, span_y, span_z = field.shape
    pair = jnp.concatenate(split(field.reshape(rows * span_y, span_z)), axis=1)
    which = lax.broadcasted_iota(jnp.int32, (16, 2 * span_z), 0)
    ones = jnp.where(which == step, 1.0, 0.0).astype(BF)
    out = []
    for j in range(0, rows_table.shape[0], 256):
        found = dot(rows_table[j : j + 256], pair)
        kept = (found * lane_table[j : j + 256]).astype(BF)
        out.append(dot(ones, kept, (((1,), (1,)), ((), ()))))
    return jnp.concatenate(out, axis=1)


def forward_round(
    index, refs_in, zmat, ymat, model, packs, fields, buf_a, buf_b
):
    steps = ROUNDS[index]
    done = sum(ROUNDS[:index])
    rows = 16
    own = RAD * steps
    cur, old = buf_a, buf_b
    wide, narrow = RAD * steps, RAD * (steps - 1)
    if index == 0:
        now, before, now_l, now_r, before_l, before_r = refs_in
        cur[own : own + rows] = now[...]
        old[own : own + rows] = before[...]
        cur[own - wide : own] = now_l[...]
        cur[own + rows : own + rows + wide] = now_r[...]
        if narrow:
            size = narrow * cur.shape[1]
            old[own - narrow : own] = before_l[:size].reshape((narrow,) + cur.shape[1:])
            old[own + rows : own + rows + narrow] = before_r[:size].reshape((narrow,) + cur.shape[1:])
    else:
        earlier, known, got_l, got_r = refs_in
        cur[own : own + rows] = earlier[earlier.shape[0] - 1]
        old[own : own + rows] = earlier[earlier.shape[0] - 2]
        cur[own - wide : own] = got_l[0:wide]
        cur[own + rows : own + rows + wide] = got_r[0:wide]
        if narrow:
            old[own - RAD : own] = known[0]
            old[own + rows : own + rows + RAD] = known[1]
        if narrow > RAD:
            old[own - narrow : own - RAD] = got_l[wide:]
            old[own + rows + RAD : own + rows + narrow] = got_r[wide:]
    cells = [jnp.max(packs[block, NT : 2 * NT]).astype(jnp.int32) for block in range(3)]
    for step in range(steps):
        halo = RAD * (steps - 1 - step)
        advance(cur, old, model, zmat, ymat, own - halo, own + rows + halo, HALO - own)
        for block in (-1, 0, 1):
            if halo or block == 0:
                pack = packs.at[block + 1]
                add_source(old, pack, cells[block + 1], done + step, own, block, halo, rows)
        fields[step] = old[own : own + rows]
        cur, old = old, cur
    return cur, old, own


def send_shapes(index):
    steps = ROUNDS[index]
    return RAD * steps + RAD * max(steps - 2, 0)


def gather_packs(pack_own, before_l, before_r, packs):
    packs[0] = before_l[before_l.shape[0] - 16 :]
    packs[1] = pack_own[...]
    packs[2] = before_r[before_r.shape[0] - 16 :]


def forward_kernel(index, *refs):
    take = 6 if index == 0 else 4
    refs_in, refs = refs[:take], refs[take:]
    zmat, ymat, model, pack, fields, known, send_l, send_r = refs[:8]
    if index == 0:
        packs, buf_a, buf_b = refs[8:]
        gather_packs(pack, refs_in[4], refs_in[5], packs)
    else:
        packs, (buf_a, buf_b) = pack, refs[8:]
    cur, old, own = forward_round(index, refs_in, zmat, ymat, model, packs, fields, buf_a, buf_b)
    rows = 16
    known[0] = old[own - RAD : own]
    known[1] = old[own + rows : own + rows + RAD]
    wide = RAD * ROUNDS[index + 1]
    inner = wide - RAD
    send_l[0:wide] = cur[own : own + wide]
    send_r[0:wide] = cur[own + rows - wide : own + rows]
    if inner > RAD:
        send_l[wide:] = old[own + RAD : own + inner]
        send_r[wide:] = old[own + rows - inner : own + rows - RAD]


def split_exactly(values):
    high = values.astype(BF)
    rest = values - high.astype(F32)
    middle = rest.astype(BF)
    return high, middle, (rest - middle.astype(F32)).astype(BF)


def in_send_order(observed, count):
    owners = observed.shape[0]
    per_owner = count // owners
    slot = lax.broadcasted_iota(jnp.int32, (owners, count), 1)
    owner = lax.broadcasted_iota(jnp.int32, (owners, count), 0)
    owned = jnp.where(slot // per_owner == owner, 1.0, 0.0).astype(BF)
    spread = jnp.zeros((NT * per_owner, count), F32)
    for part in split_exactly(observed):
        spread = spread + dot(part, owned, (((0,), (0,)), ((), ())))
    line = lax.broadcasted_iota(jnp.int32, (per_owner, count), 0)
    slot = lax.broadcasted_iota(jnp.int32, (per_owner, count), 1)
    hit = slot % per_owner == line
    out = []
    for step in range(NT):
        part = spread[step * per_owner : (step + 1) * per_owner]
        out.append(jnp.sum(jnp.where(hit, part, 0.0), axis=0, keepdims=True))
    return jnp.concatenate(out, axis=0)


def tables_kernel(count, *refs):
    (cells, observed, *fields), (rows_out, lanes_out, traces) = refs[:-3], refs[-3:]
    rows_table, lane_table = pick_tables(cells[0:1].astype(jnp.int32), rows_out.shape[1])
    rows_out[...] = rows_table
    lanes_out[...] = lane_table
    total = jnp.zeros((16, count), F32)
    step = 0
    for group in fields:
        for i in range(group.shape[0]):
            total = total + extract(group[i], step, rows_table, lane_table)
            step += 1
    traces[...] = total[:NT] - in_send_order(observed[...], count)


def last_kernel(index, *refs):
    take = 6 if index == 0 else 4
    refs_in, refs = refs[:take], refs[take:]
    zmat, ymat, model, packs, cells, rows_table, lane_table, traces = refs[:8]
    fields, adj, buf_a, buf_b = refs[8:]
    forward_round(index, refs_in, zmat, ymat, model, packs, fields, buf_a, buf_b)
    done = sum(ROUNDS[:index])
    rows_table = rows_table[...]
    lane_table = lane_table[...]
    total = extract(fields[0], done, rows_table, lane_table)
    for step in range(1, ROUNDS[index]):
        total = total + extract(fields[step], done + step, rows_table, lane_table)
    adj[0:NT] = total[0:NT] + traces[...]
    adj[NT:] = cells[...]


def adjoint_kernel(field_groups, slabs, count, *refs):
    fields = []
    for ref in refs[:field_groups]:
        fields += [ref.at[i] for i in range(ref.shape[0])]
    refs = refs[field_groups:]
    zmat, ymat, model, *adjs = refs[:8]
    outs = refs[8 : 8 + slabs]
    buf_a, buf_b, image, rows_table = refs[8 + slabs :]
    rows = 16
    own = HALO
    span_y, span_z = buf_a.shape[1:]
    table_rows = rows * span_y
    lanes = []
    for block in range(5):
        cells = adjs[block][NT : NT + 1].astype(jnp.int32)
        sub = lax.broadcasted_iota(jnp.int32, (table_rows, count), 0)
        rows_table[block] = jnp.where(sub == cells // span_z, 1.0, 0.0).astype(BF)
        lanes.append(cells % span_z)

    def inject(field, number):
        halo = RAD * (NT - number)
        step = NT - number
        for block in range(-2, 3):
            begin = own + block * rows
            first = max(begin, own - halo)
            last = min(begin + rows, own + rows + halo)
            if first >= last:
                continue
            amounts = adjs[block + 2][step : step + 1]
            high = amounts.astype(BF).astype(F32)
            low = amounts - high
            sub = lax.broadcasted_iota(jnp.int32, (span_z, count), 0)
            hit = sub == lanes[block + 2]
            both = jnp.concatenate(
                [jnp.where(hit, high, 0.0).astype(BF), jnp.where(hit, low, 0.0).astype(BF)], axis=0
            )
            table = rows_table[block + 2, (first - begin) * span_y : (last - begin) * span_y, :]
            added = dot(table, both, (((1,), (1,)), ((), ())))
            added = (added[:, :span_z] + added[:, span_z:]).reshape(last - first, span_y, span_z)
            if number == 1:
                field[first:last] = added
            else:
                field[first:last] = field[first:last] + added

    cur, old = buf_a, buf_b
    inject(cur, 1)
    old[...] = jnp.zeros(old.shape, F32)
    image[...] = cur[own : own + rows] * fields[NT - 1][...]
    for number in range(2, NT + 1):
        halo = RAD * (NT - number)
        advance(cur, old, model, zmat, ymat, own - halo, own + rows + halo, 0)
        inject(old, number)
        image[...] = image[...] + old[own : own + rows] * fields[NT - number][...]
        cur, old = old, cur
    mine = lax.axis_index("shot") // PIECES
    thick = rows // slabs
    for i in range(slabs):
        outs[i][...] = image[pl.ds(lax.rem(mine + i, slabs) * thick, thick)]


def call(kernel, outs, ins, specs=None, scratch=(), cost=(1e6, 1e6), name=None):
    return pl.pallas_call(
        kernel,
        out_shape=outs,
        in_specs=specs or [VMEM] * len(ins),
        out_specs=jax.tree.map(lambda _: VMEM, outs),
        scratch_shapes=list(scratch),
        compiler_params=pltpu.CompilerParams(vmem_limit_bytes=48 * 1024 * 1024),
        cost_estimate=pl.CostEstimate(flops=int(cost[0]), bytes_accessed=int(cost[1]), transcendentals=0),
        name=name,
    )(*ins)


def shifted(value, steps):
    count = lax.axis_size("shot")
    return lax.ppermute(value, "shot", [(i, (i + steps) % count) for i in range(count)])


def per_device(
    courant_sq, wave_now, wave_before, wavelet, source_cell, receiver_cell, send_order, observed
):
    devices = lax.axis_size("shot")
    rows, span_y, span_z = wave_now.shape
    count = receiver_cell.shape[0]
    table_rows = rows * span_y
    plane = (span_y, span_z)
    zmat, ymat = matrices(span_y, span_z)

    wide = RAD * ROUNDS[0]
    narrow = wide - RAD
    now_l, now_r = shifted(wave_now[rows - wide :], 1), shifted(wave_now[:wide], -1)
    message = jax.ShapeDtypeStruct((narrow * span_y + 16, span_z), F32)
    to_left, to_right, pack = call(
        message_kernel,
        (message, message, jax.ShapeDtypeStruct((16, span_z), F32)),
        (wave_before, wavelet, source_cell),
        specs=[VMEM, SMEM, SMEM],
        name="message",
    )
    before_l, before_r = shifted(to_right, 1), shifted(to_left, -1)

    model, cells, observed = call(
        prepare_kernel,
        (
            jax.ShapeDtypeStruct((rows + 2 * HALO,) + plane, F32),
            jax.ShapeDtypeStruct((8, count), F32),
            jax.ShapeDtypeStruct(observed.shape, F32),
        ),
        (courant_sq, receiver_cell.reshape(1, count), send_order.reshape(1, count), observed, pack),
        name="prepare",
    )
    recorded = lax.all_to_all(observed, "shot", split_axis=0, concat_axis=0, tiled=True)

    common = (zmat, ymat, model)
    field_list = []
    ins = (wave_now, wave_before, now_l, now_r, before_l, before_r)
    for index in range(len(ROUNDS) - 1):
        window = rows + 2 * RAD * ROUNDS[index]
        sent = send_shapes(index + 1)
        packs = (jax.ShapeDtypeStruct((3, 16, span_z), F32),) if index == 0 else ()
        fields, known, send_l, send_r, *made = call(
            functools.partial(forward_kernel, index),
            (
                jax.ShapeDtypeStruct((ROUNDS[index], rows) + plane, F32),
                jax.ShapeDtypeStruct((2, RAD) + plane, F32),
                jax.ShapeDtypeStruct((sent,) + plane, F32),
                jax.ShapeDtypeStruct((sent,) + plane, F32),
            )
            + packs,
            ins + common + (pack,),
            scratch=[pltpu.VMEM((window,) + plane, F32)] * 2,
            name="forward",
        )
        field_list.append(fields)
        pack = made[0] if made else pack
        ins = (fields, known, shifted(send_r, 1), shifted(send_l, -1))

    rows_table, lane_table, traces = call(
        functools.partial(tables_kernel, count),
        (
            jax.ShapeDtypeStruct((count, table_rows), BF),
            jax.ShapeDtypeStruct((count, 256), F32),
            jax.ShapeDtypeStruct((NT, count), F32),
        ),
        (cells, recorded, *field_list),
        name="traces",
    )
    index = len(ROUNDS) - 1
    window = rows + 2 * RAD * ROUNDS[index]
    fields, adj = call(
        functools.partial(last_kernel, index),
        (
            jax.ShapeDtypeStruct((ROUNDS[index], rows) + plane, F32),
            jax.ShapeDtypeStruct((2 * NT, count), F32),
        ),
        ins + common + (pack, cells, rows_table, lane_table, traces),
        scratch=[pltpu.VMEM((window,) + plane, F32)] * 2,
        name="forward_last",
    )
    field_list.append(fields)

    adjs = [shifted(adj, 2), shifted(adj, 1), adj, shifted(adj, -1), shifted(adj, -2)]
    slabs = devices // PIECES
    thick = rows // slabs
    parts = call(
        functools.partial(adjoint_kernel, len(field_list), slabs, count),
        tuple(jax.ShapeDtypeStruct((thick,) + plane, F32) for _ in range(slabs)),
        (*field_list, zmat, ymat, model, *adjs),
        scratch=[pltpu.VMEM((rows + 2 * HALO,) + plane, F32)] * 2
        + [pltpu.VMEM((rows,) + plane, F32), pltpu.VMEM((5, table_rows, count), BF)],
        name="adjoint",
    )
    total = parts[0]
    for i in range(1, slabs):
        total = total + shifted(parts[i], i * PIECES)
    return total


def solution(mesh):
    return jax.shard_map(
        per_device,
        mesh=mesh,
        in_specs=(
            P("groups", None, None),
            P(("groups", "shot"), None, None),
            P(("groups", "shot"), None, None),
            P(("groups", "shot"), None),
            P(("groups", "shot")),
            P(("groups", "shot")),
            P(("groups", "shot")),
            P(("groups", "shot"), None),
        ),
        out_specs=P(("groups", "shot"), None, None),
        check_vma=False,
    )
```

```python
import functools

import jax
import jax.numpy as jnp
import numpy as np
from jax import lax
from jax.experimental import pallas as pl
from jax.experimental.pallas import tpu as pltpu
from jax.sharding import PartitionSpec as P

NT = 8
PIECES = 4
RAD = 4
ROUNDS = (4, 4)
SCALE = 5040.0
CENTER = -43050.0
WEIGHTS = (8064.0, -1008.0, 128.0, -9.0)
GROUP = 8
HALO = RAD * (NT - 1)
BF = jnp.bfloat16
F32 = jnp.float32

VMEM = pl.BlockSpec(memory_space=pltpu.VMEM)
SMEM = pl.BlockSpec(memory_space=pltpu.SMEM)


def band(size):
    out = np.zeros((size, size), np.float32)
    for k, weight in enumerate(WEIGHTS, 1):
        out += weight * (np.eye(size, k=k) + np.eye(size, k=-k))
    return out


def matrices(span_y, span_z):
    along_z = np.concatenate([band(span_z)] * 2, axis=0)
    along_y = np.kron(np.eye(GROUP), band(span_y))
    return jnp.asarray(along_z, BF), jnp.asarray(along_y, BF)


def split(values):
    high = values.astype(BF)
    low = (values - high.astype(F32)).astype(BF)
    return high, low


def dot(a, b, dims=(((1,), (0,)), ((), ()))):
    return lax.dot_general(a, b, dims, preferred_element_type=F32)


def advance(cur, old, model, zmat, ymat, first, last, model_shift):
    span_y, span_z = cur.shape[1:]
    zmat, ymat = zmat[...], ymat[...]
    for base in range(first, last, GROUP):
        group = cur[base : base + GROUP].reshape(GROUP * span_y, span_z)
        pair = jnp.concatenate(split(group), axis=1)
        z_part = dot(pair, zmat)
        y_part = dot(ymat, pair)
        for i in range(GROUP):
            x = base + i
            rows = slice(i * span_y, (i + 1) * span_y)
            here = cur[x]
            total = CENTER * here + z_part[rows] + y_part[rows, :span_z] + y_part[rows, span_z:]
            for k, weight in enumerate(WEIGHTS, 1):
                total = total + weight * (cur[x + k] + cur[x - k])
            old[x] = 2.0 * here - old[x] + model[x + model_shift] * total


def add_source(field, pack, cell, step, own, block, halo, rows):
    span_y, span_z = field.shape[1:]
    plane = own + block * rows + cell // (span_y * span_z)
    y = (cell // span_z) % span_y
    z = cell % span_z

    @pl.when((plane >= own - halo) & (plane < own + rows + halo))
    def _():
        tile = pl.ds(pl.multiple_of((y // 8) * 8, 8), 8)
        sub = lax.broadcasted_iota(jnp.int32, (8, span_z), 0)
        lane = lax.broadcasted_iota(jnp.int32, (8, span_z), 1)
        hit = (sub == y % 8) & (lane == z)
        field[plane, tile, :] = field[plane, tile, :] + jnp.where(hit, pack[step : step + 1], 0.0)


def parity():
    return lax.rem(lax.axis_index("shot"), 2)


def message_kernel(before, wavelet, source, outer_out, mate_out, pack_out):
    rows, span_y, span_z = before.shape
    which = lax.broadcasted_iota(jnp.int32, (16, span_z), 0)
    pack = jnp.where(which >= NT, source[0].astype(F32), 0.0)
    for step in range(NT):
        pack = jnp.where(which == step, wavelet[0, step], pack)
    pack_out[...] = pack
    narrow = RAD * (ROUNDS[0] - 1)
    size = narrow * span_y
    odd = parity()
    outer_out[:size] = before[pl.ds(odd * (rows - narrow), narrow)].reshape(size, span_z)
    mate_out[:size] = before[pl.ds((1 - odd) * (rows - narrow), narrow)].reshape(size, span_z)
    outer_out[size:] = pack
    mate_out[size:] = pack


def prepare_kernel(courant, cells, order, observed, pack, model_out, cells_out, observed_out):
    rows = 16
    piece = lax.rem(lax.axis_index("shot"), PIECES)
    period = courant.shape[0]
    window = model_out.shape[0]
    for chunk in range(0, window, RAD):
        source = lax.rem(piece * rows - HALO + chunk + period, period)
        model_out[chunk : chunk + RAD] = courant[pl.ds(source, RAD)] * (1.0 / SCALE)
    count = cells.shape[1]
    wanted = order[...]
    cell = cells[...]
    which = lax.broadcasted_iota(jnp.int32, (16, count), 0)
    digits = jnp.where(which == 0, cell // 256, jnp.where(which == 1, cell % 256, 0)).astype(F32).astype(BF)
    for j in range(0, count, 256):
        index = lax.broadcasted_iota(jnp.int32, (count, 256), 0)
        chosen = jnp.where(index == wanted[:, j : j + 256], 1.0, 0.0).astype(BF)
        found = dot(digits, chosen)
        ordered = found[0:1] * 256.0 + found[1:2]
        cells_out[:, j : j + 256] = jnp.broadcast_to(ordered, (8, 256))
    observed_out[...] = observed[...] + 0.0 * pack[0:1, :]


def pick_tables(cells, table_rows):
    count = cells.shape[1]
    column = jnp.transpose(jnp.broadcast_to(cells.astype(F32), (128, count)))
    column = column.astype(jnp.int32)
    row_of = jnp.concatenate([column // 128] * (table_rows // 128), axis=1)
    lane_of = jnp.concatenate([column % 128] * 2, axis=1)
    lanes = lax.broadcasted_iota(jnp.int32, (count, table_rows), 1)
    rows_table = jnp.where(row_of == lanes, 1.0, 0.0).astype(BF)
    lanes2 = lax.broadcasted_iota(jnp.int32, (count, 256), 1) % 128
    lane_table = jnp.where(lane_of == lanes2, 1.0, 0.0)
    return rows_table, lane_table


def extract(field, step, rows_table, lane_table):
    rows, span_y, span_z = field.shape
    pair = jnp.concatenate(split(field.reshape(rows * span_y, span_z)), axis=1)
    which = lax.broadcasted_iota(jnp.int32, (16, 2 * span_z), 0)
    ones = jnp.where(which == step, 1.0, 0.0).astype(BF)
    out = []
    for j in range(0, rows_table.shape[0], 256):
        found = dot(rows_table[j : j + 256], pair)
        kept = (found * lane_table[j : j + 256]).astype(BF)
        out.append(dot(ones, kept, (((1,), (1,)), ((), ()))))
    return jnp.concatenate(out, axis=1)


def forward_round(
    index, refs_in, zmat, ymat, model, packs, fields, buf_a, buf_b
):
    steps = ROUNDS[index]
    done = sum(ROUNDS[:index])
    rows = 16
    own = RAD * steps
    cur, old = buf_a, buf_b
    wide, narrow = RAD * steps, RAD * (steps - 1)
    odd = parity()
    shape = cur.shape[1:]
    low, high = own - wide, own + rows
    cur_outer = jnp.where(odd == 0, low, high)
    cur_mate = jnp.where(odd == 0, high, low)
    if index == 0:
        now, before, now_outer, now_mate, before_outer, before_mate = refs_in
        cur[own : own + rows] = now[...]
        old[own : own + rows] = before[...]
        cur[pl.ds(cur_outer, wide)] = now_outer[...]
        cur[pl.ds(cur_mate, wide)] = now_mate[...]
        size = narrow * shape[0]
        low = own - narrow
        old[pl.ds(jnp.where(odd == 0, low, high), narrow)] = before_outer[:size].reshape((narrow,) + shape)
        old[pl.ds(jnp.where(odd == 0, high, low), narrow)] = before_mate[:size].reshape((narrow,) + shape)
    else:
        earlier, known, got_outer, got_mate = refs_in
        cur[own : own + rows] = earlier[earlier.shape[0] - 1]
        old[own : own + rows] = earlier[earlier.shape[0] - 2]
        cur[pl.ds(cur_outer, wide)] = got_outer[0:wide]
        cur[pl.ds(cur_mate, wide)] = got_mate[0:wide]
        old[own - RAD : own] = known[0]
        old[own + rows : own + rows + RAD] = known[1]
        low, high = own - narrow, own + rows + RAD
        more = narrow - RAD
        old[pl.ds(jnp.where(odd == 0, low, high), more)] = got_outer[wide:]
        old[pl.ds(jnp.where(odd == 0, high, low), more)] = got_mate[wide:]
    cells = [jnp.max(packs[block, NT : 2 * NT]).astype(jnp.int32) for block in range(3)]
    for step in range(steps):
        halo = RAD * (steps - 1 - step)
        advance(cur, old, model, zmat, ymat, own - halo, own + rows + halo, HALO - own)
        for block in (-1, 0, 1):
            if halo or block == 0:
                pack = packs.at[block + 1]
                add_source(old, pack, cells[block + 1], done + step, own, block, halo, rows)
        fields[step] = old[own : own + rows]
        cur, old = old, cur
    return cur, old, own


def gather_packs(pack_own, outer, mate, packs):
    odd = parity()
    packs[2 * odd] = outer[outer.shape[0] - 16 :]
    packs[1] = pack_own[...]
    packs[2 - 2 * odd] = mate[mate.shape[0] - 16 :]


def forward_kernel(index, *refs):
    take = 6 if index == 0 else 4
    refs_in, refs = refs[:take], refs[take:]
    zmat, ymat, model, pack, fields, known, send = refs[:7]
    if index == 0:
        packs, buf_a, buf_b = refs[7:]
        gather_packs(pack, refs_in[4], refs_in[5], packs)
    else:
        packs, (buf_a, buf_b) = pack, refs[7:]
    cur, old, own = forward_round(index, refs_in, zmat, ymat, model, packs, fields, buf_a, buf_b)
    rows = 16
    known[0] = old[own - RAD : own]
    known[1] = old[own + rows : own + rows + RAD]
    send[0:rows] = cur[own : own + rows]
    send[rows:] = old[own + RAD : own + rows - RAD]


def split_exactly(values):
    high = values.astype(BF)
    rest = values - high.astype(F32)
    middle = rest.astype(BF)
    return high, middle, (rest - middle.astype(F32)).astype(BF)


def in_send_order(observed, count):
    owners = observed.shape[0]
    per_owner = count // owners
    slot = lax.broadcasted_iota(jnp.int32, (owners, count), 1)
    owner = lax.broadcasted_iota(jnp.int32, (owners, count), 0)
    owned = jnp.where(slot // per_owner == owner, 1.0, 0.0).astype(BF)
    spread = jnp.zeros((NT * per_owner, count), F32)
    for part in split_exactly(observed):
        spread = spread + dot(part, owned, (((0,), (0,)), ((), ())))
    line = lax.broadcasted_iota(jnp.int32, (per_owner, count), 0)
    slot = lax.broadcasted_iota(jnp.int32, (per_owner, count), 1)
    hit = slot % per_owner == line
    out = []
    for step in range(NT):
        part = spread[step * per_owner : (step + 1) * per_owner]
        out.append(jnp.sum(jnp.where(hit, part, 0.0), axis=0, keepdims=True))
    return jnp.concatenate(out, axis=0)


def tables_kernel(count, *refs):
    (cells, observed, *fields), (rows_out, lanes_out, traces) = refs[:-3], refs[-3:]
    rows_table, lane_table = pick_tables(cells[0:1].astype(jnp.int32), rows_out.shape[1])
    rows_out[...] = rows_table
    lanes_out[...] = lane_table
    total = jnp.zeros((16, count), F32)
    step = 0
    for group in fields:
        for i in range(group.shape[0]):
            total = total + extract(group[i], step, rows_table, lane_table)
            step += 1
    traces[...] = total[:NT] - in_send_order(observed[...], count)


def last_kernel(index, *refs):
    take = 6 if index == 0 else 4
    refs_in, refs = refs[:take], refs[take:]
    zmat, ymat, model, packs, cells, rows_table, lane_table, traces = refs[:8]
    fields, adj, buf_a, buf_b = refs[8:]
    forward_round(index, refs_in, zmat, ymat, model, packs, fields, buf_a, buf_b)
    done = sum(ROUNDS[:index])
    rows_table = rows_table[...]
    lane_table = lane_table[...]
    total = extract(fields[0], done, rows_table, lane_table)
    for step in range(1, ROUNDS[index]):
        total = total + extract(fields[step], done + step, rows_table, lane_table)
    adj[0:NT] = total[0:NT] + traces[...]
    adj[NT:] = cells[...]


def adjoint_kernel(field_groups, slabs, count, *refs):
    fields = []
    for ref in refs[:field_groups]:
        fields += [ref.at[i] for i in range(ref.shape[0])]
    refs = refs[field_groups:]
    zmat, ymat, model, adj, outer, mate, even_pair, odd_pair = refs[:8]
    outs = refs[8 : 8 + slabs]
    buf_a, buf_b, image, rows_table, adjs = refs[8 + slabs :]
    odd = parity()
    odd_chip = lax.rem(lax.axis_index("shot") // 2, 2)
    adjs[2] = adj[...]
    adjs[1 + 2 * odd] = outer[...]
    adjs[3 - 2 * odd] = mate[...]
    adjs[4 - 4 * odd_chip] = even_pair[...]
    adjs[4 * odd_chip] = odd_pair[...]
    rows = 16
    own = HALO
    span_y, span_z = buf_a.shape[1:]
    table_rows = rows * span_y
    lanes = []
    for block in range(5):
        cells = adjs[block, NT : NT + 1].astype(jnp.int32)
        sub = lax.broadcasted_iota(jnp.int32, (table_rows, count), 0)
        rows_table[block] = jnp.where(sub == cells // span_z, 1.0, 0.0).astype(BF)
        lanes.append(cells % span_z)

    def inject(field, number):
        halo = RAD * (NT - number)
        step = NT - number
        for block in range(-2, 3):
            begin = own + block * rows
            first = max(begin, own - halo)
            last = min(begin + rows, own + rows + halo)
            if first >= last:
                continue
            amounts = adjs[block + 2, step : step + 1]
            high = amounts.astype(BF).astype(F32)
            low = amounts - high
            sub = lax.broadcasted_iota(jnp.int32, (span_z, count), 0)
            hit = sub == lanes[block + 2]
            both = jnp.concatenate(
                [jnp.where(hit, high, 0.0).astype(BF), jnp.where(hit, low, 0.0).astype(BF)], axis=0
            )
            table = rows_table[block + 2, (first - begin) * span_y : (last - begin) * span_y, :]
            added = dot(table, both, (((1,), (1,)), ((), ())))
            added = (added[:, :span_z] + added[:, span_z:]).reshape(last - first, span_y, span_z)
            if number == 1:
                field[first:last] = added
            else:
                field[first:last] = field[first:last] + added

    cur, old = buf_a, buf_b
    inject(cur, 1)
    old[...] = jnp.zeros(old.shape, F32)
    image[...] = cur[own : own + rows] * fields[NT - 1][...]
    for number in range(2, NT + 1):
        halo = RAD * (NT - number)
        advance(cur, old, model, zmat, ymat, own - halo, own + rows + halo, 0)
        inject(old, number)
        image[...] = image[...] + old[own : own + rows] * fields[NT - number][...]
        cur, old = old, cur
    mine = lax.axis_index("shot") // PIECES
    thick = rows // slabs
    for i in range(slabs):
        outs[i][...] = image[pl.ds((mine ^ i) * thick, thick)]


def call(kernel, outs, ins, specs=None, scratch=(), cost=(1e6, 1e6), name=None):
    return pl.pallas_call(
        kernel,
        out_shape=outs,
        in_specs=specs or [VMEM] * len(ins),
        out_specs=jax.tree.map(lambda _: VMEM, outs),
        scratch_shapes=list(scratch),
        compiler_params=pltpu.CompilerParams(vmem_limit_bytes=48 * 1024 * 1024),
        cost_estimate=pl.CostEstimate(flops=int(cost[0]), bytes_accessed=int(cost[1]), transcendentals=0),
        name=name,
    )(*ins)


def swapped(value, partner):
    count = lax.axis_size("shot")
    return lax.ppermute(value, "shot", [(d, partner(d) % count) for d in range(count)])


def with_mate(value):
    return swapped(value, lambda d: d ^ 1)


def with_outer(value):
    return swapped(value, lambda d: d + 1 if d % 2 else d - 1)


def with_even_pair(value):
    return swapped(value, lambda d: d ^ 2)


def with_odd_pair(value):
    return swapped(value, lambda d: d + 2 if d % 4 >= 2 else d - 2)


def per_device(
    courant_sq, wave_now, wave_before, wavelet, source_cell, receiver_cell, send_order, observed
):
    devices = lax.axis_size("shot")
    rows, span_y, span_z = wave_now.shape
    count = receiver_cell.shape[0]
    table_rows = rows * span_y
    plane = (span_y, span_z)
    zmat, ymat = matrices(span_y, span_z)

    narrow = RAD * (ROUNDS[0] - 1)
    now_outer, now_mate = with_outer(wave_now), with_mate(wave_now)
    message = jax.ShapeDtypeStruct((narrow * span_y + 16, span_z), F32)
    to_outer, to_mate, pack = call(
        message_kernel,
        (message, message, jax.ShapeDtypeStruct((16, span_z), F32)),
        (wave_before, wavelet, source_cell),
        specs=[VMEM, SMEM, SMEM],
        name="message",
    )
    before_outer, before_mate = with_outer(to_outer), with_mate(to_mate)

    model, cells, observed = call(
        prepare_kernel,
        (
            jax.ShapeDtypeStruct((rows + 2 * HALO,) + plane, F32),
            jax.ShapeDtypeStruct((8, count), F32),
            jax.ShapeDtypeStruct(observed.shape, F32),
        ),
        (courant_sq, receiver_cell.reshape(1, count), send_order.reshape(1, count), observed, pack),
        name="prepare",
    )
    recorded = lax.all_to_all(observed, "shot", split_axis=0, concat_axis=0, tiled=True)

    common = (zmat, ymat, model)
    field_list = []
    ins = (wave_now, wave_before, now_outer, now_mate, before_outer, before_mate)
    for index in range(len(ROUNDS) - 1):
        window = rows + 2 * RAD * ROUNDS[index]
        sent = 2 * rows - 2 * RAD
        packs = (jax.ShapeDtypeStruct((3, 16, span_z), F32),) if index == 0 else ()
        fields, known, send, *made = call(
            functools.partial(forward_kernel, index),
            (
                jax.ShapeDtypeStruct((ROUNDS[index], rows) + plane, F32),
                jax.ShapeDtypeStruct((2, RAD) + plane, F32),
                jax.ShapeDtypeStruct((sent,) + plane, F32),
            )
            + packs,
            ins + common + (pack,),
            scratch=[pltpu.VMEM((window,) + plane, F32)] * 2,
            name="forward",
        )
        field_list.append(fields)
        pack = made[0] if made else pack
        ins = (fields, known, with_outer(send), with_mate(send))

    rows_table, lane_table, traces = call(
        functools.partial(tables_kernel, count),
        (
            jax.ShapeDtypeStruct((count, table_rows), BF),
            jax.ShapeDtypeStruct((count, 256), F32),
            jax.ShapeDtypeStruct((NT, count), F32),
        ),
        (cells, recorded, *field_list),
        name="traces",
    )
    index = len(ROUNDS) - 1
    window = rows + 2 * RAD * ROUNDS[index]
    fields, adj = call(
        functools.partial(last_kernel, index),
        (
            jax.ShapeDtypeStruct((ROUNDS[index], rows) + plane, F32),
            jax.ShapeDtypeStruct((2 * NT, count), F32),
        ),
        ins + common + (pack, cells, rows_table, lane_table, traces),
        scratch=[pltpu.VMEM((window,) + plane, F32)] * 2,
        name="forward_last",
    )
    field_list.append(fields)

    adjs = [adj, with_outer(adj), with_mate(adj), with_even_pair(adj), with_odd_pair(adj)]
    slabs = devices // PIECES
    thick = rows // slabs
    parts = call(
        functools.partial(adjoint_kernel, len(field_list), slabs, count),
        tuple(jax.ShapeDtypeStruct((thick,) + plane, F32) for _ in range(slabs)),
        (*field_list, zmat, ymat, model, *adjs),
        scratch=[pltpu.VMEM((rows + 2 * HALO,) + plane, F32)] * 2
        + [pltpu.VMEM((rows,) + plane, F32), pltpu.VMEM((5, table_rows, count), BF)]
        + [pltpu.VMEM((5, 2 * NT, count), F32)],
        name="adjoint",
    )
    total = parts[0]
    for i in range(1, slabs):
        total = total + swapped(parts[i], lambda d: d ^ (i * PIECES))
    return total


def solution(mesh):
    return jax.shard_map(
        per_device,
        mesh=mesh,
        in_specs=(
            P("groups", None, None),
            P(("groups", "shot"), None, None),
            P(("groups", "shot"), None, None),
            P(("groups", "shot"), None),
            P(("groups", "shot")),
            P(("groups", "shot")),
            P(("groups", "shot")),
            P(("groups", "shot"), None),
        ),
        out_specs=P(("groups", "shot"), None, None),
        check_vma=False,
    )
```

```python
import functools

import jax
import jax.numpy as jnp
import numpy as np
from jax import lax
from jax.experimental import pallas as pl
from jax.experimental.pallas import tpu as pltpu
from jax.sharding import PartitionSpec as P

NT = 8
PIECES = 4
RAD = 4
ROUNDS = (4, 4)
SCALE = 5040.0
CENTER = -43050.0
WEIGHTS = (8064.0, -1008.0, 128.0, -9.0)
GROUP = 8
HALO = RAD * (NT - 1)
BF = jnp.bfloat16
F32 = jnp.float32

VMEM = pl.BlockSpec(memory_space=pltpu.VMEM)
SMEM = pl.BlockSpec(memory_space=pltpu.SMEM)


def band(size):
    out = np.zeros((size, size), np.float32)
    for k, weight in enumerate(WEIGHTS, 1):
        out += weight * (np.eye(size, k=k) + np.eye(size, k=-k))
    return out


def matrices(span_y, span_z):
    along_z = np.concatenate([band(span_z)] * 2, axis=0)
    tiles = span_y // 8
    along_y = band(span_y).reshape(tiles, 8, tiles, 8)
    full = np.zeros((tiles, GROUP, 8, tiles, GROUP, 8), np.float32)
    for i in range(GROUP):
        full[:, i, :, :, i, :] = along_y
    return jnp.asarray(along_z, BF), jnp.asarray(full.reshape(GROUP * span_y, GROUP * span_y), BF)


def split(values):
    high = values.astype(BF)
    low = (values - high.astype(F32)).astype(BF)
    return high, low


def dot(a, b, dims=(((1,), (0,)), ((), ()))):
    return lax.dot_general(a, b, dims, preferred_element_type=F32)


def advance(cur, old, model, zmat, ymat, first, last, model_shift):
    span_y, span_z = cur.shape[1:]
    zmat, ymat = zmat[...], ymat[...]
    for base in range(first, last, GROUP):
        columns = [slice(j, j + 8) for j in range(0, span_y, 8)]
        order = [(i, column) for column in columns for i in range(GROUP)]
        group = jnp.concatenate([cur[base + i, column] for i, column in order], axis=0)
        pair = jnp.concatenate(split(group), axis=1)
        z_part = dot(pair, zmat)
        y_part = dot(ymat, pair)
        for j, column in enumerate(columns):
            tiles = [cur[base - RAD + q, column] for q in range(GROUP + 2 * RAD)]
            for i in range(GROUP):
                x = base + i
                at = (j * GROUP + i) * 8
                rows = slice(at, at + 8)
                here = tiles[i + RAD]
                total = z_part[rows] + (y_part[rows, :span_z] + y_part[rows, span_z:]) + CENTER * here
                for k, weight in enumerate(WEIGHTS, 1):
                    total = total + weight * (tiles[i + RAD + k] + tiles[i + RAD - k])
                old[x, column] = (here + here - old[x, column]) + model[x + model_shift, column] * total


def add_source(field, pack, cell, step, own, block, halo, rows):
    span_y, span_z = field.shape[1:]
    plane = own + block * rows + cell // (span_y * span_z)
    y = (cell // span_z) % span_y
    z = cell % span_z

    inside = (plane >= own - halo) & (plane < own + rows + halo)
    plane = jnp.where(inside, plane, own)
    tile = pl.ds(pl.multiple_of((y // 8) * 8, 8), 8)
    sub = lax.broadcasted_iota(jnp.int32, (8, span_z), 0)
    lane = lax.broadcasted_iota(jnp.int32, (8, span_z), 1)
    hit = (sub == jnp.where(inside, y % 8, 8)) & (lane == z)
    field[plane, tile, :] = field[plane, tile, :] + jnp.where(hit, pack[step : step + 1], 0.0)


def parity():
    return lax.rem(lax.axis_index("shot"), 2)


def message_kernel(before, wavelet, source, outer_out, mate_out, pack_out):
    rows, span_y, span_z = before.shape
    which = lax.broadcasted_iota(jnp.int32, (16, span_z), 0)
    pack = jnp.where(which >= NT, source[0].astype(F32), 0.0)
    for step in range(NT):
        pack = jnp.where(which == step, wavelet[0, step], pack)
    pack_out[...] = pack
    narrow = RAD * (ROUNDS[0] - 1)
    size = narrow * span_y
    odd = parity()
    outer_out[:size] = before[pl.ds(odd * (rows - narrow), narrow)].reshape(size, span_z)
    mate_out[:size] = before[pl.ds((1 - odd) * (rows - narrow), narrow)].reshape(size, span_z)
    outer_out[size:] = pack
    mate_out[size:] = pack


def prepare_kernel(courant, cells, order, observed, pack, model_out, cells_out, observed_out):
    rows = 16
    piece = lax.rem(lax.axis_index("shot"), PIECES)
    period = courant.shape[0]
    window = model_out.shape[0]
    for chunk in range(0, window, RAD):
        source = lax.rem(piece * rows - HALO + chunk + period, period)
        model_out[chunk : chunk + RAD] = courant[pl.ds(source, RAD)] * (1.0 / SCALE)
    count = cells.shape[1]
    wanted = order[...]
    cell = cells[...]
    which = lax.broadcasted_iota(jnp.int32, (16, count), 0)
    digits = jnp.where(which == 0, cell // 256, jnp.where(which == 1, cell % 256, 0)).astype(F32).astype(BF)
    for j in range(0, count, 256):
        index = lax.broadcasted_iota(jnp.int32, (count, 256), 0)
        chosen = jnp.where(index == wanted[:, j : j + 256], 1.0, 0.0).astype(BF)
        found = dot(digits, chosen)
        ordered = found[0:1] * 256.0 + found[1:2]
        cells_out[:, j : j + 256] = jnp.broadcast_to(ordered, (8, 256))
    observed_out[...] = observed[...] + 0.0 * pack[0:1, :]


def pick_tables(cells, table_rows):
    count = cells.shape[1]
    column = jnp.transpose(jnp.broadcast_to(cells.astype(F32), (128, count)))
    column = column.astype(jnp.int32)
    row_of = jnp.concatenate([column // 128] * (table_rows // 128), axis=1)
    lane_of = jnp.concatenate([column % 128] * 2, axis=1)
    lanes = lax.broadcasted_iota(jnp.int32, (count, table_rows), 1)
    rows_table = jnp.where(row_of == lanes, 1.0, 0.0).astype(BF)
    lanes2 = lax.broadcasted_iota(jnp.int32, (count, 256), 1) % 128
    lane_table = jnp.where(lane_of == lanes2, 1.0, 0.0)
    return rows_table, lane_table


def extract(field, step, rows_table, lane_table):
    rows, span_y, span_z = field.shape
    pair = jnp.concatenate(split(field.reshape(rows * span_y, span_z)), axis=1)
    which = lax.broadcasted_iota(jnp.int32, (16, 2 * span_z), 0)
    ones = jnp.where(which == step, 1.0, 0.0).astype(BF)
    out = []
    for j in range(0, rows_table.shape[0], 256):
        found = dot(rows_table[j : j + 256], pair)
        kept = (found * lane_table[j : j + 256]).astype(BF)
        out.append(dot(ones, kept, (((1,), (1,)), ((), ()))))
    return jnp.concatenate(out, axis=1)


def forward_round(
    index, refs_in, zmat, ymat, model, packs, fields, buf_a, buf_b
):
    steps = ROUNDS[index]
    done = sum(ROUNDS[:index])
    rows = 16
    own = RAD * steps
    cur, old = buf_a, buf_b
    wide, narrow = RAD * steps, RAD * (steps - 1)
    odd = parity()
    shape = cur.shape[1:]
    low, high = own - wide, own + rows
    cur_outer = jnp.where(odd == 0, low, high)
    cur_mate = jnp.where(odd == 0, high, low)
    if index == 0:
        now, before, now_outer, now_mate, before_outer, before_mate = refs_in
        cur[own : own + rows] = now[...]
        old[own : own + rows] = before[...]
        cur[pl.ds(cur_outer, wide)] = now_outer[...]
        cur[pl.ds(cur_mate, wide)] = now_mate[...]
        size = narrow * shape[0]
        low = own - narrow
        old[pl.ds(jnp.where(odd == 0, low, high), narrow)] = before_outer[:size].reshape((narrow,) + shape)
        old[pl.ds(jnp.where(odd == 0, high, low), narrow)] = before_mate[:size].reshape((narrow,) + shape)
    else:
        earlier, known, got_outer, got_mate = refs_in
        cur[own : own + rows] = earlier[earlier.shape[0] - 1]
        old[own : own + rows] = earlier[earlier.shape[0] - 2]
        cur[pl.ds(cur_outer, wide)] = got_outer[0:wide]
        cur[pl.ds(cur_mate, wide)] = got_mate[0:wide]
        old[own - RAD : own] = known[0]
        old[own + rows : own + rows + RAD] = known[1]
        low, high = own - narrow, own + rows + RAD
        more = narrow - RAD
        old[pl.ds(jnp.where(odd == 0, low, high), more)] = got_outer[wide:]
        old[pl.ds(jnp.where(odd == 0, high, low), more)] = got_mate[wide:]
    cells = [jnp.max(packs[block, NT : 2 * NT]).astype(jnp.int32) for block in range(3)]
    for step in range(steps):
        halo = RAD * (steps - 1 - step)
        advance(cur, old, model, zmat, ymat, own - halo, own + rows + halo, HALO - own)
        for block in (-1, 0, 1):
            if halo or block == 0:
                pack = packs.at[block + 1]
                add_source(old, pack, cells[block + 1], done + step, own, block, halo, rows)
        fields[step] = old[own : own + rows]
        cur, old = old, cur
    return cur, old, own


def gather_packs(pack_own, outer, mate, packs):
    odd = parity()
    packs[2 * odd] = outer[outer.shape[0] - 16 :]
    packs[1] = pack_own[...]
    packs[2 - 2 * odd] = mate[mate.shape[0] - 16 :]


def forward_kernel(index, *refs):
    take = 6 if index == 0 else 4
    refs_in, refs = refs[:take], refs[take:]
    zmat, ymat, model, pack, fields, known, send = refs[:7]
    if index == 0:
        packs, buf_a, buf_b = refs[7:]
        gather_packs(pack, refs_in[4], refs_in[5], packs)
    else:
        packs, (buf_a, buf_b) = pack, refs[7:]
    cur, old, own = forward_round(index, refs_in, zmat, ymat, model, packs, fields, buf_a, buf_b)
    rows = 16
    known[0] = old[own - RAD : own]
    known[1] = old[own + rows : own + rows + RAD]
    send[0:rows] = cur[own : own + rows]
    send[rows:] = old[own + RAD : own + rows - RAD]


def split_exactly(values):
    high = values.astype(BF)
    rest = values - high.astype(F32)
    middle = rest.astype(BF)
    return high, middle, (rest - middle.astype(F32)).astype(BF)


def in_send_order(observed, count):
    owners = observed.shape[0]
    per_owner = count // owners
    slot = lax.broadcasted_iota(jnp.int32, (owners, count), 1)
    owner = lax.broadcasted_iota(jnp.int32, (owners, count), 0)
    owned = jnp.where(slot // per_owner == owner, 1.0, 0.0).astype(BF)
    spread = jnp.zeros((NT * per_owner, count), F32)
    for part in split_exactly(observed):
        spread = spread + dot(part, owned, (((0,), (0,)), ((), ())))
    line = lax.broadcasted_iota(jnp.int32, (per_owner, count), 0)
    slot = lax.broadcasted_iota(jnp.int32, (per_owner, count), 1)
    hit = slot % per_owner == line
    out = []
    for step in range(NT):
        part = spread[step * per_owner : (step + 1) * per_owner]
        out.append(jnp.sum(jnp.where(hit, part, 0.0), axis=0, keepdims=True))
    return jnp.concatenate(out, axis=0)


def tables_kernel(count, *refs):
    (cells, observed, *fields), (rows_out, lanes_out, traces) = refs[:-3], refs[-3:]
    rows_table, lane_table = pick_tables(cells[0:1].astype(jnp.int32), rows_out.shape[1])
    rows_out[...] = rows_table
    lanes_out[...] = lane_table
    total = jnp.zeros((16, count), F32)
    step = 0
    for group in fields:
        for i in range(group.shape[0]):
            total = total + extract(group[i], step, rows_table, lane_table)
            step += 1
    traces[...] = total[:NT] - in_send_order(observed[...], count)


def last_kernel(index, *refs):
    take = 6 if index == 0 else 4
    refs_in, refs = refs[:take], refs[take:]
    zmat, ymat, model, packs, cells, rows_table, lane_table, traces = refs[:8]
    fields, adj, buf_a, buf_b = refs[8:]
    forward_round(index, refs_in, zmat, ymat, model, packs, fields, buf_a, buf_b)
    done = sum(ROUNDS[:index])
    rows_table = rows_table[...]
    lane_table = lane_table[...]
    total = extract(fields[0], done, rows_table, lane_table)
    for step in range(1, ROUNDS[index]):
        total = total + extract(fields[step], done + step, rows_table, lane_table)
    adj[0:NT] = total[0:NT] + traces[...]
    adj[NT:] = cells[...]


def source_planes(rows_table, lanes, amounts, span_z):
    high = amounts.astype(BF).astype(F32)
    low = amounts - high
    sub = lax.broadcasted_iota(jnp.int32, (span_z, lanes.shape[1]), 0)
    hit = sub == lanes
    both = jnp.concatenate([jnp.where(hit, high, 0.0).astype(BF), jnp.where(hit, low, 0.0).astype(BF)], axis=0)
    added = dot(rows_table, both, (((1,), (1,)), ((), ())))
    return added[:, :span_z] + added[:, span_z:]


def injection_table(cells, table_rows, span_z):
    sub = lax.broadcasted_iota(jnp.int32, (table_rows, cells.shape[1]), 0)
    return jnp.where(sub == cells // span_z, 1.0, 0.0).astype(BF)


def own_sources_kernel(adj, out):
    rows, span_y, span_z = out.shape[1:]
    cells = adj[NT : NT + 1].astype(jnp.int32)
    table = injection_table(cells, rows * span_y, span_z)
    for step in range(NT):
        added = source_planes(table, cells % span_z, adj[step : step + 1], span_z)
        out[step] = added.reshape(rows, span_y, span_z)


def adjoint_kernel(field_groups, slabs, *refs):
    fields = []
    for ref in refs[:field_groups]:
        fields += [ref.at[i] for i in range(ref.shape[0])]
    refs = refs[field_groups:]
    zmat, ymat, model, sources, outer, mate, even_pair, odd_pair = refs[:8]
    outs = refs[8 : 8 + slabs]
    buf_a, buf_b, image, rows_table, adjs = refs[8 + slabs :]
    odd = parity()
    odd_chip = lax.rem(lax.axis_index("shot") // 2, 2)
    adjs[1 + 2 * odd] = outer[...]
    adjs[3 - 2 * odd] = mate[...]
    adjs[4 - 4 * odd_chip] = even_pair[...]
    adjs[4 * odd_chip] = odd_pair[...]
    rows = 16
    own = HALO
    span_y, span_z = buf_a.shape[1:]
    table_rows = rows * span_y
    lanes = {}
    for block in (-2, -1, 1, 2):
        cells = adjs[block + 2, NT : NT + 1].astype(jnp.int32)
        rows_table[block + 2] = injection_table(cells, table_rows, span_z)
        lanes[block] = cells % span_z

    def inject(field, number):
        halo = RAD * (NT - number)
        step = NT - number
        for block in range(-2, 3):
            begin = own + block * rows
            first = max(begin, own - halo)
            last = min(begin + rows, own + rows + halo)
            if first >= last:
                continue
            if block:
                table = rows_table[block + 2, (first - begin) * span_y : (last - begin) * span_y, :]
                added = source_planes(table, lanes[block], adjs[block + 2, step : step + 1], span_z)
                added = added.reshape(last - first, span_y, span_z)
            else:
                added = sources[step]
            if number == 1:
                field[first:last] = added
            else:
                field[first:last] = field[first:last] + added

    cur, old = buf_a, buf_b
    inject(cur, 1)
    old[...] = jnp.zeros(old.shape, F32)
    image[...] = cur[own : own + rows] * fields[NT - 1][...]
    for number in range(2, NT + 1):
        halo = RAD * (NT - number)
        advance(cur, old, model, zmat, ymat, own - halo, own + rows + halo, 0)
        inject(old, number)
        image[...] = image[...] + old[own : own + rows] * fields[NT - number][...]
        cur, old = old, cur
    mine = lax.axis_index("shot") // PIECES
    thick = rows // slabs
    for i in range(slabs):
        outs[i][...] = image[pl.ds((mine ^ i) * thick, thick)]


def call(kernel, outs, ins, specs=None, scratch=(), cost=(1e6, 1e6), name=None):
    return pl.pallas_call(
        kernel,
        out_shape=outs,
        in_specs=specs or [VMEM] * len(ins),
        out_specs=jax.tree.map(lambda _: VMEM, outs),
        scratch_shapes=list(scratch),
        compiler_params=pltpu.CompilerParams(vmem_limit_bytes=48 * 1024 * 1024),
        cost_estimate=pl.CostEstimate(flops=int(cost[0]), bytes_accessed=int(cost[1]), transcendentals=0),
        name=name,
    )(*ins)


def swapped(value, partner):
    count = lax.axis_size("shot")
    return lax.ppermute(value, "shot", [(d, partner(d) % count) for d in range(count)])


def with_mate(value):
    return swapped(value, lambda d: d ^ 1)


def with_outer(value):
    return swapped(value, lambda d: d + 1 if d % 2 else d - 1)


def with_even_pair(value):
    return swapped(value, lambda d: d ^ 2)


def with_odd_pair(value):
    return swapped(value, lambda d: d + 2 if d % 4 >= 2 else d - 2)


def per_device(
    courant_sq, wave_now, wave_before, wavelet, source_cell, receiver_cell, send_order, observed
):
    devices = lax.axis_size("shot")
    rows, span_y, span_z = wave_now.shape
    count = receiver_cell.shape[0]
    table_rows = rows * span_y
    plane = (span_y, span_z)
    zmat, ymat = matrices(span_y, span_z)

    narrow = RAD * (ROUNDS[0] - 1)
    now_outer, now_mate = with_outer(wave_now), with_mate(wave_now)
    message = jax.ShapeDtypeStruct((narrow * span_y + 16, span_z), F32)
    to_outer, to_mate, pack = call(
        message_kernel,
        (message, message, jax.ShapeDtypeStruct((16, span_z), F32)),
        (wave_before, wavelet, source_cell),
        specs=[VMEM, SMEM, SMEM],
        name="message",
    )
    before_outer, before_mate = with_outer(to_outer), with_mate(to_mate)

    model, cells, observed = call(
        prepare_kernel,
        (
            jax.ShapeDtypeStruct((rows + 2 * HALO,) + plane, F32),
            jax.ShapeDtypeStruct((8, count), F32),
            jax.ShapeDtypeStruct(observed.shape, F32),
        ),
        (courant_sq, receiver_cell.reshape(1, count), send_order.reshape(1, count), observed, pack),
        name="prepare",
    )
    recorded = lax.all_to_all(observed, "shot", split_axis=0, concat_axis=0, tiled=True)

    common = (zmat, ymat, model)
    field_list = []
    ins = (wave_now, wave_before, now_outer, now_mate, before_outer, before_mate)
    for index in range(len(ROUNDS) - 1):
        window = rows + 2 * RAD * ROUNDS[index]
        sent = 2 * rows - 2 * RAD
        packs = (jax.ShapeDtypeStruct((3, 16, span_z), F32),) if index == 0 else ()
        fields, known, send, *made = call(
            functools.partial(forward_kernel, index),
            (
                jax.ShapeDtypeStruct((ROUNDS[index], rows) + plane, F32),
                jax.ShapeDtypeStruct((2, RAD) + plane, F32),
                jax.ShapeDtypeStruct((sent,) + plane, F32),
            )
            + packs,
            ins + common + (pack,),
            scratch=[pltpu.VMEM((window,) + plane, F32)] * 2,
            name="forward",
        )
        field_list.append(fields)
        pack = made[0] if made else pack
        ins = (fields, known, with_outer(send), with_mate(send))

    rows_table, lane_table, traces = call(
        functools.partial(tables_kernel, count),
        (
            jax.ShapeDtypeStruct((count, table_rows), BF),
            jax.ShapeDtypeStruct((count, 256), F32),
            jax.ShapeDtypeStruct((NT, count), F32),
        ),
        (cells, recorded, *field_list),
        name="traces",
    )
    index = len(ROUNDS) - 1
    window = rows + 2 * RAD * ROUNDS[index]
    fields, adj = call(
        functools.partial(last_kernel, index),
        (
            jax.ShapeDtypeStruct((ROUNDS[index], rows) + plane, F32),
            jax.ShapeDtypeStruct((2 * NT, count), F32),
        ),
        ins + common + (pack, cells, rows_table, lane_table, traces),
        scratch=[pltpu.VMEM((window,) + plane, F32)] * 2,
        name="forward_last",
    )
    field_list.append(fields)

    sources = call(
        own_sources_kernel, jax.ShapeDtypeStruct((NT, rows) + plane, F32), (adj,), name="own_sources"
    )
    adjs = [sources, with_outer(adj), with_mate(adj), with_even_pair(adj), with_odd_pair(adj)]
    slabs = devices // PIECES
    thick = rows // slabs
    parts = call(
        functools.partial(adjoint_kernel, len(field_list), slabs),
        tuple(jax.ShapeDtypeStruct((thick,) + plane, F32) for _ in range(slabs)),
        (*field_list, zmat, ymat, model, *adjs),
        scratch=[pltpu.VMEM((rows + 2 * HALO,) + plane, F32)] * 2
        + [pltpu.VMEM((rows,) + plane, F32), pltpu.VMEM((5, table_rows, count), BF)]
        + [pltpu.VMEM((5, 2 * NT, count), F32)],
        name="adjoint",
    )
    total = parts[0]
    for i in range(1, slabs):
        total = total + swapped(parts[i], lambda d: d ^ (i * PIECES))
    return total


def solution(mesh):
    return jax.shard_map(
        per_device,
        mesh=mesh,
        in_specs=(
            P("groups", None, None),
            P(("groups", "shot"), None, None),
            P(("groups", "shot"), None, None),
            P(("groups", "shot"), None),
            P(("groups", "shot")),
            P(("groups", "shot")),
            P(("groups", "shot")),
            P(("groups", "shot"), None),
        ),
        out_specs=P(("groups", "shot"), None, None),
        check_vma=False,
    )
```

```python
import functools

import jax
import jax.numpy as jnp
from jax import lax
from jax.experimental import pallas as pl
from jax.experimental.pallas import tpu as pltpu
from jax.sharding import PartitionSpec as P

NT = 8
PIECES = 4
RAD = 4
ROUNDS = (4, 4)
SCALE = 5040.0
CENTER_Y = -43008.0
CENTER_Z = -42.0
WEIGHTS = (8064.0, -1008.0, 128.0, -9.0)
GROUP = 8
HALO = RAD * (NT - 1)
BF = jnp.bfloat16
F32 = jnp.float32

VMEM = pl.BlockSpec(memory_space=pltpu.VMEM)
SMEM = pl.BlockSpec(memory_space=pltpu.SMEM)


def band(distance, center):
    out = jnp.where(distance == 0, center, 0.0)
    for k, weight in enumerate(WEIGHTS, 1):
        out = jnp.where(jnp.abs(distance) == k, weight, out)
    return out


def build_bands(span_y, span_z, rows_out, fixed_out):
    size = GROUP * span_y
    row = lax.broadcasted_iota(jnp.int32, (size, size), 0)
    col = lax.broadcasted_iota(jnp.int32, (size, size), 1)
    tile = 8 * GROUP
    y_row = row // tile * 8 + row % 8
    y_col = col // tile * 8 + col % 8
    same = (row // 8) % GROUP == (col // 8) % GROUP
    rows_out[...] = jnp.where(same, band(y_row - y_col, CENTER_Y), 0.0).astype(BF)
    z = lax.broadcasted_iota(jnp.int32, (2 * span_z, 2 * span_z), 0) % span_z
    to = lax.broadcasted_iota(jnp.int32, (2 * span_z, 2 * span_z), 1)
    fixed_out[...] = jnp.where(to < span_z, band(z - to, CENTER_Z), 0.0).astype(BF)


def split(values):
    high = values.astype(BF)
    low = (values - high.astype(F32)).astype(BF)
    return high, low


def dot(a, b, dims=(((1,), (0,)), ((), ()))):
    return lax.dot_general(a, b, dims, preferred_element_type=F32)


def advance(cur, old, model, zmat, ymat, first, last, model_shift):
    span_y, span_z = cur.shape[1:]
    zmat, ymat = zmat[...], ymat[...]
    for base in range(first, last, GROUP):
        columns = [slice(j, j + 8) for j in range(0, span_y, 8)]
        order = [(i, column) for column in columns for i in range(GROUP)]
        group = jnp.concatenate([cur[base + i, column] for i, column in order], axis=0)
        pair = jnp.concatenate(split(group), axis=1)
        left = jnp.concatenate([ymat, pair], axis=1)
        right = jnp.concatenate([pair, zmat], axis=0)
        part = dot(left, right)
        for j, column in enumerate(columns):
            tiles = [cur[base - RAD + q, column] for q in range(GROUP + 2 * RAD)]
            for i in range(GROUP):
                x = base + i
                at = (j * GROUP + i) * 8
                rows = slice(at, at + 8)
                here = tiles[i + RAD]
                total = part[rows, :span_z] + part[rows, span_z:]
                for k, weight in enumerate(WEIGHTS, 1):
                    total = total + weight * (tiles[i + RAD + k] + tiles[i + RAD - k])
                old[x, column] = (here + here - old[x, column]) + model[x + model_shift, column] * total


def add_source(field, pack, cell, step, own, block, halo, rows):
    span_y, span_z = field.shape[1:]
    plane = own + block * rows + cell // (span_y * span_z)
    y = (cell // span_z) % span_y
    z = cell % span_z

    inside = (plane >= own - halo) & (plane < own + rows + halo)
    plane = jnp.where(inside, plane, own)
    tile = pl.ds(pl.multiple_of((y // 8) * 8, 8), 8)
    sub = lax.broadcasted_iota(jnp.int32, (8, span_z), 0)
    lane = lax.broadcasted_iota(jnp.int32, (8, span_z), 1)
    hit = (sub == jnp.where(inside, y % 8, 8)) & (lane == z)
    field[plane, tile, :] = field[plane, tile, :] + jnp.where(hit, pack[step : step + 1], 0.0)


def parity():
    return lax.rem(lax.axis_index("shot"), 2)


def message_kernel(before, wavelet, source, outer_out, mate_out, pack_out, before_out):
    rows, span_y, span_z = before.shape
    which = lax.broadcasted_iota(jnp.int32, (16, span_z), 0)
    pack = jnp.where(which >= NT, source[0].astype(F32), 0.0)
    for step in range(NT):
        pack = jnp.where(which == step, wavelet[0, step], pack)
    pack_out[...] = pack
    before_out[...] = before[...]
    narrow = RAD * (ROUNDS[0] - 1)
    size = narrow * span_y
    odd = parity()
    outer_out[:size] = before[pl.ds(odd * (rows - narrow), narrow)].reshape(size, span_z)
    mate_out[:size] = before[pl.ds((1 - odd) * (rows - narrow), narrow)].reshape(size, span_z)
    outer_out[size:] = pack
    mate_out[size:] = pack


def prepare_kernel(
    courant, cells, order, observed, pack, now, model_out, cells_out, observed_out, now_out, ymat_out, zmat_out
):
    rows, span_y, span_z = now.shape
    now_out[...] = now[...]
    build_bands(span_y, span_z, ymat_out, zmat_out)
    piece = lax.rem(lax.axis_index("shot"), PIECES)
    period = courant.shape[0]
    window = model_out.shape[0]
    for chunk in range(0, window, RAD):
        source = lax.rem(piece * rows - HALO + chunk + period, period)
        model_out[chunk : chunk + RAD] = courant[pl.ds(source, RAD)] * (1.0 / SCALE)
    count = cells.shape[1]
    wanted = order[...]
    cell = cells[...]
    which = lax.broadcasted_iota(jnp.int32, (16, count), 0)
    digits = jnp.where(which == 0, cell // 256, jnp.where(which == 1, cell % 256, 0)).astype(F32).astype(BF)
    for j in range(0, count, 256):
        index = lax.broadcasted_iota(jnp.int32, (count, 256), 0)
        chosen = jnp.where(index == wanted[:, j : j + 256], 1.0, 0.0).astype(BF)
        found = dot(digits, chosen)
        ordered = found[0:1] * 256.0 + found[1:2]
        cells_out[:, j : j + 256] = jnp.broadcast_to(ordered, (8, 256))
    observed_out[...] = observed[...] + 0.0 * pack[0:1, :]


def pick_tables(cells, table_rows):
    count = cells.shape[1]
    column = jnp.transpose(jnp.broadcast_to(cells.astype(F32), (128, count)))
    column = column.astype(jnp.int32)
    row_of = jnp.concatenate([column // 128] * (table_rows // 128), axis=1)
    lane_of = jnp.concatenate([column % 128] * 2, axis=1)
    lanes = lax.broadcasted_iota(jnp.int32, (count, table_rows), 1)
    rows_table = jnp.where(row_of == lanes, 1.0, 0.0).astype(BF)
    lanes2 = lax.broadcasted_iota(jnp.int32, (count, 256), 1) % 128
    lane_table = jnp.where(lane_of == lanes2, 1.0, 0.0)
    return rows_table, lane_table


def extract(field, step, rows_table, lane_table):
    rows, span_y, span_z = field.shape
    pair = jnp.concatenate(split(field.reshape(rows * span_y, span_z)), axis=1)
    which = lax.broadcasted_iota(jnp.int32, (16, 2 * span_z), 0)
    ones = jnp.where(which == step, 1.0, 0.0).astype(BF)
    out = []
    for j in range(0, rows_table.shape[0], 256):
        found = dot(rows_table[j : j + 256], pair)
        kept = (found * lane_table[j : j + 256]).astype(BF)
        out.append(dot(ones, kept, (((1,), (1,)), ((), ()))))
    return jnp.concatenate(out, axis=1)


def forward_round(
    index, refs_in, zmat, ymat, model, packs, fields, buf_a, buf_b
):
    steps = ROUNDS[index]
    done = sum(ROUNDS[:index])
    rows = 16
    own = RAD * steps
    cur, old = buf_a, buf_b
    wide, narrow = RAD * steps, RAD * (steps - 1)
    odd = parity()
    shape = cur.shape[1:]
    low, high = own - wide, own + rows
    cur_outer = jnp.where(odd == 0, low, high)
    cur_mate = jnp.where(odd == 0, high, low)
    if index == 0:
        now, before, now_outer, now_mate, before_outer, before_mate = refs_in
        cur[own : own + rows] = now[...]
        old[own : own + rows] = before[...]
        cur[pl.ds(cur_outer, wide)] = now_outer[...]
        cur[pl.ds(cur_mate, wide)] = now_mate[...]
        size = narrow * shape[0]
        low = own - narrow
        old[pl.ds(jnp.where(odd == 0, low, high), narrow)] = before_outer[:size].reshape((narrow,) + shape)
        old[pl.ds(jnp.where(odd == 0, high, low), narrow)] = before_mate[:size].reshape((narrow,) + shape)
    else:
        earlier, known, got_outer, got_mate = refs_in
        cur[own : own + rows] = earlier[earlier.shape[0] - 1]
        old[own : own + rows] = earlier[earlier.shape[0] - 2]
        cur[pl.ds(cur_outer, wide)] = got_outer[0:wide]
        cur[pl.ds(cur_mate, wide)] = got_mate[0:wide]
        old[own - RAD : own] = known[0]
        old[own + rows : own + rows + RAD] = known[1]
        low, high = own - narrow, own + rows + RAD
        more = narrow - RAD
        old[pl.ds(jnp.where(odd == 0, low, high), more)] = got_outer[wide:]
        old[pl.ds(jnp.where(odd == 0, high, low), more)] = got_mate[wide:]
    cells = [jnp.max(packs[block, NT : 2 * NT]).astype(jnp.int32) for block in range(3)]
    for step in range(steps):
        halo = RAD * (steps - 1 - step)
        advance(cur, old, model, zmat, ymat, own - halo, own + rows + halo, HALO - own)
        for block in (-1, 0, 1):
            if halo or block == 0:
                pack = packs.at[block + 1]
                add_source(old, pack, cells[block + 1], done + step, own, block, halo, rows)
        fields[step] = old[own : own + rows]
        cur, old = old, cur
    return cur, old, own


def gather_packs(pack_own, outer, mate, packs):
    odd = parity()
    packs[2 * odd] = outer[outer.shape[0] - 16 :]
    packs[1] = pack_own[...]
    packs[2 - 2 * odd] = mate[mate.shape[0] - 16 :]


def forward_kernel(index, *refs):
    take = 6 if index == 0 else 4
    refs_in, refs = refs[:take], refs[take:]
    zmat, ymat, model, pack, fields, known, send = refs[:7]
    if index == 0:
        packs, buf_a, buf_b = refs[7:]
        gather_packs(pack, refs_in[4], refs_in[5], packs)
    else:
        packs, (buf_a, buf_b) = pack, refs[7:]
    cur, old, own = forward_round(index, refs_in, zmat, ymat, model, packs, fields, buf_a, buf_b)
    rows = 16
    known[0] = old[own - RAD : own]
    known[1] = old[own + rows : own + rows + RAD]
    send[0:rows] = cur[own : own + rows]
    send[rows:] = old[own + RAD : own + rows - RAD]


def split_exactly(values):
    high = values.astype(BF)
    rest = values - high.astype(F32)
    middle = rest.astype(BF)
    return high, middle, (rest - middle.astype(F32)).astype(BF)


def in_send_order(observed, count):
    owners = observed.shape[0]
    per_owner = count // owners
    slot = lax.broadcasted_iota(jnp.int32, (owners, count), 1)
    owner = lax.broadcasted_iota(jnp.int32, (owners, count), 0)
    owned = jnp.where(slot // per_owner == owner, 1.0, 0.0).astype(BF)
    spread = jnp.zeros((NT * per_owner, count), F32)
    for part in split_exactly(observed):
        spread = spread + dot(part, owned, (((0,), (0,)), ((), ())))
    line = lax.broadcasted_iota(jnp.int32, (per_owner, count), 0)
    slot = lax.broadcasted_iota(jnp.int32, (per_owner, count), 1)
    hit = slot % per_owner == line
    out = []
    for step in range(NT):
        part = spread[step * per_owner : (step + 1) * per_owner]
        out.append(jnp.sum(jnp.where(hit, part, 0.0), axis=0, keepdims=True))
    return jnp.concatenate(out, axis=0)


def tables_kernel(count, *refs):
    (cells, observed, *fields), (rows_out, lanes_out, traces) = refs[:-3], refs[-3:]
    rows_table, lane_table = pick_tables(cells[0:1].astype(jnp.int32), rows_out.shape[1])
    rows_out[...] = rows_table
    lanes_out[...] = lane_table
    total = jnp.zeros((16, count), F32)
    step = 0
    for group in fields:
        for i in range(group.shape[0]):
            total = total + extract(group[i], step, rows_table, lane_table)
            step += 1
    traces[...] = total[:NT] - in_send_order(observed[...], count)


def last_kernel(index, *refs):
    take = 6 if index == 0 else 4
    refs_in, refs = refs[:take], refs[take:]
    zmat, ymat, model, packs, cells, rows_table, lane_table, traces = refs[:8]
    fields, adj, buf_a, buf_b = refs[8:]
    forward_round(index, refs_in, zmat, ymat, model, packs, fields, buf_a, buf_b)
    done = sum(ROUNDS[:index])
    rows_table = rows_table[...]
    lane_table = lane_table[...]
    total = extract(fields[0], done, rows_table, lane_table)
    for step in range(1, ROUNDS[index]):
        total = total + extract(fields[step], done + step, rows_table, lane_table)
    adj[0:NT] = total[0:NT] + traces[...]
    adj[NT:] = cells[...]


def source_planes(rows_table, lanes, amounts, span_z):
    high = amounts.astype(BF).astype(F32)
    low = amounts - high
    sub = lax.broadcasted_iota(jnp.int32, (span_z, lanes.shape[1]), 0)
    hit = sub == lanes
    both = jnp.concatenate([jnp.where(hit, high, 0.0).astype(BF), jnp.where(hit, low, 0.0).astype(BF)], axis=0)
    added = dot(rows_table, both, (((1,), (1,)), ((), ())))
    return added[:, :span_z] + added[:, span_z:]


def injection_table(cells, table_rows, span_z):
    sub = lax.broadcasted_iota(jnp.int32, (table_rows, cells.shape[1]), 0)
    return jnp.where(sub == cells // span_z, 1.0, 0.0).astype(BF)


def own_sources_kernel(adj, out):
    rows, span_y, span_z = out.shape[1:]
    cells = adj[NT : NT + 1].astype(jnp.int32)
    table = injection_table(cells, rows * span_y, span_z)
    for step in range(NT):
        added = source_planes(table, cells % span_z, adj[step : step + 1], span_z)
        out[step] = added.reshape(rows, span_y, span_z)


def pair_kernel(adj, mate, out):
    odd = parity()
    out[odd] = adj[...]
    out[1 - odd] = mate[...]


def adjoint_kernel(field_groups, slabs, *refs):
    fields = []
    for ref in refs[:field_groups]:
        fields += [ref.at[i] for i in range(ref.shape[0])]
    refs = refs[field_groups:]
    zmat, ymat, model, sources, own_pair, even_pair, odd_pair = refs[:7]
    outs = refs[7 : 7 + slabs]
    buf_a, buf_b, image, rows_table, adjs, near = refs[7 + slabs :]
    odd = parity()
    odd_chip = lax.rem(lax.axis_index("shot") // 2, 2)
    near[2:4] = own_pair[...]
    near[pl.ds(4 - 4 * odd_chip, 2)] = even_pair[...]
    near[pl.ds(4 * odd_chip, 2)] = odd_pair[...]
    rows = 16
    own = HALO
    span_y, span_z = buf_a.shape[1:]
    table_rows = rows * span_y
    lanes = {}
    for block in (-2, -1, 1, 2):
        adjs[block + 2] = near[2 + odd + block]
        cells = adjs[block + 2, NT : NT + 1].astype(jnp.int32)
        rows_table[block + 2] = injection_table(cells, table_rows, span_z)
        lanes[block] = cells % span_z

    def inject(field, number):
        halo = RAD * (NT - number)
        step = NT - number
        for block in range(-2, 3):
            begin = own + block * rows
            first = max(begin, own - halo)
            last = min(begin + rows, own + rows + halo)
            if first >= last:
                continue
            if block:
                table = rows_table[block + 2, (first - begin) * span_y : (last - begin) * span_y, :]
                added = source_planes(table, lanes[block], adjs[block + 2, step : step + 1], span_z)
                added = added.reshape(last - first, span_y, span_z)
            else:
                added = sources[step]
            if number == 1:
                field[first:last] = added
            else:
                field[first:last] = field[first:last] + added

    cur, old = buf_a, buf_b
    inject(cur, 1)
    old[...] = jnp.zeros(old.shape, F32)
    image[...] = cur[own : own + rows] * fields[NT - 1][...]
    for number in range(2, NT + 1):
        halo = RAD * (NT - number)
        advance(cur, old, model, zmat, ymat, own - halo, own + rows + halo, 0)
        inject(old, number)
        image[...] = image[...] + old[own : own + rows] * fields[NT - number][...]
        cur, old = old, cur
    mine = lax.axis_index("shot") // PIECES
    thick = rows // slabs
    for i in range(slabs):
        outs[i][...] = image[pl.ds((mine ^ i) * thick, thick)]


def call(kernel, outs, ins, specs=None, scratch=(), cost=(1e6, 1e6), name=None):
    return pl.pallas_call(
        kernel,
        out_shape=outs,
        in_specs=specs or [VMEM] * len(ins),
        out_specs=jax.tree.map(lambda _: VMEM, outs),
        scratch_shapes=list(scratch),
        compiler_params=pltpu.CompilerParams(vmem_limit_bytes=48 * 1024 * 1024),
        cost_estimate=pl.CostEstimate(flops=int(cost[0]), bytes_accessed=int(cost[1]), transcendentals=0),
        name=name,
    )(*ins)


def swapped(value, partner):
    count = lax.axis_size("shot")
    return lax.ppermute(value, "shot", [(d, partner(d) % count) for d in range(count)])


def with_mate(value):
    return swapped(value, lambda d: d ^ 1)


def with_outer(value):
    return swapped(value, lambda d: d + 1 if d % 2 else d - 1)


def with_even_pair(value):
    return swapped(value, lambda d: d ^ 2)


def with_odd_pair(value):
    return swapped(value, lambda d: d + 2 if d % 4 >= 2 else d - 2)


def per_device(
    courant_sq, wave_now, wave_before, wavelet, source_cell, receiver_cell, send_order, observed
):
    devices = lax.axis_size("shot")
    rows, span_y, span_z = wave_now.shape
    count = receiver_cell.shape[0]
    table_rows = rows * span_y
    plane = (span_y, span_z)

    narrow = RAD * (ROUNDS[0] - 1)
    now_outer, now_mate = with_outer(wave_now), with_mate(wave_now)
    message = jax.ShapeDtypeStruct((narrow * span_y + 16, span_z), F32)
    to_outer, to_mate, pack, before = call(
        message_kernel,
        (message, message, jax.ShapeDtypeStruct((16, span_z), F32), jax.ShapeDtypeStruct(wave_before.shape, F32)),
        (wave_before, wavelet, source_cell),
        specs=[VMEM, SMEM, SMEM],
        name="message",
    )
    before_outer, before_mate = with_outer(to_outer), with_mate(to_mate)

    model, cells, observed, now, ymat, zmat = call(
        prepare_kernel,
        (
            jax.ShapeDtypeStruct((rows + 2 * HALO,) + plane, F32),
            jax.ShapeDtypeStruct((8, count), F32),
            jax.ShapeDtypeStruct(observed.shape, F32),
            jax.ShapeDtypeStruct(wave_now.shape, F32),
            jax.ShapeDtypeStruct((GROUP * span_y, GROUP * span_y), BF),
            jax.ShapeDtypeStruct((2 * span_z, 2 * span_z), BF),
        ),
        (courant_sq, receiver_cell.reshape(1, count), send_order.reshape(1, count), observed, pack, wave_now),
        name="prepare",
    )
    recorded = lax.all_to_all(observed, "shot", split_axis=0, concat_axis=0, tiled=True)

    common = (zmat, ymat, model)
    field_list = []
    ins = (now, before, now_outer, now_mate, before_outer, before_mate)
    for index in range(len(ROUNDS) - 1):
        window = rows + 2 * RAD * ROUNDS[index]
        sent = 2 * rows - 2 * RAD
        packs = (jax.ShapeDtypeStruct((3, 16, span_z), F32),) if index == 0 else ()
        fields, known, send, *made = call(
            functools.partial(forward_kernel, index),
            (
                jax.ShapeDtypeStruct((ROUNDS[index], rows) + plane, F32),
                jax.ShapeDtypeStruct((2, RAD) + plane, F32),
                jax.ShapeDtypeStruct((sent,) + plane, F32),
            )
            + packs,
            ins + common + (pack,),
            scratch=[pltpu.VMEM((window,) + plane, F32)] * 2,
            name="forward",
        )
        field_list.append(fields)
        pack = made[0] if made else pack
        ins = (fields, known, with_outer(send), with_mate(send))

    rows_table, lane_table, traces = call(
        functools.partial(tables_kernel, count),
        (
            jax.ShapeDtypeStruct((count, table_rows), BF),
            jax.ShapeDtypeStruct((count, 256), F32),
            jax.ShapeDtypeStruct((NT, count), F32),
        ),
        (cells, recorded, *field_list),
        name="traces",
    )
    index = len(ROUNDS) - 1
    window = rows + 2 * RAD * ROUNDS[index]
    fields, adj = call(
        functools.partial(last_kernel, index),
        (
            jax.ShapeDtypeStruct((ROUNDS[index], rows) + plane, F32),
            jax.ShapeDtypeStruct((2 * NT, count), F32),
        ),
        ins + common + (pack, cells, rows_table, lane_table, traces),
        scratch=[pltpu.VMEM((window,) + plane, F32)] * 2,
        name="forward_last",
    )
    field_list.append(fields)

    sources = call(
        own_sources_kernel, jax.ShapeDtypeStruct((NT, rows) + plane, F32), (adj,), name="own_sources"
    )
    pair = call(
        pair_kernel, jax.ShapeDtypeStruct((2, 2 * NT, count), F32), (adj, with_mate(adj)), name="pair"
    )
    adjs = [sources, pair, with_even_pair(pair), with_odd_pair(pair)]
    slabs = devices // PIECES
    thick = rows // slabs
    parts = call(
        functools.partial(adjoint_kernel, len(field_list), slabs),
        tuple(jax.ShapeDtypeStruct((thick,) + plane, F32) for _ in range(slabs)),
        (*field_list, zmat, ymat, model, *adjs),
        scratch=[pltpu.VMEM((rows + 2 * HALO,) + plane, F32)] * 2
        + [pltpu.VMEM((rows,) + plane, F32), pltpu.VMEM((5, table_rows, count), BF)]
        + [pltpu.VMEM((5, 2 * NT, count), F32), pltpu.VMEM((6, 2 * NT, count), F32)],
        name="adjoint",
    )
    total = parts[0]
    for i in range(1, slabs):
        total = total + swapped(parts[i], lambda d: d ^ (i * PIECES))
    return total


def solution(mesh):
    return jax.shard_map(
        per_device,
        mesh=mesh,
        in_specs=(
            P("groups", None, None),
            P(("groups", "shot"), None, None),
            P(("groups", "shot"), None, None),
            P(("groups", "shot"), None),
            P(("groups", "shot")),
            P(("groups", "shot")),
            P(("groups", "shot")),
            P(("groups", "shot"), None),
        ),
        out_specs=P(("groups", "shot"), None, None),
        check_vma=False,
    )
```

```python
import functools

import jax
import jax.numpy as jnp
from jax import lax
from jax.experimental import pallas as pl
from jax.experimental.pallas import tpu as pltpu
from jax.sharding import PartitionSpec as P

NT = 8
PIECES = 4
RAD = 4
ROUNDS = (4, 4)
SCALE = 5040.0
CENTER_Y = -43008.0
CENTER_Z = -42.0
WEIGHTS = (8064.0, -1008.0, 128.0, -9.0)
GROUP = 8
HALO = RAD * (NT - 1)
BF = jnp.bfloat16
F32 = jnp.float32

VMEM = pl.BlockSpec(memory_space=pltpu.VMEM)
SMEM = pl.BlockSpec(memory_space=pltpu.SMEM)


def band(distance, center):
    out = jnp.where(distance == 0, center, 0.0)
    for k, weight in enumerate(WEIGHTS, 1):
        out = jnp.where(jnp.abs(distance) == k, weight, out)
    return out


def build_bands(span_y, span_z, rows_out, fixed_out):
    size = GROUP * span_y
    row = lax.broadcasted_iota(jnp.int32, (size, size), 0)
    col = lax.broadcasted_iota(jnp.int32, (size, size), 1)
    tile = 8 * GROUP
    y_row = row // tile * 8 + row % 8
    y_col = col // tile * 8 + col % 8
    same = (row // 8) % GROUP == (col // 8) % GROUP
    rows_out[...] = jnp.where(same, band(y_row - y_col, CENTER_Y), 0.0).astype(BF)
    z = lax.broadcasted_iota(jnp.int32, (2 * span_z, 2 * span_z), 0) % span_z
    to = lax.broadcasted_iota(jnp.int32, (2 * span_z, 2 * span_z), 1)
    fixed_out[...] = jnp.where(to < span_z, band(z - to, CENTER_Z), 0.0).astype(BF)


def split(values):
    high = values.astype(BF)
    low = (values - high.astype(F32)).astype(BF)
    return high, low


def dot(a, b, dims=(((1,), (0,)), ((), ()))):
    return lax.dot_general(a, b, dims, preferred_element_type=F32)


def advance(cur, old, model, zmat, ymat, first, last, model_shift):
    span_y, span_z = cur.shape[1:]
    zmat, ymat = zmat[...], ymat[...]
    for base in range(first, last, GROUP):
        columns = [slice(j, j + 8) for j in range(0, span_y, 8)]
        order = [(i, column) for column in columns for i in range(GROUP)]
        group = jnp.concatenate([cur[base + i, column] for i, column in order], axis=0)
        pair = jnp.concatenate(split(group), axis=1)
        left = jnp.concatenate([ymat, pair], axis=1)
        right = jnp.concatenate([pair, zmat], axis=0)
        part = dot(left, right)
        for j, column in enumerate(columns):
            tiles = [cur[base - RAD + q, column] for q in range(GROUP + 2 * RAD)]
            for i in range(GROUP):
                x = base + i
                at = (j * GROUP + i) * 8
                rows = slice(at, at + 8)
                here = tiles[i + RAD]
                total = part[rows, :span_z] + part[rows, span_z:]
                for k, weight in enumerate(WEIGHTS, 1):
                    total = total + weight * (tiles[i + RAD + k] + tiles[i + RAD - k])
                old[x, column] = (here + here - old[x, column]) + model[x + model_shift, column] * total


def add_source(field, pack, cell, step, own, block, halo, rows):
    span_y, span_z = field.shape[1:]
    plane = own + block * rows + cell // (span_y * span_z)
    y = (cell // span_z) % span_y
    z = cell % span_z

    inside = (plane >= own - halo) & (plane < own + rows + halo)
    plane = jnp.where(inside, plane, own)
    tile = pl.ds(pl.multiple_of((y // 8) * 8, 8), 8)
    sub = lax.broadcasted_iota(jnp.int32, (8, span_z), 0)
    lane = lax.broadcasted_iota(jnp.int32, (8, span_z), 1)
    hit = (sub == jnp.where(inside, y % 8, 8)) & (lane == z)
    field[plane, tile, :] = field[plane, tile, :] + jnp.where(hit, pack[step : step + 1], 0.0)


def parity():
    return lax.rem(lax.axis_index("shot"), 2)


def message_kernel(now, before, wavelet, source, outer_out, mate_out, pack_out, now_out, before_out):
    rows, span_y, span_z = before.shape
    which = lax.broadcasted_iota(jnp.int32, (16, span_z), 0)
    pack = jnp.where(which >= NT, source[0].astype(F32), 0.0)
    for step in range(NT):
        pack = jnp.where(which == step, wavelet[0, step], pack)
    pack_out[...] = pack
    narrow = RAD * (ROUNDS[0] - 1)
    wide = rows * span_y
    size = wide + narrow * span_y
    odd = parity()
    field = now[...]
    now_out[...] = field
    before_out[...] = before[...]
    for out, side in ((outer_out, odd), (mate_out, 1 - odd)):
        out[:wide] = field.reshape(wide, span_z)
        out[wide:size] = before[pl.ds(side * (rows - narrow), narrow)].reshape(size - wide, span_z)
        out[size:] = pack


def prepare_kernel(courant, cells, order, observed, pack, model_out, cells_out, ymat_out, zmat_out, *parts_out):
    rows = 16
    span_y, span_z = courant.shape[1:]
    build_bands(span_y, span_z, ymat_out, zmat_out)
    piece = lax.rem(lax.axis_index("shot"), PIECES)
    period = courant.shape[0]
    window = model_out.shape[0]
    for chunk in range(0, window, RAD):
        source = lax.rem(piece * rows - HALO + chunk + period, period)
        model_out[chunk : chunk + RAD] = courant[pl.ds(source, RAD)] * (1.0 / SCALE)
    count = cells.shape[1]
    wanted = order[...]
    cell = cells[...]
    which = lax.broadcasted_iota(jnp.int32, (16, count), 0)
    digits = jnp.where(which == 0, cell // 256, jnp.where(which == 1, cell % 256, 0)).astype(F32).astype(BF)
    for j in range(0, count, 256):
        index = lax.broadcasted_iota(jnp.int32, (count, 256), 0)
        chosen = jnp.where(index == wanted[:, j : j + 256], 1.0, 0.0).astype(BF)
        found = dot(digits, chosen)
        ordered = found[0:1] * 256.0 + found[1:2]
        cells_out[:, j : j + 256] = jnp.broadcast_to(ordered, (8, 256))
    period = lax.axis_index("shot") // PIECES
    for i, out in enumerate(parts_out):
        out[...] = observed[pl.ds((period ^ i) * PIECES, PIECES)]


def middle_kernel(*refs):
    half = len(refs) - PIECES - 1
    (pack, *parts), (pack_out, *outs) = refs[:half], refs[half:]
    pack_out[...] = pack[...]
    period = lax.axis_index("shot") // PIECES
    piece = lax.rem(lax.axis_index("shot"), PIECES)
    for i, part in enumerate(parts):
        for j, out in enumerate(outs):
            out[period ^ i] = part[piece ^ j]


def pick_tables(cells, table_rows):
    count = cells.shape[1]
    column = jnp.transpose(jnp.broadcast_to(cells.astype(F32), (128, count)))
    column = column.astype(jnp.int32)
    row_of = jnp.concatenate([column // 128] * (table_rows // 128), axis=1)
    lane_of = jnp.concatenate([column % 128] * 2, axis=1)
    lanes = lax.broadcasted_iota(jnp.int32, (count, table_rows), 1)
    rows_table = jnp.where(row_of == lanes, 1.0, 0.0).astype(BF)
    lanes2 = lax.broadcasted_iota(jnp.int32, (count, 256), 1) % 128
    lane_table = jnp.where(lane_of == lanes2, 1.0, 0.0)
    return rows_table, lane_table


def extract(field, step, rows_table, lane_table):
    rows, span_y, span_z = field.shape
    pair = jnp.concatenate(split(field.reshape(rows * span_y, span_z)), axis=1)
    which = lax.broadcasted_iota(jnp.int32, (16, 2 * span_z), 0)
    ones = jnp.where(which == step, 1.0, 0.0).astype(BF)
    out = []
    for j in range(0, rows_table.shape[0], 256):
        found = dot(rows_table[j : j + 256], pair)
        kept = (found * lane_table[j : j + 256]).astype(BF)
        out.append(dot(ones, kept, (((1,), (1,)), ((), ()))))
    return jnp.concatenate(out, axis=1)


def forward_round(
    index, refs_in, zmat, ymat, model, packs, fields, buf_a, buf_b
):
    steps = ROUNDS[index]
    done = sum(ROUNDS[:index])
    rows = 16
    own = RAD * steps
    cur, old = buf_a, buf_b
    wide, narrow = RAD * steps, RAD * (steps - 1)
    odd = parity()
    shape = cur.shape[1:]
    low, high = own - wide, own + rows
    cur_outer = jnp.where(odd == 0, low, high)
    cur_mate = jnp.where(odd == 0, high, low)
    if index == 0:
        now, before, got_outer, got_mate = refs_in
        edge = wide * shape[0]
        cur[own : own + rows] = now[...]
        old[own : own + rows] = before[...]
        cur[pl.ds(cur_outer, wide)] = got_outer[:edge].reshape((wide,) + shape)
        cur[pl.ds(cur_mate, wide)] = got_mate[:edge].reshape((wide,) + shape)
        size = edge + narrow * shape[0]
        low = own - narrow
        old[pl.ds(jnp.where(odd == 0, low, high), narrow)] = got_outer[edge:size].reshape((narrow,) + shape)
        old[pl.ds(jnp.where(odd == 0, high, low), narrow)] = got_mate[edge:size].reshape((narrow,) + shape)
    else:
        earlier, known, got_outer, got_mate = refs_in
        cur[own : own + rows] = earlier[earlier.shape[0] - 1]
        old[own : own + rows] = earlier[earlier.shape[0] - 2]
        cur[pl.ds(cur_outer, wide)] = got_outer[0:wide]
        cur[pl.ds(cur_mate, wide)] = got_mate[0:wide]
        old[own - RAD : own] = known[0]
        old[own + rows : own + rows + RAD] = known[1]
        low, high = own - narrow, own + rows + RAD
        more = narrow - RAD
        old[pl.ds(jnp.where(odd == 0, low, high), more)] = got_outer[wide:]
        old[pl.ds(jnp.where(odd == 0, high, low), more)] = got_mate[wide:]
    cells = [jnp.max(packs[block, NT : 2 * NT]).astype(jnp.int32) for block in range(3)]
    for step in range(steps):
        halo = RAD * (steps - 1 - step)
        advance(cur, old, model, zmat, ymat, own - halo, own + rows + halo, HALO - own)
        for block in (-1, 0, 1):
            if halo or block == 0:
                pack = packs.at[block + 1]
                add_source(old, pack, cells[block + 1], done + step, own, block, halo, rows)
        fields[step] = old[own : own + rows]
        cur, old = old, cur
    return cur, old, own


def gather_packs(pack_own, outer, mate, packs):
    odd = parity()
    packs[2 * odd] = outer[outer.shape[0] - 16 :]
    packs[1] = pack_own[...]
    packs[2 - 2 * odd] = mate[mate.shape[0] - 16 :]


def forward_kernel(index, *refs):
    refs_in, refs = refs[:4], refs[4:]
    zmat, ymat, model, pack, fields, known, send = refs[:7]
    if index == 0:
        packs, buf_a, buf_b = refs[7:]
        gather_packs(pack, refs_in[2], refs_in[3], packs)
    else:
        packs, (buf_a, buf_b) = pack, refs[7:]
    cur, old, own = forward_round(index, refs_in, zmat, ymat, model, packs, fields, buf_a, buf_b)
    rows = 16
    known[0] = old[own - RAD : own]
    known[1] = old[own + rows : own + rows + RAD]
    send[0:rows] = cur[own : own + rows]
    send[rows:] = old[own + RAD : own + rows - RAD]


def split_exactly(values):
    high = values.astype(BF)
    rest = values - high.astype(F32)
    middle = rest.astype(BF)
    return high, middle, (rest - middle.astype(F32)).astype(BF)


def in_send_order(observed, count):
    owners = observed.shape[0]
    per_owner = count // owners
    slot = lax.broadcasted_iota(jnp.int32, (owners, count), 1)
    owner = lax.broadcasted_iota(jnp.int32, (owners, count), 0)
    owned = jnp.where(slot // per_owner == owner, 1.0, 0.0).astype(BF)
    spread = jnp.zeros((NT * per_owner, count), F32)
    for part in split_exactly(observed):
        spread = spread + dot(part, owned, (((0,), (0,)), ((), ())))
    line = lax.broadcasted_iota(jnp.int32, (per_owner, count), 0)
    slot = lax.broadcasted_iota(jnp.int32, (per_owner, count), 1)
    hit = slot % per_owner == line
    out = []
    for step in range(NT):
        part = spread[step * per_owner : (step + 1) * per_owner]
        out.append(jnp.sum(jnp.where(hit, part, 0.0), axis=0, keepdims=True))
    return jnp.concatenate(out, axis=0)


def tables_kernel(count, *refs):
    (cells, *refs), (rows_out, lanes_out, traces, observed) = refs[:-4], refs[-4:]
    groups, fields = refs[:PIECES], refs[PIECES:]
    piece = lax.rem(lax.axis_index("shot"), PIECES)
    for j, group in enumerate(groups):
        for period in range(group.shape[0]):
            observed[pl.ds(period * PIECES + (piece ^ j), 1)] = group[period]
    rows_table, lane_table = pick_tables(cells[0:1].astype(jnp.int32), rows_out.shape[1])
    rows_out[...] = rows_table
    lanes_out[...] = lane_table
    total = jnp.zeros((16, count), F32)
    step = 0
    for group in fields:
        for i in range(group.shape[0]):
            total = total + extract(group[i], step, rows_table, lane_table)
            step += 1
    traces[...] = total[:NT] - in_send_order(observed[...], count)


def last_kernel(index, *refs):
    refs_in, refs = refs[:4], refs[4:]
    zmat, ymat, model, packs, cells, rows_table, lane_table, traces = refs[:8]
    fields, adj, buf_a, buf_b = refs[8:]
    forward_round(index, refs_in, zmat, ymat, model, packs, fields, buf_a, buf_b)
    done = sum(ROUNDS[:index])
    rows_table = rows_table[...]
    lane_table = lane_table[...]
    total = extract(fields[0], done, rows_table, lane_table)
    for step in range(1, ROUNDS[index]):
        total = total + extract(fields[step], done + step, rows_table, lane_table)
    adj[0:NT] = total[0:NT] + traces[...]
    adj[NT:] = cells[...]


def source_planes(rows_table, lanes, amounts, span_z):
    high = amounts.astype(BF).astype(F32)
    low = amounts - high
    sub = lax.broadcasted_iota(jnp.int32, (span_z, lanes.shape[1]), 0)
    hit = sub == lanes
    both = jnp.concatenate([jnp.where(hit, high, 0.0).astype(BF), jnp.where(hit, low, 0.0).astype(BF)], axis=0)
    added = dot(rows_table, both, (((1,), (1,)), ((), ())))
    return added[:, :span_z] + added[:, span_z:]


def injection_table(cells, table_rows, span_z):
    sub = lax.broadcasted_iota(jnp.int32, (table_rows, cells.shape[1]), 0)
    return jnp.where(sub == cells // span_z, 1.0, 0.0).astype(BF)


def own_sources_kernel(adj, out):
    rows, span_y, span_z = out.shape[1:]
    cells = adj[NT : NT + 1].astype(jnp.int32)
    table = injection_table(cells, rows * span_y, span_z)
    for step in range(NT):
        added = source_planes(table, cells % span_z, adj[step : step + 1], span_z)
        out[step] = added.reshape(rows, span_y, span_z)


def pair_kernel(adj, mate, out):
    odd = parity()
    out[odd] = adj[...]
    out[1 - odd] = mate[...]


def adjoint_kernel(field_groups, slabs, *refs):
    fields = []
    for ref in refs[:field_groups]:
        fields += [ref.at[i] for i in range(ref.shape[0])]
    refs = refs[field_groups:]
    zmat, ymat, model, sources, own_pair, even_pair, odd_pair = refs[:7]
    outs = refs[7 : 7 + slabs]
    buf_a, buf_b, image, rows_table, adjs, near = refs[7 + slabs :]
    odd = parity()
    odd_chip = lax.rem(lax.axis_index("shot") // 2, 2)
    near[2:4] = own_pair[...]
    near[pl.ds(4 - 4 * odd_chip, 2)] = even_pair[...]
    near[pl.ds(4 * odd_chip, 2)] = odd_pair[...]
    rows = 16
    own = HALO
    span_y, span_z = buf_a.shape[1:]
    table_rows = rows * span_y
    lanes = {}
    for block in (-2, -1, 1, 2):
        adjs[block + 2] = near[2 + odd + block]
        cells = adjs[block + 2, NT : NT + 1].astype(jnp.int32)
        rows_table[block + 2] = injection_table(cells, table_rows, span_z)
        lanes[block] = cells % span_z

    def inject(field, number):
        halo = RAD * (NT - number)
        step = NT - number
        for block in range(-2, 3):
            begin = own + block * rows
            first = max(begin, own - halo)
            last = min(begin + rows, own + rows + halo)
            if first >= last:
                continue
            if block:
                table = rows_table[block + 2, (first - begin) * span_y : (last - begin) * span_y, :]
                added = source_planes(table, lanes[block], adjs[block + 2, step : step + 1], span_z)
                added = added.reshape(last - first, span_y, span_z)
            else:
                added = sources[step]
            if number == 1:
                field[first:last] = added
            else:
                field[first:last] = field[first:last] + added

    cur, old = buf_a, buf_b
    inject(cur, 1)
    old[...] = jnp.zeros(old.shape, F32)
    image[...] = cur[own : own + rows] * fields[NT - 1][...]
    for number in range(2, NT + 1):
        halo = RAD * (NT - number)
        advance(cur, old, model, zmat, ymat, own - halo, own + rows + halo, 0)
        inject(old, number)
        image[...] = image[...] + old[own : own + rows] * fields[NT - number][...]
        cur, old = old, cur
    mine = lax.axis_index("shot") // PIECES
    thick = rows // slabs
    for i in range(slabs):
        outs[i][...] = image[pl.ds((mine ^ i) * thick, thick)]


def call(kernel, outs, ins, specs=None, scratch=(), cost=(1e6, 1e6), name=None):
    return pl.pallas_call(
        kernel,
        out_shape=outs,
        in_specs=specs or [VMEM] * len(ins),
        out_specs=jax.tree.map(lambda _: VMEM, outs),
        scratch_shapes=list(scratch),
        compiler_params=pltpu.CompilerParams(vmem_limit_bytes=48 * 1024 * 1024),
        cost_estimate=pl.CostEstimate(flops=int(cost[0]), bytes_accessed=int(cost[1]), transcendentals=0),
        name=name,
    )(*ins)


def swapped(value, partner):
    count = lax.axis_size("shot")
    return lax.ppermute(value, "shot", [(d, partner(d) % count) for d in range(count)])


def with_mate(value):
    return swapped(value, lambda d: d ^ 1)


def with_outer(value):
    return swapped(value, lambda d: d + 1 if d % 2 else d - 1)


def with_even_pair(value):
    return swapped(value, lambda d: d ^ 2)


def with_odd_pair(value):
    return swapped(value, lambda d: d + 2 if d % 4 >= 2 else d - 2)


def per_device(
    courant_sq, wave_now, wave_before, wavelet, source_cell, receiver_cell, send_order, observed
):
    devices = lax.axis_size("shot")
    rows, span_y, span_z = wave_now.shape
    count = receiver_cell.shape[0]
    table_rows = rows * span_y
    plane = (span_y, span_z)

    narrow = RAD * (ROUNDS[0] - 1)
    message = jax.ShapeDtypeStruct(((rows + narrow) * span_y + 16, span_z), F32)
    to_outer, to_mate, pack, now, before = call(
        message_kernel,
        (
            message,
            message,
            jax.ShapeDtypeStruct((16, span_z), F32),
            jax.ShapeDtypeStruct(wave_now.shape, F32),
            jax.ShapeDtypeStruct(wave_before.shape, F32),
        ),
        (wave_now, wave_before, wavelet, source_cell),
        specs=[VMEM, VMEM, SMEM, SMEM],
        name="message",
    )
    got_outer, got_mate = with_outer(to_outer), with_mate(to_mate)

    slabs = devices // PIECES
    part = jax.ShapeDtypeStruct((PIECES, 1, observed.shape[1]), F32)
    model, cells, ymat, zmat, *parts = call(
        prepare_kernel,
        (
            jax.ShapeDtypeStruct((rows + 2 * HALO,) + plane, F32),
            jax.ShapeDtypeStruct((8, count), F32),
            jax.ShapeDtypeStruct((GROUP * span_y, GROUP * span_y), BF),
            jax.ShapeDtypeStruct((2 * span_z, 2 * span_z), BF),
        )
        + (part,) * slabs,
        (
            courant_sq,
            receiver_cell.reshape(1, count),
            send_order.reshape(1, count),
            observed.reshape(devices, 1, observed.shape[1]),
            pack,
        ),
        name="prepare",
    )
    parts[1:] = [swapped(parts[i], lambda d: d ^ (i * PIECES)) for i in range(1, slabs)]
    pack, *groups = call(
        middle_kernel,
        (jax.ShapeDtypeStruct(pack.shape, F32),)
        + (jax.ShapeDtypeStruct((slabs, 1, observed.shape[1]), F32),) * PIECES,
        (pack, *parts),
        name="middle",
    )
    groups = [groups[0]] + [swapped(groups[j], lambda d: d ^ j) for j in range(1, PIECES)]

    common = (zmat, ymat, model)
    field_list = []
    ins = (now, before, got_outer, got_mate)
    for index in range(len(ROUNDS) - 1):
        window = rows + 2 * RAD * ROUNDS[index]
        sent = 2 * rows - 2 * RAD
        packs = (jax.ShapeDtypeStruct((3, 16, span_z), F32),) if index == 0 else ()
        fields, known, send, *made = call(
            functools.partial(forward_kernel, index),
            (
                jax.ShapeDtypeStruct((ROUNDS[index], rows) + plane, F32),
                jax.ShapeDtypeStruct((2, RAD) + plane, F32),
                jax.ShapeDtypeStruct((sent,) + plane, F32),
            )
            + packs,
            ins + common + (pack,),
            scratch=[pltpu.VMEM((window,) + plane, F32)] * 2,
            name="forward",
        )
        field_list.append(fields)
        pack = made[0] if made else pack
        ins = (fields, known, with_outer(send), with_mate(send))

    rows_table, lane_table, traces = call(
        functools.partial(tables_kernel, count),
        (
            jax.ShapeDtypeStruct((count, table_rows), BF),
            jax.ShapeDtypeStruct((count, 256), F32),
            jax.ShapeDtypeStruct((NT, count), F32),
        ),
        (cells, *groups, *field_list),
        scratch=[pltpu.VMEM(observed.shape, F32)],
        name="traces",
    )
    index = len(ROUNDS) - 1
    window = rows + 2 * RAD * ROUNDS[index]
    fields, adj = call(
        functools.partial(last_kernel, index),
        (
            jax.ShapeDtypeStruct((ROUNDS[index], rows) + plane, F32),
            jax.ShapeDtypeStruct((2 * NT, count), F32),
        ),
        ins + common + (pack, cells, rows_table, lane_table, traces),
        scratch=[pltpu.VMEM((window,) + plane, F32)] * 2,
        name="forward_last",
    )
    field_list.append(fields)

    sources = call(
        own_sources_kernel, jax.ShapeDtypeStruct((NT, rows) + plane, F32), (adj,), name="own_sources"
    )
    pair = call(
        pair_kernel, jax.ShapeDtypeStruct((2, 2 * NT, count), F32), (adj, with_mate(adj)), name="pair"
    )
    adjs = [sources, pair, with_even_pair(pair), with_odd_pair(pair)]
    thick = rows // slabs
    parts = call(
        functools.partial(adjoint_kernel, len(field_list), slabs),
        tuple(jax.ShapeDtypeStruct((thick,) + plane, F32) for _ in range(slabs)),
        (*field_list, zmat, ymat, model, *adjs),
        scratch=[pltpu.VMEM((rows + 2 * HALO,) + plane, F32)] * 2
        + [pltpu.VMEM((rows,) + plane, F32), pltpu.VMEM((5, table_rows, count), BF)]
        + [pltpu.VMEM((5, 2 * NT, count), F32), pltpu.VMEM((6, 2 * NT, count), F32)],
        name="adjoint",
    )
    total = parts[0]
    for i in range(1, slabs):
        total = total + swapped(parts[i], lambda d: d ^ (i * PIECES))
    return total


def solution(mesh):
    return jax.shard_map(
        per_device,
        mesh=mesh,
        in_specs=(
            P("groups", None, None),
            P(("groups", "shot"), None, None),
            P(("groups", "shot"), None, None),
            P(("groups", "shot"), None),
            P(("groups", "shot")),
            P(("groups", "shot")),
            P(("groups", "shot")),
            P(("groups", "shot"), None),
        ),
        out_specs=P(("groups", "shot"), None, None),
        check_vma=False,
    )
```

```python
import functools

import jax
import jax.numpy as jnp
from jax import lax
from jax.experimental import pallas as pl
from jax.experimental.pallas import tpu as pltpu
from jax.sharding import PartitionSpec as P

NT = 8
PIECES = 4
RAD = 4
ROUNDS = (4, 4)
SCALE = 5040.0
CENTER_Y = -43008.0
CENTER_Z = -42.0
WEIGHTS = (8064.0, -1008.0, 128.0, -9.0)
GROUP = 8
HALO = RAD * (NT - 1)
BF = jnp.bfloat16
F32 = jnp.float32

VMEM = pl.BlockSpec(memory_space=pltpu.VMEM)
SMEM = pl.BlockSpec(memory_space=pltpu.SMEM)


def band(distance, center):
    out = jnp.where(distance == 0, center, 0.0)
    for k, weight in enumerate(WEIGHTS, 1):
        out = jnp.where(jnp.abs(distance) == k, weight, out)
    return out


def build_bands(span_y, span_z, rows_out, fixed_out):
    size = GROUP * span_y
    row = lax.broadcasted_iota(jnp.int32, (size, size), 0)
    col = lax.broadcasted_iota(jnp.int32, (size, size), 1)
    tile = 8 * GROUP
    y_row = row // tile * 8 + row % 8
    y_col = col // tile * 8 + col % 8
    same = (row // 8) % GROUP == (col // 8) % GROUP
    rows_out[...] = jnp.where(same, band(y_row - y_col, CENTER_Y), 0.0).astype(BF)
    z = lax.broadcasted_iota(jnp.int32, (2 * span_z, 2 * span_z), 0) % span_z
    to = lax.broadcasted_iota(jnp.int32, (2 * span_z, 2 * span_z), 1)
    fixed_out[...] = jnp.where(to < span_z, band(z - to, CENTER_Z), 0.0).astype(BF)


def split(values):
    high = values.astype(BF)
    low = (values - high.astype(F32)).astype(BF)
    return high, low


def dot(a, b, dims=(((1,), (0,)), ((), ()))):
    return lax.dot_general(a, b, dims, preferred_element_type=F32)


def advance(cur, old, model, zmat, ymat, first, last, model_shift):
    span_y, span_z = cur.shape[1:]
    zmat, ymat = zmat[...], ymat[...]
    for base in range(first, last, GROUP):
        columns = [slice(j, j + 8) for j in range(0, span_y, 8)]
        order = [(i, column) for column in columns for i in range(GROUP)]
        group = jnp.concatenate([cur[base + i, column] for i, column in order], axis=0)
        pair = jnp.concatenate(split(group), axis=1)
        left = jnp.concatenate([ymat, pair], axis=1)
        right = jnp.concatenate([pair, zmat], axis=0)
        part = dot(left, right)
        for j, column in enumerate(columns):
            tiles = [cur[base - RAD + q, column] for q in range(GROUP + 2 * RAD)]
            for i in range(GROUP):
                x = base + i
                at = (j * GROUP + i) * 8
                rows = slice(at, at + 8)
                here = tiles[i + RAD]
                total = part[rows, :span_z] + part[rows, span_z:]
                for k, weight in enumerate(WEIGHTS, 1):
                    total = total + weight * (tiles[i + RAD + k] + tiles[i + RAD - k])
                old[x, column] = (here + here - old[x, column]) + model[x + model_shift, column] * total


def add_source(field, pack, cell, step, own, block, halo, rows):
    span_y, span_z = field.shape[1:]
    plane = own + block * rows + cell // (span_y * span_z)
    y = (cell // span_z) % span_y
    z = cell % span_z

    inside = (plane >= own - halo) & (plane < own + rows + halo)
    plane = jnp.where(inside, plane, own)
    tile = pl.ds(pl.multiple_of((y // 8) * 8, 8), 8)
    sub = lax.broadcasted_iota(jnp.int32, (8, span_z), 0)
    lane = lax.broadcasted_iota(jnp.int32, (8, span_z), 1)
    hit = (sub == jnp.where(inside, y % 8, 8)) & (lane == z)
    field[plane, tile, :] = field[plane, tile, :] + jnp.where(hit, pack[step : step + 1], 0.0)


def parity():
    return lax.rem(lax.axis_index("shot"), 2)


def message_kernel(before, wavelet, source, outer_out, mate_out, pack_out, before_out):
    rows, span_y, span_z = before.shape
    which = lax.broadcasted_iota(jnp.int32, (16, span_z), 0)
    pack = jnp.where(which >= NT, source[0].astype(F32), 0.0)
    for step in range(NT):
        pack = jnp.where(which == step, wavelet[0, step], pack)
    pack_out[...] = pack
    before_out[...] = before[...]
    narrow = RAD * (ROUNDS[0] - 1)
    size = narrow * span_y
    odd = parity()
    outer_out[:size] = before[pl.ds(odd * (rows - narrow), narrow)].reshape(size, span_z)
    mate_out[:size] = before[pl.ds((1 - odd) * (rows - narrow), narrow)].reshape(size, span_z)
    outer_out[size:] = pack
    mate_out[size:] = pack


def prepare_kernel(
    courant, cells, order, observed, pack, now, model_out, cells_out, observed_out, now_out, ymat_out, zmat_out
):
    rows, span_y, span_z = now.shape
    now_out[...] = now[...]
    build_bands(span_y, span_z, ymat_out, zmat_out)
    piece = lax.rem(lax.axis_index("shot"), PIECES)
    period = courant.shape[0]
    window = model_out.shape[0]
    for chunk in range(0, window, RAD):
        source = lax.rem(piece * rows - HALO + chunk + period, period)
        model_out[chunk : chunk + RAD] = courant[pl.ds(source, RAD)] * (1.0 / SCALE)
    count = cells.shape[1]
    wanted = order[...]
    cell = cells[...]
    which = lax.broadcasted_iota(jnp.int32, (16, count), 0)
    digits = jnp.where(which == 0, cell // 256, jnp.where(which == 1, cell % 256, 0)).astype(F32).astype(BF)
    for j in range(0, count, 256):
        index = lax.broadcasted_iota(jnp.int32, (count, 256), 0)
        chosen = jnp.where(index == wanted[:, j : j + 256], 1.0, 0.0).astype(BF)
        found = dot(digits, chosen)
        ordered = found[0:1] * 256.0 + found[1:2]
        cells_out[:, j : j + 256] = jnp.broadcast_to(ordered, (8, 256))
    observed_out[...] = observed[...] + 0.0 * pack[0:1, :]


def pick_tables(cells, table_rows):
    count = cells.shape[1]
    column = jnp.transpose(jnp.broadcast_to(cells.astype(F32), (128, count)))
    column = column.astype(jnp.int32)
    row_of = jnp.concatenate([column // 128] * (table_rows // 128), axis=1)
    lane_of = jnp.concatenate([column % 128] * 2, axis=1)
    lanes = lax.broadcasted_iota(jnp.int32, (count, table_rows), 1)
    rows_table = jnp.where(row_of == lanes, 1.0, 0.0).astype(BF)
    lanes2 = lax.broadcasted_iota(jnp.int32, (count, 256), 1) % 128
    lane_table = jnp.where(lane_of == lanes2, 1.0, 0.0)
    return rows_table, lane_table


def extract(field, step, rows_table, lane_table):
    rows, span_y, span_z = field.shape
    pair = jnp.concatenate(split(field.reshape(rows * span_y, span_z)), axis=1)
    which = lax.broadcasted_iota(jnp.int32, (16, 2 * span_z), 0)
    ones = jnp.where(which == step, 1.0, 0.0).astype(BF)
    out = []
    for j in range(0, rows_table.shape[0], 256):
        found = dot(rows_table[j : j + 256], pair)
        kept = (found * lane_table[j : j + 256]).astype(BF)
        out.append(dot(ones, kept, (((1,), (1,)), ((), ()))))
    return jnp.concatenate(out, axis=1)


def forward_round(
    index, refs_in, zmat, ymat, model, packs, fields, buf_a, buf_b, after_step=None
):
    steps = ROUNDS[index]
    done = sum(ROUNDS[:index])
    rows = 16
    own = RAD * steps
    cur, old = buf_a, buf_b
    wide, narrow = RAD * steps, RAD * (steps - 1)
    odd = parity()
    shape = cur.shape[1:]
    low, high = own - wide, own + rows
    cur_outer = jnp.where(odd == 0, low, high)
    cur_mate = jnp.where(odd == 0, high, low)
    if index == 0:
        now, before, now_outer, now_mate, before_outer, before_mate = refs_in
        cur[own : own + rows] = now[...]
        old[own : own + rows] = before[...]
        cur[pl.ds(cur_outer, wide)] = now_outer[...]
        cur[pl.ds(cur_mate, wide)] = now_mate[...]
        size = narrow * shape[0]
        low = own - narrow
        old[pl.ds(jnp.where(odd == 0, low, high), narrow)] = before_outer[:size].reshape((narrow,) + shape)
        old[pl.ds(jnp.where(odd == 0, high, low), narrow)] = before_mate[:size].reshape((narrow,) + shape)
    else:
        earlier, known, got_outer, got_mate = refs_in
        cur[own : own + rows] = earlier[earlier.shape[0] - 1]
        old[own : own + rows] = earlier[earlier.shape[0] - 2]
        cur[pl.ds(cur_outer, wide)] = got_outer[0:wide]
        cur[pl.ds(cur_mate, wide)] = got_mate[0:wide]
        old[own - RAD : own] = known[0]
        old[own + rows : own + rows + RAD] = known[1]
        low, high = own - narrow, own + rows + RAD
        more = narrow - RAD
        old[pl.ds(jnp.where(odd == 0, low, high), more)] = got_outer[wide:]
        old[pl.ds(jnp.where(odd == 0, high, low), more)] = got_mate[wide:]
    cells = [jnp.max(packs[block, NT : 2 * NT]).astype(jnp.int32) for block in range(3)]
    for step in range(steps):
        halo = RAD * (steps - 1 - step)
        advance(cur, old, model, zmat, ymat, own - halo, own + rows + halo, HALO - own)
        for block in (-1, 0, 1):
            if halo or block == 0:
                pack = packs.at[block + 1]
                add_source(old, pack, cells[block + 1], done + step, own, block, halo, rows)
        fields[step] = old[own : own + rows]
        if after_step:
            after_step(step, old[own : own + rows])
        cur, old = old, cur
    return cur, old, own


def gather_packs(pack_own, outer, mate, packs):
    odd = parity()
    packs[2 * odd] = outer[outer.shape[0] - 16 :]
    packs[1] = pack_own[...]
    packs[2 - 2 * odd] = mate[mate.shape[0] - 16 :]


def forward_kernel(index, *refs):
    take = 6 if index == 0 else 4
    refs_in, refs = refs[:take], refs[take:]
    zmat, ymat, model, pack, fields, known, send = refs[:7]
    if index == 0:
        packs, buf_a, buf_b = refs[7:]
        gather_packs(pack, refs_in[4], refs_in[5], packs)
    else:
        packs, (buf_a, buf_b) = pack, refs[7:]
    cur, old, own = forward_round(index, refs_in, zmat, ymat, model, packs, fields, buf_a, buf_b)
    rows = 16
    known[0] = old[own - RAD : own]
    known[1] = old[own + rows : own + rows + RAD]
    send[0:rows] = cur[own : own + rows]
    send[rows:] = old[own + RAD : own + rows - RAD]


def split_exactly(values):
    high = values.astype(BF)
    rest = values - high.astype(F32)
    middle = rest.astype(BF)
    return high, middle, (rest - middle.astype(F32)).astype(BF)


def in_send_order(observed, count):
    owners = observed.shape[0]
    per_owner = count // owners
    slot = lax.broadcasted_iota(jnp.int32, (owners, count), 1)
    owner = lax.broadcasted_iota(jnp.int32, (owners, count), 0)
    owned = jnp.where(slot // per_owner == owner, 1.0, 0.0).astype(BF)
    spread = jnp.zeros((NT * per_owner, count), F32)
    for part in split_exactly(observed):
        spread = spread + dot(part, owned, (((0,), (0,)), ((), ())))
    line = lax.broadcasted_iota(jnp.int32, (per_owner, count), 0)
    slot = lax.broadcasted_iota(jnp.int32, (per_owner, count), 1)
    hit = slot % per_owner == line
    out = []
    for step in range(NT):
        part = spread[step * per_owner : (step + 1) * per_owner]
        out.append(jnp.sum(jnp.where(hit, part, 0.0), axis=0, keepdims=True))
    return jnp.concatenate(out, axis=0)


def tables_kernel(count, *refs):
    (cells, observed, *fields), (rows_out, lanes_out, traces) = refs[:-3], refs[-3:]
    rows_table, lane_table = pick_tables(cells[0:1].astype(jnp.int32), rows_out.shape[1])
    rows_out[...] = rows_table
    lanes_out[...] = lane_table
    total = jnp.zeros((16, count), F32)
    step = 0
    for group in fields:
        for i in range(group.shape[0]):
            total = total + extract(group[i], step, rows_table, lane_table)
            step += 1
    traces[...] = total[:NT] - in_send_order(observed[...], count)


def last_kernel(index, *refs):
    take = 6 if index == 0 else 4
    refs_in, refs = refs[:take], refs[take:]
    zmat, ymat, model, packs, cells, rows_table, lane_table, traces = refs[:8]
    fields, adj, buf_a, buf_b = refs[8:]
    done = sum(ROUNDS[:index])
    total = [traces[...]]

    def pick(step, field):
        total[0] = total[0] + extract(field, done + step, rows_table[...], lane_table[...])[:NT]

    forward_round(index, refs_in, zmat, ymat, model, packs, fields, buf_a, buf_b, pick)
    adj[0:NT] = total[0]
    adj[NT:] = cells[...]


def source_planes(rows_table, lane_table, amounts, span_z):
    tiles = split(jnp.broadcast_to(amounts, (16, amounts.shape[1])))
    both = jnp.concatenate(
        [lane_table[z : z + 16] * tile for tile in tiles for z in range(0, span_z, 16)], axis=0
    )
    added = dot(rows_table, both, (((1,), (1,)), ((), ())))
    return added[:, :span_z] + added[:, span_z:]


def injection_lanes(cells, span_z):
    sub = lax.broadcasted_iota(jnp.int32, (span_z, cells.shape[1]), 0)
    return jnp.where(sub == cells % span_z, 1.0, 0.0).astype(BF)


def injection_table(cells, table_rows, span_z):
    sub = lax.broadcasted_iota(jnp.int32, (table_rows, cells.shape[1]), 0)
    return jnp.where(sub == cells // span_z, 1.0, 0.0).astype(BF)


def own_sources_kernel(adj, out):
    rows, span_y, span_z = out.shape[1:]
    cells = adj[NT : NT + 1].astype(jnp.int32)
    table = injection_table(cells, rows * span_y, span_z)
    lanes = injection_lanes(cells, span_z)
    for step in range(NT):
        added = source_planes(table, lanes, adj[step : step + 1], span_z)
        out[step] = added.reshape(rows, span_y, span_z)


def pair_kernel(adj, mate, out):
    odd = parity()
    out[odd] = adj[...]
    out[1 - odd] = mate[...]


def adjoint_kernel(field_groups, slabs, *refs):
    fields = []
    for ref in refs[:field_groups]:
        fields += [ref.at[i] for i in range(ref.shape[0])]
    refs = refs[field_groups:]
    zmat, ymat, model, sources, own_pair, even_pair, odd_pair = refs[:7]
    outs = refs[7 : 7 + slabs]
    buf_a, buf_b, image, rows_table, adjs, near = refs[7 + slabs :]
    odd = parity()
    odd_chip = lax.rem(lax.axis_index("shot") // 2, 2)
    near[2:4] = own_pair[...]
    near[pl.ds(4 - 4 * odd_chip, 2)] = even_pair[...]
    near[pl.ds(4 * odd_chip, 2)] = odd_pair[...]
    rows = 16
    own = HALO
    span_y, span_z = buf_a.shape[1:]
    table_rows = rows * span_y
    lanes = {}
    for block in (-2, -1, 1, 2):
        adjs[block + 2] = near[2 + odd + block]
        cells = adjs[block + 2, NT : NT + 1].astype(jnp.int32)
        rows_table[block + 2] = injection_table(cells, table_rows, span_z)
        lanes[block] = injection_lanes(cells, span_z)

    def inject(field, number):
        halo = RAD * (NT - number)
        step = NT - number
        for block in range(-2, 3):
            begin = own + block * rows
            first = max(begin, own - halo)
            last = min(begin + rows, own + rows + halo)
            if first >= last:
                continue
            if block:
                table = rows_table[block + 2, (first - begin) * span_y : (last - begin) * span_y, :]
                added = source_planes(table, lanes[block], adjs[block + 2, step : step + 1], span_z)
                added = added.reshape(last - first, span_y, span_z)
            else:
                added = sources[step]
            if number == 1:
                field[first:last] = added
            else:
                field[first:last] = field[first:last] + added

    cur, old = buf_a, buf_b
    inject(cur, 1)
    old[...] = jnp.zeros(old.shape, F32)
    image[...] = cur[own : own + rows] * fields[NT - 1][...]
    for number in range(2, NT + 1):
        halo = RAD * (NT - number)
        advance(cur, old, model, zmat, ymat, own - halo, own + rows + halo, 0)
        inject(old, number)
        image[...] = image[...] + old[own : own + rows] * fields[NT - number][...]
        cur, old = old, cur
    mine = lax.axis_index("shot") // PIECES
    thick = rows // slabs
    for i in range(slabs):
        outs[i][...] = image[pl.ds((mine ^ i) * thick, thick)]


def call(kernel, outs, ins, specs=None, scratch=(), cost=(1e6, 1e6), name=None):
    return pl.pallas_call(
        kernel,
        out_shape=outs,
        in_specs=specs or [VMEM] * len(ins),
        out_specs=jax.tree.map(lambda _: VMEM, outs),
        scratch_shapes=list(scratch),
        compiler_params=pltpu.CompilerParams(vmem_limit_bytes=48 * 1024 * 1024),
        cost_estimate=pl.CostEstimate(flops=int(cost[0]), bytes_accessed=int(cost[1]), transcendentals=0),
        name=name,
    )(*ins)


def swapped(value, partner):
    count = lax.axis_size("shot")
    return lax.ppermute(value, "shot", [(d, partner(d) % count) for d in range(count)])


def with_mate(value):
    return swapped(value, lambda d: d ^ 1)


def with_outer(value):
    return swapped(value, lambda d: d + 1 if d % 2 else d - 1)


def with_even_pair(value):
    return swapped(value, lambda d: d ^ 2)


def with_odd_pair(value):
    return swapped(value, lambda d: d + 2 if d % 4 >= 2 else d - 2)


def per_device(
    courant_sq, wave_now, wave_before, wavelet, source_cell, receiver_cell, send_order, observed
):
    devices = lax.axis_size("shot")
    rows, span_y, span_z = wave_now.shape
    count = receiver_cell.shape[0]
    table_rows = rows * span_y
    plane = (span_y, span_z)

    narrow = RAD * (ROUNDS[0] - 1)
    now_outer, now_mate = with_outer(wave_now), with_mate(wave_now)
    message = jax.ShapeDtypeStruct((narrow * span_y + 16, span_z), F32)
    to_outer, to_mate, pack, before = call(
        message_kernel,
        (message, message, jax.ShapeDtypeStruct((16, span_z), F32), jax.ShapeDtypeStruct(wave_before.shape, F32)),
        (wave_before, wavelet, source_cell),
        specs=[VMEM, SMEM, SMEM],
        name="message",
    )
    before_outer, before_mate = with_outer(to_outer), with_mate(to_mate)

    model, cells, observed, now, ymat, zmat = call(
        prepare_kernel,
        (
            jax.ShapeDtypeStruct((rows + 2 * HALO,) + plane, F32),
            jax.ShapeDtypeStruct((8, count), F32),
            jax.ShapeDtypeStruct(observed.shape, F32),
            jax.ShapeDtypeStruct(wave_now.shape, F32),
            jax.ShapeDtypeStruct((GROUP * span_y, GROUP * span_y), BF),
            jax.ShapeDtypeStruct((2 * span_z, 2 * span_z), BF),
        ),
        (courant_sq, receiver_cell.reshape(1, count), send_order.reshape(1, count), observed, pack, wave_now),
        name="prepare",
    )
    recorded = lax.all_to_all(observed, "shot", split_axis=0, concat_axis=0, tiled=True)

    common = (zmat, ymat, model)
    field_list = []
    ins = (now, before, now_outer, now_mate, before_outer, before_mate)
    for index in range(len(ROUNDS) - 1):
        window = rows + 2 * RAD * ROUNDS[index]
        sent = 2 * rows - 2 * RAD
        packs = (jax.ShapeDtypeStruct((3, 16, span_z), F32),) if index == 0 else ()
        fields, known, send, *made = call(
            functools.partial(forward_kernel, index),
            (
                jax.ShapeDtypeStruct((ROUNDS[index], rows) + plane, F32),
                jax.ShapeDtypeStruct((2, RAD) + plane, F32),
                jax.ShapeDtypeStruct((sent,) + plane, F32),
            )
            + packs,
            ins + common + (pack,),
            scratch=[pltpu.VMEM((window,) + plane, F32)] * 2,
            name="forward",
        )
        field_list.append(fields)
        pack = made[0] if made else pack
        ins = (fields, known, with_outer(send), with_mate(send))

    rows_table, lane_table, traces = call(
        functools.partial(tables_kernel, count),
        (
            jax.ShapeDtypeStruct((count, table_rows), BF),
            jax.ShapeDtypeStruct((count, 256), F32),
            jax.ShapeDtypeStruct((NT, count), F32),
        ),
        (cells, recorded, *field_list),
        name="traces",
    )
    index = len(ROUNDS) - 1
    window = rows + 2 * RAD * ROUNDS[index]
    fields, adj = call(
        functools.partial(last_kernel, index),
        (
            jax.ShapeDtypeStruct((ROUNDS[index], rows) + plane, F32),
            jax.ShapeDtypeStruct((2 * NT, count), F32),
        ),
        ins + common + (pack, cells, rows_table, lane_table, traces),
        scratch=[pltpu.VMEM((window,) + plane, F32)] * 2,
        name="forward_last",
    )
    field_list.append(fields)

    sources = call(
        own_sources_kernel, jax.ShapeDtypeStruct((NT, rows) + plane, F32), (adj,), name="own_sources"
    )
    pair = call(
        pair_kernel, jax.ShapeDtypeStruct((2, 2 * NT, count), F32), (adj, with_mate(adj)), name="pair"
    )
    adjs = [sources, pair, with_even_pair(pair), with_odd_pair(pair)]
    slabs = devices // PIECES
    thick = rows // slabs
    parts = call(
        functools.partial(adjoint_kernel, len(field_list), slabs),
        tuple(jax.ShapeDtypeStruct((thick,) + plane, F32) for _ in range(slabs)),
        (*field_list, zmat, ymat, model, *adjs),
        scratch=[pltpu.VMEM((rows + 2 * HALO,) + plane, F32)] * 2
        + [pltpu.VMEM((rows,) + plane, F32), pltpu.VMEM((5, table_rows, count), BF)]
        + [pltpu.VMEM((5, 2 * NT, count), F32), pltpu.VMEM((6, 2 * NT, count), F32)],
        name="adjoint",
    )
    total = parts[0]
    for i in range(1, slabs):
        total = total + swapped(parts[i], lambda d: d ^ (i * PIECES))
    return total


def solution(mesh):
    return jax.shard_map(
        per_device,
        mesh=mesh,
        in_specs=(
            P("groups", None, None),
            P(("groups", "shot"), None, None),
            P(("groups", "shot"), None, None),
            P(("groups", "shot"), None),
            P(("groups", "shot")),
            P(("groups", "shot")),
            P(("groups", "shot")),
            P(("groups", "shot"), None),
        ),
        out_specs=P(("groups", "shot"), None, None),
        check_vma=False,
    )
```

```python
import functools

import jax
import jax.numpy as jnp
from jax import lax
from jax.experimental import pallas as pl
from jax.experimental.pallas import tpu as pltpu
from jax.sharding import PartitionSpec as P

NT = 8
PIECES = 4
RAD = 4
ROUNDS = (4, 4)
SCALE = 5040.0
CENTER_Y = -43008.0
CENTER_Z = -42.0
WEIGHTS = (8064.0, -1008.0, 128.0, -9.0)
GROUP = 8
HALO = RAD * (NT - 1)
BF = jnp.bfloat16
F32 = jnp.float32

VMEM = pl.BlockSpec(memory_space=pltpu.VMEM)
SMEM = pl.BlockSpec(memory_space=pltpu.SMEM)


def band(distance, center):
    out = jnp.where(distance == 0, center, 0.0)
    for k, weight in enumerate(WEIGHTS, 1):
        out = jnp.where(jnp.abs(distance) == k, weight, out)
    return out


def build_bands(span_y, span_z, rows_out, fixed_out):
    size = GROUP * span_y
    row = lax.broadcasted_iota(jnp.int32, (size, size), 0)
    col = lax.broadcasted_iota(jnp.int32, (size, size), 1)
    tile = 8 * GROUP
    y_row = row // tile * 8 + row % 8
    y_col = col // tile * 8 + col % 8
    same = (row // 8) % GROUP == (col // 8) % GROUP
    rows_out[...] = jnp.where(same, band(y_row - y_col, CENTER_Y), 0.0).astype(BF)
    z = lax.broadcasted_iota(jnp.int32, (2 * span_z, 2 * span_z), 0) % span_z
    to = lax.broadcasted_iota(jnp.int32, (2 * span_z, 2 * span_z), 1)
    fixed_out[...] = jnp.where(to < span_z, band(z - to, CENTER_Z), 0.0).astype(BF)


def split(values):
    high = values.astype(BF)
    low = (values - high.astype(F32)).astype(BF)
    return high, low


def dot(a, b, dims=(((1,), (0,)), ((), ()))):
    return lax.dot_general(a, b, dims, preferred_element_type=F32)


def advance(cur, old, model, zmat, ymat, first, last, model_shift, extra, keep):
    span_y, span_z = cur.shape[1:]
    zmat, ymat = zmat[...], ymat[...]
    for base in range(first, last, GROUP):
        columns = [slice(j, j + 8) for j in range(0, span_y, 8)]
        order = [(i, column) for column in columns for i in range(GROUP)]
        group = jnp.concatenate([cur[base + i, column] for i, column in order], axis=0)
        pair = jnp.concatenate(split(group), axis=1)
        left = jnp.concatenate([ymat, pair], axis=1)
        right = jnp.concatenate([pair, zmat], axis=0)
        part = dot(left, right)
        for j, column in enumerate(columns):
            tiles = [cur[base - RAD + q, column] for q in range(GROUP + 2 * RAD)]
            for i in range(GROUP):
                x = base + i
                at = (j * GROUP + i) * 8
                rows = slice(at, at + 8)
                here = tiles[i + RAD]
                total = part[rows, :span_z] + part[rows, span_z:]
                for k, weight in enumerate(WEIGHTS, 1):
                    total = total + weight * (tiles[i + RAD + k] + tiles[i + RAD - k])
                tile = (here + here - old[x, column]) + model[x + model_shift, column] * total + extra(x, column)
                old[x, column] = tile
                keep(x, column, tile)


def mark_source(mask, cell, block, rows):
    span_y, span_z = mask.shape[1:]
    plane = (1 + block) * rows + cell // (span_y * span_z)
    y = (cell // span_z) % span_y
    tile = pl.ds(pl.multiple_of((y // 8) * 8, 8), 8)
    sub = lax.broadcasted_iota(jnp.int32, (8, span_z), 0)
    lane = lax.broadcasted_iota(jnp.int32, (8, span_z), 1)
    mask[plane, tile, :] = jnp.where((sub == y % 8) & (lane == cell % span_z), 1.0, 0.0)


def parity():
    return lax.rem(lax.axis_index("shot"), 2)


def message_kernel(before, wavelet, source, outer_out, mate_out, pack_out, before_out):
    rows, span_y, span_z = before.shape
    which = lax.broadcasted_iota(jnp.int32, (16, span_z), 0)
    pack = jnp.where(which >= NT, source[0].astype(F32), 0.0)
    for step in range(NT):
        pack = jnp.where(which == step, wavelet[0, step], pack)
    pack_out[...] = pack
    before_out[...] = before[...]
    narrow = RAD * (ROUNDS[0] - 1)
    size = narrow * span_y
    odd = parity()
    outer_out[:size] = before[pl.ds(odd * (rows - narrow), narrow)].reshape(size, span_z)
    mate_out[:size] = before[pl.ds((1 - odd) * (rows - narrow), narrow)].reshape(size, span_z)
    outer_out[size:] = pack
    mate_out[size:] = pack


def prepare_kernel(
    courant, cells, order, observed, pack, now, model_out, cells_out, observed_out, now_out, ymat_out, zmat_out
):
    rows, span_y, span_z = now.shape
    now_out[...] = now[...]
    build_bands(span_y, span_z, ymat_out, zmat_out)
    piece = lax.rem(lax.axis_index("shot"), PIECES)
    period = courant.shape[0]
    window = model_out.shape[0]
    for chunk in range(0, window, RAD):
        source = lax.rem(piece * rows - HALO + chunk + period, period)
        model_out[chunk : chunk + RAD] = courant[pl.ds(source, RAD)] * (1.0 / SCALE)
    count = cells.shape[1]
    wanted = order[...]
    cell = cells[...]
    which = lax.broadcasted_iota(jnp.int32, (16, count), 0)
    digits = jnp.where(which == 0, cell // 256, jnp.where(which == 1, cell % 256, 0)).astype(F32).astype(BF)
    for j in range(0, count, 256):
        index = lax.broadcasted_iota(jnp.int32, (count, 256), 0)
        chosen = jnp.where(index == wanted[:, j : j + 256], 1.0, 0.0).astype(BF)
        found = dot(digits, chosen)
        ordered = found[0:1] * 256.0 + found[1:2]
        cells_out[:, j : j + 256] = jnp.broadcast_to(ordered, (8, 256))
    observed_out[...] = observed[...] + 0.0 * pack[0:1, :]


def pick_tables(cells, table_rows):
    count = cells.shape[1]
    column = jnp.transpose(jnp.broadcast_to(cells.astype(F32), (128, count)))
    column = column.astype(jnp.int32)
    row_of = jnp.concatenate([column // 128] * (table_rows // 128), axis=1)
    lane_of = jnp.concatenate([column % 128] * 2, axis=1)
    lanes = lax.broadcasted_iota(jnp.int32, (count, table_rows), 1)
    rows_table = jnp.where(row_of == lanes, 1.0, 0.0).astype(BF)
    lanes2 = lax.broadcasted_iota(jnp.int32, (count, 256), 1) % 128
    lane_table = jnp.where(lane_of == lanes2, 1.0, 0.0)
    return rows_table, lane_table


def extract(field, step, rows_table, lane_table):
    rows, span_y, span_z = field.shape
    pair = jnp.concatenate(split(field.reshape(rows * span_y, span_z)), axis=1)
    which = lax.broadcasted_iota(jnp.int32, (16, 2 * span_z), 0)
    ones = jnp.where(which == step, 1.0, 0.0).astype(BF)
    out = []
    for j in range(0, rows_table.shape[0], 256):
        found = dot(rows_table[j : j + 256], pair)
        kept = (found * lane_table[j : j + 256]).astype(BF)
        out.append(dot(ones, kept, (((1,), (1,)), ((), ()))))
    return jnp.concatenate(out, axis=1)


def forward_round(
    index, refs_in, zmat, ymat, model, packs, fields, buf_a, buf_b, mask, after_step=None
):
    steps = ROUNDS[index]
    done = sum(ROUNDS[:index])
    rows = 16
    own = RAD * steps
    cur, old = buf_a, buf_b
    wide, narrow = RAD * steps, RAD * (steps - 1)
    odd = parity()
    shape = cur.shape[1:]
    low, high = own - wide, own + rows
    cur_outer = jnp.where(odd == 0, low, high)
    cur_mate = jnp.where(odd == 0, high, low)
    if index == 0:
        now, before, now_outer, now_mate, before_outer, before_mate = refs_in
        cur[own : own + rows] = now[...]
        old[own : own + rows] = before[...]
        cur[pl.ds(cur_outer, wide)] = now_outer[...]
        cur[pl.ds(cur_mate, wide)] = now_mate[...]
        size = narrow * shape[0]
        low = own - narrow
        old[pl.ds(jnp.where(odd == 0, low, high), narrow)] = before_outer[:size].reshape((narrow,) + shape)
        old[pl.ds(jnp.where(odd == 0, high, low), narrow)] = before_mate[:size].reshape((narrow,) + shape)
    else:
        earlier, known, got_outer, got_mate = refs_in
        cur[own : own + rows] = earlier[earlier.shape[0] - 1]
        old[own : own + rows] = earlier[earlier.shape[0] - 2]
        cur[pl.ds(cur_outer, wide)] = got_outer[0:wide]
        cur[pl.ds(cur_mate, wide)] = got_mate[0:wide]
        old[own - RAD : own] = known[0]
        old[own + rows : own + rows + RAD] = known[1]
        low, high = own - narrow, own + rows + RAD
        more = narrow - RAD
        old[pl.ds(jnp.where(odd == 0, low, high), more)] = got_outer[wide:]
        old[pl.ds(jnp.where(odd == 0, high, low), more)] = got_mate[wide:]
    mask[...] = jnp.zeros(mask.shape, F32)
    for block in (-1, 0, 1):
        mark_source(mask, jnp.max(packs[block + 1, NT : 2 * NT]).astype(jnp.int32), block, rows)
    for step in range(steps):
        halo = RAD * (steps - 1 - step)
        amounts = [jnp.broadcast_to(packs[i, done + step : done + step + 1], (8, shape[1])) for i in range(3)]

        def extra(x, column):
            place = x - own + rows
            return mask[place, column] * amounts[place // rows]

        def keep(x, column, tile):
            if own <= x < own + rows:
                fields[step, x - own, column] = tile

        advance(cur, old, model, zmat, ymat, own - halo, own + rows + halo, HALO - own, extra, keep)
        if after_step:
            after_step(step, old[own : own + rows])
        cur, old = old, cur
    return cur, old, own


def gather_packs(pack_own, outer, mate, packs):
    odd = parity()
    packs[2 * odd] = outer[outer.shape[0] - 16 :]
    packs[1] = pack_own[...]
    packs[2 - 2 * odd] = mate[mate.shape[0] - 16 :]


def forward_kernel(index, *refs):
    take = 6 if index == 0 else 4
    refs_in, refs = refs[:take], refs[take:]
    zmat, ymat, model, pack, fields, known, send = refs[:7]
    if index == 0:
        packs, buf_a, buf_b, mask = refs[7:]
        gather_packs(pack, refs_in[4], refs_in[5], packs)
    else:
        packs, (buf_a, buf_b, mask) = pack, refs[7:]
    cur, old, own = forward_round(index, refs_in, zmat, ymat, model, packs, fields, buf_a, buf_b, mask)
    rows = 16
    known[0] = old[own - RAD : own]
    known[1] = old[own + rows : own + rows + RAD]
    send[0:rows] = cur[own : own + rows]
    send[rows:] = old[own + RAD : own + rows - RAD]


def split_exactly(values):
    high = values.astype(BF)
    rest = values - high.astype(F32)
    middle = rest.astype(BF)
    return high, middle, (rest - middle.astype(F32)).astype(BF)


def in_send_order(observed, count):
    owners = observed.shape[0]
    per_owner = count // owners
    slot = lax.broadcasted_iota(jnp.int32, (owners, count), 1)
    owner = lax.broadcasted_iota(jnp.int32, (owners, count), 0)
    owned = jnp.where(slot // per_owner == owner, 1.0, 0.0).astype(BF)
    spread = jnp.zeros((NT * per_owner, count), F32)
    for part in split_exactly(observed):
        spread = spread + dot(part, owned, (((0,), (0,)), ((), ())))
    line = lax.broadcasted_iota(jnp.int32, (per_owner, count), 0)
    slot = lax.broadcasted_iota(jnp.int32, (per_owner, count), 1)
    hit = slot % per_owner == line
    out = []
    for step in range(NT):
        part = spread[step * per_owner : (step + 1) * per_owner]
        out.append(jnp.sum(jnp.where(hit, part, 0.0), axis=0, keepdims=True))
    return jnp.concatenate(out, axis=0)


def tables_kernel(count, *refs):
    (cells, observed, *fields), (rows_out, lanes_out, traces) = refs[:-3], refs[-3:]
    rows_table, lane_table = pick_tables(cells[0:1].astype(jnp.int32), rows_out.shape[1])
    rows_out[...] = rows_table
    lanes_out[...] = lane_table
    total = jnp.zeros((16, count), F32)
    step = 0
    for group in fields:
        for i in range(group.shape[0]):
            total = total + extract(group[i], step, rows_table, lane_table)
            step += 1
    traces[...] = total[:NT] - in_send_order(observed[...], count)


def last_kernel(index, *refs):
    take = 6 if index == 0 else 4
    refs_in, refs = refs[:take], refs[take:]
    zmat, ymat, model, packs, cells, rows_table, lane_table, traces = refs[:8]
    fields, adj, buf_a, buf_b, mask = refs[8:]
    done = sum(ROUNDS[:index])
    total = [traces[...]]

    def pick(step, field):
        total[0] = total[0] + extract(field, done + step, rows_table[...], lane_table[...])[:NT]

    forward_round(index, refs_in, zmat, ymat, model, packs, fields, buf_a, buf_b, mask, pick)
    adj[0:NT] = total[0]
    adj[NT:] = cells[...]


def source_planes(rows_table, lane_table, amounts, span_z):
    tiles = split(jnp.broadcast_to(amounts, (16, amounts.shape[1])))
    both = jnp.concatenate(
        [lane_table[z : z + 16] * tile for tile in tiles for z in range(0, span_z, 16)], axis=0
    )
    added = dot(rows_table, both, (((1,), (1,)), ((), ())))
    return added[:, :span_z] + added[:, span_z:]


def injection_lanes(cells, span_z):
    sub = lax.broadcasted_iota(jnp.int32, (span_z, cells.shape[1]), 0)
    return jnp.where(sub == cells % span_z, 1.0, 0.0).astype(BF)


def injection_table(cells, table_rows, span_z):
    sub = lax.broadcasted_iota(jnp.int32, (table_rows, cells.shape[1]), 0)
    return jnp.where(sub == cells // span_z, 1.0, 0.0).astype(BF)


def own_sources_kernel(adj, out):
    rows, span_y, span_z = out.shape[1:]
    cells = adj[NT : NT + 1].astype(jnp.int32)
    table = injection_table(cells, rows * span_y, span_z)
    lanes = injection_lanes(cells, span_z)
    for step in range(NT):
        added = source_planes(table, lanes, adj[step : step + 1], span_z)
        out[step] = added.reshape(rows, span_y, span_z)


def pair_kernel(adj, mate, out):
    odd = parity()
    out[odd] = adj[...]
    out[1 - odd] = mate[...]


def adjoint_kernel(field_groups, slabs, *refs):
    fields = []
    for ref in refs[:field_groups]:
        fields += [ref.at[i] for i in range(ref.shape[0])]
    refs = refs[field_groups:]
    zmat, ymat, model, sources, own_pair, even_pair, odd_pair = refs[:7]
    outs = refs[7 : 7 + slabs]
    buf_a, buf_b, planes, image, rows_table, adjs, near = refs[7 + slabs :]
    odd = parity()
    odd_chip = lax.rem(lax.axis_index("shot") // 2, 2)
    near[2:4] = own_pair[...]
    near[pl.ds(4 - 4 * odd_chip, 2)] = even_pair[...]
    near[pl.ds(4 * odd_chip, 2)] = odd_pair[...]
    rows = 16
    own = HALO
    span_y, span_z = buf_a.shape[1:]
    table_rows = rows * span_y
    lanes = {}
    for block in (-2, -1, 1, 2):
        adjs[block + 2] = near[2 + odd + block]
        cells = adjs[block + 2, NT : NT + 1].astype(jnp.int32)
        rows_table[block + 2] = injection_table(cells, table_rows, span_z)
        lanes[block] = injection_lanes(cells, span_z)

    def place_sources(number, out):
        halo = RAD * (NT - number)
        step = NT - number
        for block in (-2, -1, 1, 2):
            begin = own + block * rows
            first = max(begin, own - halo)
            last = min(begin + rows, own + rows + halo)
            if first >= last:
                continue
            table = rows_table[block + 2, (first - begin) * span_y : (last - begin) * span_y, :]
            added = source_planes(table, lanes[block], adjs[block + 2, step : step + 1], span_z)
            out[first:last] = added.reshape(last - first, span_y, span_z)

    cur, old = buf_a, buf_b
    place_sources(1, cur)
    cur[own : own + rows] = sources[NT - 1]
    old[...] = jnp.zeros(old.shape, F32)
    image[...] = sources[NT - 1] * fields[NT - 1][...]
    for number in range(2, NT + 1):
        halo = RAD * (NT - number)
        step = NT - number
        place_sources(number, planes)

        def extra(x, column):
            return sources[step, x - own, column] if own <= x < own + rows else planes[x, column]

        def keep(x, column, tile):
            if own <= x < own + rows:
                image[x - own, column] = image[x - own, column] + tile * fields[step][x - own, column]

        advance(cur, old, model, zmat, ymat, own - halo, own + rows + halo, 0, extra, keep)
        cur, old = old, cur
    mine = lax.axis_index("shot") // PIECES
    thick = rows // slabs
    for i in range(slabs):
        outs[i][...] = image[pl.ds((mine ^ i) * thick, thick)]


def call(kernel, outs, ins, specs=None, scratch=(), cost=(1e6, 1e6), name=None):
    return pl.pallas_call(
        kernel,
        out_shape=outs,
        in_specs=specs or [VMEM] * len(ins),
        out_specs=jax.tree.map(lambda _: VMEM, outs),
        scratch_shapes=list(scratch),
        compiler_params=pltpu.CompilerParams(vmem_limit_bytes=48 * 1024 * 1024),
        cost_estimate=pl.CostEstimate(flops=int(cost[0]), bytes_accessed=int(cost[1]), transcendentals=0),
        name=name,
    )(*ins)


def swapped(value, partner):
    count = lax.axis_size("shot")
    return lax.ppermute(value, "shot", [(d, partner(d) % count) for d in range(count)])


def with_mate(value):
    return swapped(value, lambda d: d ^ 1)


def with_outer(value):
    return swapped(value, lambda d: d + 1 if d % 2 else d - 1)


def with_even_pair(value):
    return swapped(value, lambda d: d ^ 2)


def with_odd_pair(value):
    return swapped(value, lambda d: d + 2 if d % 4 >= 2 else d - 2)


def per_device(
    courant_sq, wave_now, wave_before, wavelet, source_cell, receiver_cell, send_order, observed
):
    devices = lax.axis_size("shot")
    rows, span_y, span_z = wave_now.shape
    count = receiver_cell.shape[0]
    table_rows = rows * span_y
    plane = (span_y, span_z)

    narrow = RAD * (ROUNDS[0] - 1)
    now_outer, now_mate = with_outer(wave_now), with_mate(wave_now)
    message = jax.ShapeDtypeStruct((narrow * span_y + 16, span_z), F32)
    to_outer, to_mate, pack, before = call(
        message_kernel,
        (message, message, jax.ShapeDtypeStruct((16, span_z), F32), jax.ShapeDtypeStruct(wave_before.shape, F32)),
        (wave_before, wavelet, source_cell),
        specs=[VMEM, SMEM, SMEM],
        name="message",
    )
    before_outer, before_mate = with_outer(to_outer), with_mate(to_mate)

    model, cells, observed, now, ymat, zmat = call(
        prepare_kernel,
        (
            jax.ShapeDtypeStruct((rows + 2 * HALO,) + plane, F32),
            jax.ShapeDtypeStruct((8, count), F32),
            jax.ShapeDtypeStruct(observed.shape, F32),
            jax.ShapeDtypeStruct(wave_now.shape, F32),
            jax.ShapeDtypeStruct((GROUP * span_y, GROUP * span_y), BF),
            jax.ShapeDtypeStruct((2 * span_z, 2 * span_z), BF),
        ),
        (courant_sq, receiver_cell.reshape(1, count), send_order.reshape(1, count), observed, pack, wave_now),
        name="prepare",
    )
    recorded = lax.all_to_all(observed, "shot", split_axis=0, concat_axis=0, tiled=True)

    common = (zmat, ymat, model)
    field_list = []
    ins = (now, before, now_outer, now_mate, before_outer, before_mate)
    for index in range(len(ROUNDS) - 1):
        window = rows + 2 * RAD * ROUNDS[index]
        sent = 2 * rows - 2 * RAD
        packs = (jax.ShapeDtypeStruct((3, 16, span_z), F32),) if index == 0 else ()
        fields, known, send, *made = call(
            functools.partial(forward_kernel, index),
            (
                jax.ShapeDtypeStruct((ROUNDS[index], rows) + plane, F32),
                jax.ShapeDtypeStruct((2, RAD) + plane, F32),
                jax.ShapeDtypeStruct((sent,) + plane, F32),
            )
            + packs,
            ins + common + (pack,),
            scratch=[pltpu.VMEM((window,) + plane, F32)] * 2 + [pltpu.VMEM((3 * rows,) + plane, F32)],
            name="forward",
        )
        field_list.append(fields)
        pack = made[0] if made else pack
        ins = (fields, known, with_outer(send), with_mate(send))

    rows_table, lane_table, traces = call(
        functools.partial(tables_kernel, count),
        (
            jax.ShapeDtypeStruct((count, table_rows), BF),
            jax.ShapeDtypeStruct((count, 256), F32),
            jax.ShapeDtypeStruct((NT, count), F32),
        ),
        (cells, recorded, *field_list),
        name="traces",
    )
    index = len(ROUNDS) - 1
    window = rows + 2 * RAD * ROUNDS[index]
    fields, adj = call(
        functools.partial(last_kernel, index),
        (
            jax.ShapeDtypeStruct((ROUNDS[index], rows) + plane, F32),
            jax.ShapeDtypeStruct((2 * NT, count), F32),
        ),
        ins + common + (pack, cells, rows_table, lane_table, traces),
        scratch=[pltpu.VMEM((window,) + plane, F32)] * 2 + [pltpu.VMEM((3 * rows,) + plane, F32)],
        name="forward_last",
    )
    field_list.append(fields)

    sources = call(
        own_sources_kernel, jax.ShapeDtypeStruct((NT, rows) + plane, F32), (adj,), name="own_sources"
    )
    pair = call(
        pair_kernel, jax.ShapeDtypeStruct((2, 2 * NT, count), F32), (adj, with_mate(adj)), name="pair"
    )
    adjs = [sources, pair, with_even_pair(pair), with_odd_pair(pair)]
    slabs = devices // PIECES
    thick = rows // slabs
    parts = call(
        functools.partial(adjoint_kernel, len(field_list), slabs),
        tuple(jax.ShapeDtypeStruct((thick,) + plane, F32) for _ in range(slabs)),
        (*field_list, zmat, ymat, model, *adjs),
        scratch=[pltpu.VMEM((rows + 2 * HALO,) + plane, F32)] * 3
        + [pltpu.VMEM((rows,) + plane, F32), pltpu.VMEM((5, table_rows, count), BF)]
        + [pltpu.VMEM((5, 2 * NT, count), F32), pltpu.VMEM((6, 2 * NT, count), F32)],
        name="adjoint",
    )
    total = parts[0]
    for i in range(1, slabs):
        total = total + swapped(parts[i], lambda d: d ^ (i * PIECES))
    return total


def solution(mesh):
    return jax.shard_map(
        per_device,
        mesh=mesh,
        in_specs=(
            P("groups", None, None),
            P(("groups", "shot"), None, None),
            P(("groups", "shot"), None, None),
            P(("groups", "shot"), None),
            P(("groups", "shot")),
            P(("groups", "shot")),
            P(("groups", "shot")),
            P(("groups", "shot"), None),
        ),
        out_specs=P(("groups", "shot"), None, None),
        check_vma=False,
    )
```

```python
import functools

import jax
import jax.numpy as jnp
from jax import lax
from jax.experimental import pallas as pl
from jax.experimental.pallas import tpu as pltpu
from jax.sharding import PartitionSpec as P

NT = 8
PIECES = 4
RAD = 4
ROUNDS = (4, 4)
SCALE = 5040.0
CENTER_Y = -43008.0
CENTER_Z = -42.0
WEIGHTS = (8064.0, -1008.0, 128.0, -9.0)
GROUP = 8
HALO = RAD * (NT - 1)
BF = jnp.bfloat16
F32 = jnp.float32

VMEM = pl.BlockSpec(memory_space=pltpu.VMEM)
SMEM = pl.BlockSpec(memory_space=pltpu.SMEM)


def band(distance, center):
    out = jnp.where(distance == 0, center, 0.0)
    for k, weight in enumerate(WEIGHTS, 1):
        out = jnp.where(jnp.abs(distance) == k, weight, out)
    return out


def build_bands(span_y, span_z, rows_out, fixed_out):
    size = GROUP * span_y
    row = lax.broadcasted_iota(jnp.int32, (size, size), 0)
    col = lax.broadcasted_iota(jnp.int32, (size, size), 1)
    tile = 8 * GROUP
    y_row = row // tile * 8 + row % 8
    y_col = col // tile * 8 + col % 8
    x_far = (row // 8) % GROUP - (col // 8) % GROUP
    y_far = y_row - y_col
    across = jnp.where(y_far == 0, band(x_far, 0.0), 0.0)
    rows_out[...] = jnp.where(x_far == 0, band(y_far, CENTER_Y), across).astype(BF)
    z = lax.broadcasted_iota(jnp.int32, (2 * span_z, 2 * span_z), 0) % span_z
    to = lax.broadcasted_iota(jnp.int32, (2 * span_z, 2 * span_z), 1)
    fixed_out[...] = jnp.where(to < span_z, band(z - to, CENTER_Z), 0.0).astype(BF)


def split(values):
    high = values.astype(BF)
    low = (values - high.astype(F32)).astype(BF)
    return high, low


def dot(a, b, dims=(((1,), (0,)), ((), ()))):
    return lax.dot_general(a, b, dims, preferred_element_type=F32)


def advance(cur, old, model, zmat, ymat, first, last, model_shift, extra, keep):
    span_y, span_z = cur.shape[1:]
    zmat, ymat = zmat[...], ymat[...]
    for base in range(first, last, GROUP):
        columns = [slice(j, j + 8) for j in range(0, span_y, 8)]
        order = [(i, column) for column in columns for i in range(GROUP)]
        group = jnp.concatenate([cur[base + i, column] for i, column in order], axis=0)
        pair = jnp.concatenate(split(group), axis=1)
        left = jnp.concatenate([ymat, pair], axis=1)
        right = jnp.concatenate([pair, zmat], axis=0)
        part = dot(left, right)
        for j, column in enumerate(columns):
            tiles = [cur[base - RAD + q, column] for q in range(GROUP + 2 * RAD)]
            for i in range(GROUP):
                x = base + i
                at = (j * GROUP + i) * 8
                rows = slice(at, at + 8)
                here = tiles[i + RAD]
                total = part[rows, :span_z] + part[rows, span_z:]
                for k, weight in enumerate(WEIGHTS, 1):
                    if i + k >= GROUP:
                        total = total + weight * tiles[i + RAD + k]
                    if i < k:
                        total = total + weight * tiles[i + RAD - k]
                tile = (here + here - old[x, column]) + model[x + model_shift, column] * total + extra(x, column)
                old[x, column] = tile
                keep(x, column, tile)


def mark_source(mask, cell, block, rows):
    span_y, span_z = mask.shape[1:]
    plane = (1 + block) * rows + cell // (span_y * span_z)
    y = (cell // span_z) % span_y
    tile = pl.ds(pl.multiple_of((y // 8) * 8, 8), 8)
    sub = lax.broadcasted_iota(jnp.int32, (8, span_z), 0)
    lane = lax.broadcasted_iota(jnp.int32, (8, span_z), 1)
    mask[plane, tile, :] = jnp.where((sub == y % 8) & (lane == cell % span_z), 1.0, 0.0)


def parity():
    return lax.rem(lax.axis_index("shot"), 2)


def message_kernel(before, wavelet, source, outer_out, mate_out, pack_out, before_out):
    rows, span_y, span_z = before.shape
    which = lax.broadcasted_iota(jnp.int32, (16, span_z), 0)
    pack = jnp.where(which >= NT, source[0].astype(F32), 0.0)
    for step in range(NT):
        pack = jnp.where(which == step, wavelet[0, step], pack)
    pack_out[...] = pack
    before_out[...] = before[...]
    narrow = RAD * (ROUNDS[0] - 1)
    size = narrow * span_y
    odd = parity()
    outer_out[:size] = before[pl.ds(odd * (rows - narrow), narrow)].reshape(size, span_z)
    mate_out[:size] = before[pl.ds((1 - odd) * (rows - narrow), narrow)].reshape(size, span_z)
    outer_out[size:] = pack
    mate_out[size:] = pack


def prepare_kernel(
    courant, cells, order, observed, pack, now, model_out, cells_out, observed_out, now_out, ymat_out, zmat_out
):
    rows, span_y, span_z = now.shape
    now_out[...] = now[...]
    build_bands(span_y, span_z, ymat_out, zmat_out)
    piece = lax.rem(lax.axis_index("shot"), PIECES)
    period = courant.shape[0]
    window = model_out.shape[0]
    for chunk in range(0, window, RAD):
        source = lax.rem(piece * rows - HALO + chunk + period, period)
        model_out[chunk : chunk + RAD] = courant[pl.ds(source, RAD)] * (1.0 / SCALE)
    count = cells.shape[1]
    wanted = order[...]
    cell = cells[...]
    which = lax.broadcasted_iota(jnp.int32, (16, count), 0)
    digits = jnp.where(which == 0, cell // 256, jnp.where(which == 1, cell % 256, 0)).astype(F32).astype(BF)
    for j in range(0, count, 256):
        index = lax.broadcasted_iota(jnp.int32, (count, 256), 0)
        chosen = jnp.where(index == wanted[:, j : j + 256], 1.0, 0.0).astype(BF)
        found = dot(digits, chosen)
        ordered = found[0:1] * 256.0 + found[1:2]
        cells_out[:, j : j + 256] = jnp.broadcast_to(ordered, (8, 256))
    observed_out[...] = observed[...] + 0.0 * pack[0:1, :]


def pick_tables(cells, table_rows):
    count = cells.shape[1]
    column = jnp.transpose(jnp.broadcast_to(cells.astype(F32), (128, count)))
    column = column.astype(jnp.int32)
    row_of = jnp.concatenate([column // 128] * (table_rows // 128), axis=1)
    lane_of = jnp.concatenate([column % 128] * 2, axis=1)
    lanes = lax.broadcasted_iota(jnp.int32, (count, table_rows), 1)
    rows_table = jnp.where(row_of == lanes, 1.0, 0.0).astype(BF)
    lanes2 = lax.broadcasted_iota(jnp.int32, (count, 256), 1) % 128
    lane_table = jnp.where(lane_of == lanes2, 1.0, 0.0)
    return rows_table, lane_table


def extract(field, step, rows_table, lane_table):
    rows, span_y, span_z = field.shape
    pair = jnp.concatenate(split(field.reshape(rows * span_y, span_z)), axis=1)
    which = lax.broadcasted_iota(jnp.int32, (16, 2 * span_z), 0)
    ones = jnp.where(which == step, 1.0, 0.0).astype(BF)
    out = []
    for j in range(0, rows_table.shape[0], 256):
        found = dot(rows_table[j : j + 256], pair)
        kept = (found * lane_table[j : j + 256]).astype(BF)
        out.append(dot(ones, kept, (((1,), (1,)), ((), ()))))
    return jnp.concatenate(out, axis=1)


def forward_round(
    index, refs_in, zmat, ymat, model, packs, fields, buf_a, buf_b, mask, after_step=None
):
    steps = ROUNDS[index]
    done = sum(ROUNDS[:index])
    rows = 16
    own = RAD * steps
    cur, old = buf_a, buf_b
    wide, narrow = RAD * steps, RAD * (steps - 1)
    odd = parity()
    shape = cur.shape[1:]
    low, high = own - wide, own + rows
    cur_outer = jnp.where(odd == 0, low, high)
    cur_mate = jnp.where(odd == 0, high, low)
    if index == 0:
        now, before, now_outer, now_mate, before_outer, before_mate = refs_in
        cur[own : own + rows] = now[...]
        old[own : own + rows] = before[...]
        cur[pl.ds(cur_outer, wide)] = now_outer[...]
        cur[pl.ds(cur_mate, wide)] = now_mate[...]
        size = narrow * shape[0]
        low = own - narrow
        old[pl.ds(jnp.where(odd == 0, low, high), narrow)] = before_outer[:size].reshape((narrow,) + shape)
        old[pl.ds(jnp.where(odd == 0, high, low), narrow)] = before_mate[:size].reshape((narrow,) + shape)
    else:
        earlier, known, got_outer, got_mate = refs_in
        cur[own : own + rows] = earlier[earlier.shape[0] - 1]
        old[own : own + rows] = earlier[earlier.shape[0] - 2]
        cur[pl.ds(cur_outer, wide)] = got_outer[0:wide]
        cur[pl.ds(cur_mate, wide)] = got_mate[0:wide]
        old[own - RAD : own] = known[0]
        old[own + rows : own + rows + RAD] = known[1]
        low, high = own - narrow, own + rows + RAD
        more = narrow - RAD
        old[pl.ds(jnp.where(odd == 0, low, high), more)] = got_outer[wide:]
        old[pl.ds(jnp.where(odd == 0, high, low), more)] = got_mate[wide:]
    mask[...] = jnp.zeros(mask.shape, F32)
    for block in (-1, 0, 1):
        mark_source(mask, jnp.max(packs[block + 1, NT : 2 * NT]).astype(jnp.int32), block, rows)
    for step in range(steps):
        halo = RAD * (steps - 1 - step)
        amounts = [jnp.broadcast_to(packs[i, done + step : done + step + 1], (8, shape[1])) for i in range(3)]

        def extra(x, column):
            place = x - own + rows
            return mask[place, column] * amounts[place // rows]

        def keep(x, column, tile):
            if own <= x < own + rows:
                fields[step, x - own, column] = tile

        advance(cur, old, model, zmat, ymat, own - halo, own + rows + halo, HALO - own, extra, keep)
        if after_step:
            after_step(step, old[own : own + rows])
        cur, old = old, cur
    return cur, old, own


def gather_packs(pack_own, outer, mate, packs):
    odd = parity()
    packs[2 * odd] = outer[outer.shape[0] - 16 :]
    packs[1] = pack_own[...]
    packs[2 - 2 * odd] = mate[mate.shape[0] - 16 :]


def forward_kernel(index, *refs):
    take = 6 if index == 0 else 4
    refs_in, refs = refs[:take], refs[take:]
    zmat, ymat, model, pack, fields, known, send = refs[:7]
    if index == 0:
        packs, buf_a, buf_b, mask = refs[7:]
        gather_packs(pack, refs_in[4], refs_in[5], packs)
    else:
        packs, (buf_a, buf_b, mask) = pack, refs[7:]
    cur, old, own = forward_round(index, refs_in, zmat, ymat, model, packs, fields, buf_a, buf_b, mask)
    rows = 16
    known[0] = old[own - RAD : own]
    known[1] = old[own + rows : own + rows + RAD]
    send[0:rows] = cur[own : own + rows]
    send[rows:] = old[own + RAD : own + rows - RAD]


def split_exactly(values):
    high = values.astype(BF)
    rest = values - high.astype(F32)
    middle = rest.astype(BF)
    return high, middle, (rest - middle.astype(F32)).astype(BF)


def in_send_order(observed, count):
    owners = observed.shape[0]
    per_owner = count // owners
    slot = lax.broadcasted_iota(jnp.int32, (owners, count), 1)
    owner = lax.broadcasted_iota(jnp.int32, (owners, count), 0)
    owned = jnp.where(slot // per_owner == owner, 1.0, 0.0).astype(BF)
    spread = jnp.zeros((NT * per_owner, count), F32)
    for part in split_exactly(observed):
        spread = spread + dot(part, owned, (((0,), (0,)), ((), ())))
    line = lax.broadcasted_iota(jnp.int32, (per_owner, count), 0)
    slot = lax.broadcasted_iota(jnp.int32, (per_owner, count), 1)
    hit = slot % per_owner == line
    out = []
    for step in range(NT):
        part = spread[step * per_owner : (step + 1) * per_owner]
        out.append(jnp.sum(jnp.where(hit, part, 0.0), axis=0, keepdims=True))
    return jnp.concatenate(out, axis=0)


def tables_kernel(count, *refs):
    (cells, observed, *fields), (rows_out, lanes_out, traces) = refs[:-3], refs[-3:]
    rows_table, lane_table = pick_tables(cells[0:1].astype(jnp.int32), rows_out.shape[1])
    rows_out[...] = rows_table
    lanes_out[...] = lane_table
    total = jnp.zeros((16, count), F32)
    step = 0
    for group in fields:
        for i in range(group.shape[0]):
            total = total + extract(group[i], step, rows_table, lane_table)
            step += 1
    traces[...] = total[:NT] - in_send_order(observed[...], count)


def last_kernel(index, *refs):
    take = 6 if index == 0 else 4
    refs_in, refs = refs[:take], refs[take:]
    zmat, ymat, model, packs, cells, rows_table, lane_table, traces = refs[:8]
    fields, adj, buf_a, buf_b, mask = refs[8:]
    done = sum(ROUNDS[:index])
    total = [traces[...]]

    def pick(step, field):
        total[0] = total[0] + extract(field, done + step, rows_table[...], lane_table[...])[:NT]

    forward_round(index, refs_in, zmat, ymat, model, packs, fields, buf_a, buf_b, mask, pick)
    adj[0:NT] = total[0]
    adj[NT:] = cells[...]


def source_planes(rows_table, lane_table, amounts, span_z):
    tiles = split(jnp.broadcast_to(amounts, (16, amounts.shape[1])))
    both = jnp.concatenate(
        [lane_table[z : z + 16] * tile for tile in tiles for z in range(0, span_z, 16)], axis=0
    )
    added = dot(rows_table, both, (((1,), (1,)), ((), ())))
    return added[:, :span_z] + added[:, span_z:]


def injection_lanes(cells, span_z):
    sub = lax.broadcasted_iota(jnp.int32, (span_z, cells.shape[1]), 0)
    return jnp.where(sub == cells % span_z, 1.0, 0.0).astype(BF)


def injection_table(cells, table_rows, span_z):
    sub = lax.broadcasted_iota(jnp.int32, (table_rows, cells.shape[1]), 0)
    return jnp.where(sub == cells // span_z, 1.0, 0.0).astype(BF)


def own_sources_kernel(adj, out):
    rows, span_y, span_z = out.shape[1:]
    cells = adj[NT : NT + 1].astype(jnp.int32)
    table = injection_table(cells, rows * span_y, span_z)
    lanes = injection_lanes(cells, span_z)
    for step in range(NT):
        added = source_planes(table, lanes, adj[step : step + 1], span_z)
        out[step] = added.reshape(rows, span_y, span_z)


def pair_kernel(adj, mate, out):
    odd = parity()
    out[odd] = adj[...]
    out[1 - odd] = mate[...]


def adjoint_kernel(field_groups, slabs, *refs):
    fields = []
    for ref in refs[:field_groups]:
        fields += [ref.at[i] for i in range(ref.shape[0])]
    refs = refs[field_groups:]
    zmat, ymat, model, sources, own_pair, even_pair, odd_pair = refs[:7]
    outs = refs[7 : 7 + slabs]
    buf_a, buf_b, planes, image, rows_table, adjs, near = refs[7 + slabs :]
    odd = parity()
    odd_chip = lax.rem(lax.axis_index("shot") // 2, 2)
    near[2:4] = own_pair[...]
    near[pl.ds(4 - 4 * odd_chip, 2)] = even_pair[...]
    near[pl.ds(4 * odd_chip, 2)] = odd_pair[...]
    rows = 16
    own = HALO
    span_y, span_z = buf_a.shape[1:]
    table_rows = rows * span_y
    lanes = {}
    for block in (-2, -1, 1, 2):
        adjs[block + 2] = near[2 + odd + block]
        cells = adjs[block + 2, NT : NT + 1].astype(jnp.int32)
        rows_table[block + 2] = injection_table(cells, table_rows, span_z)
        lanes[block] = injection_lanes(cells, span_z)

    def place_sources(number, out):
        halo = RAD * (NT - number)
        step = NT - number
        for block in (-2, -1, 1, 2):
            begin = own + block * rows
            first = max(begin, own - halo)
            last = min(begin + rows, own + rows + halo)
            if first >= last:
                continue
            table = rows_table[block + 2, (first - begin) * span_y : (last - begin) * span_y, :]
            added = source_planes(table, lanes[block], adjs[block + 2, step : step + 1], span_z)
            out[first:last] = added.reshape(last - first, span_y, span_z)

    cur, old = buf_a, buf_b
    place_sources(1, cur)
    cur[own : own + rows] = sources[NT - 1]
    old[...] = jnp.zeros(old.shape, F32)
    image[...] = sources[NT - 1] * fields[NT - 1][...]
    for number in range(2, NT + 1):
        halo = RAD * (NT - number)
        step = NT - number
        place_sources(number, planes)

        def extra(x, column):
            return sources[step, x - own, column] if own <= x < own + rows else planes[x, column]

        def keep(x, column, tile):
            if own <= x < own + rows:
                image[x - own, column] = image[x - own, column] + tile * fields[step][x - own, column]

        advance(cur, old, model, zmat, ymat, own - halo, own + rows + halo, 0, extra, keep)
        cur, old = old, cur
    mine = lax.axis_index("shot") // PIECES
    thick = rows // slabs
    for i in range(slabs):
        outs[i][...] = image[pl.ds((mine ^ i) * thick, thick)]


def call(kernel, outs, ins, specs=None, scratch=(), cost=(1e6, 1e6), name=None):
    return pl.pallas_call(
        kernel,
        out_shape=outs,
        in_specs=specs or [VMEM] * len(ins),
        out_specs=jax.tree.map(lambda _: VMEM, outs),
        scratch_shapes=list(scratch),
        compiler_params=pltpu.CompilerParams(vmem_limit_bytes=48 * 1024 * 1024),
        cost_estimate=pl.CostEstimate(flops=int(cost[0]), bytes_accessed=int(cost[1]), transcendentals=0),
        name=name,
    )(*ins)


def swapped(value, partner):
    count = lax.axis_size("shot")
    return lax.ppermute(value, "shot", [(d, partner(d) % count) for d in range(count)])


def with_mate(value):
    return swapped(value, lambda d: d ^ 1)


def with_outer(value):
    return swapped(value, lambda d: d + 1 if d % 2 else d - 1)


def with_even_pair(value):
    return swapped(value, lambda d: d ^ 2)


def with_odd_pair(value):
    return swapped(value, lambda d: d + 2 if d % 4 >= 2 else d - 2)


def per_device(
    courant_sq, wave_now, wave_before, wavelet, source_cell, receiver_cell, send_order, observed
):
    devices = lax.axis_size("shot")
    rows, span_y, span_z = wave_now.shape
    count = receiver_cell.shape[0]
    table_rows = rows * span_y
    plane = (span_y, span_z)

    narrow = RAD * (ROUNDS[0] - 1)
    now_outer, now_mate = with_outer(wave_now), with_mate(wave_now)
    message = jax.ShapeDtypeStruct((narrow * span_y + 16, span_z), F32)
    to_outer, to_mate, pack, before = call(
        message_kernel,
        (message, message, jax.ShapeDtypeStruct((16, span_z), F32), jax.ShapeDtypeStruct(wave_before.shape, F32)),
        (wave_before, wavelet, source_cell),
        specs=[VMEM, SMEM, SMEM],
        name="message",
    )
    before_outer, before_mate = with_outer(to_outer), with_mate(to_mate)

    model, cells, observed, now, ymat, zmat = call(
        prepare_kernel,
        (
            jax.ShapeDtypeStruct((rows + 2 * HALO,) + plane, F32),
            jax.ShapeDtypeStruct((8, count), F32),
            jax.ShapeDtypeStruct(observed.shape, F32),
            jax.ShapeDtypeStruct(wave_now.shape, F32),
            jax.ShapeDtypeStruct((GROUP * span_y, GROUP * span_y), BF),
            jax.ShapeDtypeStruct((2 * span_z, 2 * span_z), BF),
        ),
        (courant_sq, receiver_cell.reshape(1, count), send_order.reshape(1, count), observed, pack, wave_now),
        name="prepare",
    )
    recorded = lax.all_to_all(observed, "shot", split_axis=0, concat_axis=0, tiled=True)

    common = (zmat, ymat, model)
    field_list = []
    ins = (now, before, now_outer, now_mate, before_outer, before_mate)
    for index in range(len(ROUNDS) - 1):
        window = rows + 2 * RAD * ROUNDS[index]
        sent = 2 * rows - 2 * RAD
        packs = (jax.ShapeDtypeStruct((3, 16, span_z), F32),) if index == 0 else ()
        fields, known, send, *made = call(
            functools.partial(forward_kernel, index),
            (
                jax.ShapeDtypeStruct((ROUNDS[index], rows) + plane, F32),
                jax.ShapeDtypeStruct((2, RAD) + plane, F32),
                jax.ShapeDtypeStruct((sent,) + plane, F32),
            )
            + packs,
            ins + common + (pack,),
            scratch=[pltpu.VMEM((window,) + plane, F32)] * 2 + [pltpu.VMEM((3 * rows,) + plane, F32)],
            name="forward",
        )
        field_list.append(fields)
        pack = made[0] if made else pack
        ins = (fields, known, with_outer(send), with_mate(send))

    rows_table, lane_table, traces = call(
        functools.partial(tables_kernel, count),
        (
            jax.ShapeDtypeStruct((count, table_rows), BF),
            jax.ShapeDtypeStruct((count, 256), F32),
            jax.ShapeDtypeStruct((NT, count), F32),
        ),
        (cells, recorded, *field_list),
        name="traces",
    )
    index = len(ROUNDS) - 1
    window = rows + 2 * RAD * ROUNDS[index]
    fields, adj = call(
        functools.partial(last_kernel, index),
        (
            jax.ShapeDtypeStruct((ROUNDS[index], rows) + plane, F32),
            jax.ShapeDtypeStruct((2 * NT, count), F32),
        ),
        ins + common + (pack, cells, rows_table, lane_table, traces),
        scratch=[pltpu.VMEM((window,) + plane, F32)] * 2 + [pltpu.VMEM((3 * rows,) + plane, F32)],
        name="forward_last",
    )
    field_list.append(fields)

    sources = call(
        own_sources_kernel, jax.ShapeDtypeStruct((NT, rows) + plane, F32), (adj,), name="own_sources"
    )
    pair = call(
        pair_kernel, jax.ShapeDtypeStruct((2, 2 * NT, count), F32), (adj, with_mate(adj)), name="pair"
    )
    adjs = [sources, pair, with_even_pair(pair), with_odd_pair(pair)]
    slabs = devices // PIECES
    thick = rows // slabs
    parts = call(
        functools.partial(adjoint_kernel, len(field_list), slabs),
        tuple(jax.ShapeDtypeStruct((thick,) + plane, F32) for _ in range(slabs)),
        (*field_list, zmat, ymat, model, *adjs),
        scratch=[pltpu.VMEM((rows + 2 * HALO,) + plane, F32)] * 3
        + [pltpu.VMEM((rows,) + plane, F32), pltpu.VMEM((5, table_rows, count), BF)]
        + [pltpu.VMEM((5, 2 * NT, count), F32), pltpu.VMEM((6, 2 * NT, count), F32)],
        name="adjoint",
    )
    total = parts[0]
    for i in range(1, slabs):
        total = total + swapped(parts[i], lambda d: d ^ (i * PIECES))
    return total


def solution(mesh):
    return jax.shard_map(
        per_device,
        mesh=mesh,
        in_specs=(
            P("groups", None, None),
            P(("groups", "shot"), None, None),
            P(("groups", "shot"), None, None),
            P(("groups", "shot"), None),
            P(("groups", "shot")),
            P(("groups", "shot")),
            P(("groups", "shot")),
            P(("groups", "shot"), None),
        ),
        out_specs=P(("groups", "shot"), None, None),
        check_vma=False,
    )
```

```python
import functools

import jax
import jax.numpy as jnp
from jax import lax
from jax.experimental import pallas as pl
from jax.experimental.pallas import tpu as pltpu
from jax.sharding import PartitionSpec as P

NT = 8
PIECES = 4
RAD = 4
ROUNDS = (4, 4)
SCALE = 5040.0
CENTER_Y = -43008.0
CENTER_Z = -42.0
WEIGHTS = (8064.0, -1008.0, 128.0, -9.0)
GROUP = 8
HALO = RAD * (NT - 1)
BF = jnp.bfloat16
F32 = jnp.float32

VMEM = pl.BlockSpec(memory_space=pltpu.VMEM)
SMEM = pl.BlockSpec(memory_space=pltpu.SMEM)


def band(distance, center):
    out = jnp.where(distance == 0, center, 0.0)
    for k, weight in enumerate(WEIGHTS, 1):
        out = jnp.where(jnp.abs(distance) == k, weight, out)
    return out


def build_bands(span_y, span_z, rows_out, fixed_out):
    size = GROUP * span_y
    row = lax.broadcasted_iota(jnp.int32, (size, size), 0)
    col = lax.broadcasted_iota(jnp.int32, (size, size), 1)
    tile = 8 * GROUP
    y_row = row // tile * 8 + row % 8
    y_col = col // tile * 8 + col % 8
    x_far = (row // 8) % GROUP - (col // 8) % GROUP
    y_far = y_row - y_col
    across = jnp.where(y_far == 0, band(x_far, 0.0), 0.0)
    rows_out[...] = jnp.where(x_far == 0, band(y_far, CENTER_Y), across).astype(BF)
    z = lax.broadcasted_iota(jnp.int32, (2 * span_z, 2 * span_z), 0) % span_z
    to = lax.broadcasted_iota(jnp.int32, (2 * span_z, 2 * span_z), 1)
    fixed_out[...] = jnp.where(to < span_z, band(z - to, CENTER_Z), 0.0).astype(BF)


def split(values):
    high = values.astype(BF)
    low = (values - high.astype(F32)).astype(BF)
    return high, low


def dot(a, b, dims=(((1,), (0,)), ((), ()))):
    return lax.dot_general(a, b, dims, preferred_element_type=F32)


def advance(cur, old, model, zmat, ymat, first, last, model_shift, extra, keep):
    span_y, span_z = cur.shape[1:]
    zmat, ymat = zmat[...], ymat[...]
    for base in range(first, last, GROUP):
        columns = [slice(j, j + 8) for j in range(0, span_y, 8)]
        order = [(i, column) for column in columns for i in range(GROUP)]
        group = jnp.concatenate([cur[base + i, column] for i, column in order], axis=0)
        pair = jnp.concatenate(split(group), axis=1)
        left = jnp.concatenate([ymat, pair], axis=1)
        right = jnp.concatenate([pair, zmat], axis=0)
        part = dot(left, right)
        for j, column in enumerate(columns):
            tiles = [cur[base - RAD + q, column] for q in range(GROUP + 2 * RAD)]
            for i in range(GROUP):
                x = base + i
                at = (j * GROUP + i) * 8
                rows = slice(at, at + 8)
                here = tiles[i + RAD]
                total = part[rows, :span_z] + part[rows, span_z:]
                for k, weight in enumerate(WEIGHTS, 1):
                    if i + k >= GROUP:
                        total = total + weight * tiles[i + RAD + k]
                    if i < k:
                        total = total + weight * tiles[i + RAD - k]
                tile = (here + here - old[x, column]) + model[x + model_shift, column] * total + extra(x, column)
                old[x, column] = tile
                keep(x, column, tile)


def mark_source(mask, cell, block, rows):
    span_y, span_z = mask.shape[1:]
    plane = (1 + block) * rows + cell // (span_y * span_z)
    y = (cell // span_z) % span_y
    tile = pl.ds(pl.multiple_of((y // 8) * 8, 8), 8)
    sub = lax.broadcasted_iota(jnp.int32, (8, span_z), 0)
    lane = lax.broadcasted_iota(jnp.int32, (8, span_z), 1)
    mask[plane, tile, :] = jnp.where((sub == y % 8) & (lane == cell % span_z), 1.0, 0.0)


def parity():
    return lax.rem(lax.axis_index("shot"), 2)


def message_kernel(before, wavelet, source, outer_out, mate_out, pack_out, before_out):
    rows, span_y, span_z = before.shape
    which = lax.broadcasted_iota(jnp.int32, (16, span_z), 0)
    pack = jnp.where(which >= NT, source[0].astype(F32), 0.0)
    for step in range(NT):
        pack = jnp.where(which == step, wavelet[0, step], pack)
    pack_out[...] = pack
    before_out[...] = before[...]
    narrow = RAD * (ROUNDS[0] - 1)
    size = narrow * span_y
    odd = parity()
    outer_out[:size] = before[pl.ds(odd * (rows - narrow), narrow)].reshape(size, span_z)
    mate_out[:size] = before[pl.ds((1 - odd) * (rows - narrow), narrow)].reshape(size, span_z)
    outer_out[size:] = pack
    mate_out[size:] = pack


def prepare_kernel(courant, table, observed, pack, now, model_out, cells_out, observed_out, now_out, ymat_out, zmat_out):
    rows, span_y, span_z = now.shape
    now_out[...] = now[...]
    build_bands(span_y, span_z, ymat_out, zmat_out)
    piece = lax.rem(lax.axis_index("shot"), PIECES)
    period = courant.shape[0]
    window = model_out.shape[0]
    for chunk in range(0, window, RAD):
        source = lax.rem(piece * rows - HALO + chunk + period, period)
        model_out[chunk : chunk + RAD] = courant[pl.ds(source, RAD)] * (1.0 / SCALE)
    count = cells_out.shape[1]
    cell = table[:, :count]
    wanted = table[:, count:]
    which = lax.broadcasted_iota(jnp.int32, (16, count), 0)
    digits = jnp.where(which == 0, cell // 256, jnp.where(which == 1, cell % 256, 0)).astype(F32).astype(BF)
    for j in range(0, count, 256):
        index = lax.broadcasted_iota(jnp.int32, (count, 256), 0)
        chosen = jnp.where(index == wanted[:, j : j + 256], 1.0, 0.0).astype(BF)
        found = dot(digits, chosen)
        ordered = found[0:1] * 256.0 + found[1:2]
        cells_out[:, j : j + 256] = jnp.broadcast_to(ordered, (8, 256))
    observed_out[...] = observed[...] + 0.0 * pack[0:1, :]


def pick_tables(cells, table_rows):
    count = cells.shape[1]
    column = jnp.transpose(jnp.broadcast_to(cells.astype(F32), (128, count)))
    column = column.astype(jnp.int32)
    row_of = jnp.concatenate([column // 128] * (table_rows // 128), axis=1)
    lane_of = jnp.concatenate([column % 128] * 2, axis=1)
    lanes = lax.broadcasted_iota(jnp.int32, (count, table_rows), 1)
    rows_table = jnp.where(row_of == lanes, 1.0, 0.0).astype(BF)
    lanes2 = lax.broadcasted_iota(jnp.int32, (count, 256), 1) % 128
    lane_table = jnp.where(lane_of == lanes2, 1.0, 0.0)
    return rows_table, lane_table


def extract(field, step, rows_table, lane_table):
    rows, span_y, span_z = field.shape
    pair = jnp.concatenate(split(field.reshape(rows * span_y, span_z)), axis=1)
    which = lax.broadcasted_iota(jnp.int32, (16, 2 * span_z), 0)
    ones = jnp.where(which == step, 1.0, 0.0).astype(BF)
    out = []
    for j in range(0, rows_table.shape[0], 256):
        found = dot(rows_table[j : j + 256], pair)
        kept = (found * lane_table[j : j + 256]).astype(BF)
        out.append(dot(ones, kept, (((1,), (1,)), ((), ()))))
    return jnp.concatenate(out, axis=1)


def forward_round(
    index, refs_in, zmat, ymat, model, packs, fields, buf_a, buf_b, mask, after_step=None
):
    steps = ROUNDS[index]
    done = sum(ROUNDS[:index])
    rows = 16
    own = RAD * steps
    cur, old = buf_a, buf_b
    wide, narrow = RAD * steps, RAD * (steps - 1)
    odd = parity()
    shape = cur.shape[1:]
    low, high = own - wide, own + rows
    cur_outer = jnp.where(odd == 0, low, high)
    cur_mate = jnp.where(odd == 0, high, low)
    if index == 0:
        now, before, now_outer, now_mate, before_outer, before_mate = refs_in
        cur[own : own + rows] = now[...]
        old[own : own + rows] = before[...]
        cur[pl.ds(cur_outer, wide)] = now_outer[...]
        cur[pl.ds(cur_mate, wide)] = now_mate[...]
        size = narrow * shape[0]
        low = own - narrow
        old[pl.ds(jnp.where(odd == 0, low, high), narrow)] = before_outer[:size].reshape((narrow,) + shape)
        old[pl.ds(jnp.where(odd == 0, high, low), narrow)] = before_mate[:size].reshape((narrow,) + shape)
    else:
        earlier, known, got_outer, got_mate = refs_in
        cur[own : own + rows] = earlier[earlier.shape[0] - 1]
        old[own : own + rows] = earlier[earlier.shape[0] - 2]
        cur[pl.ds(cur_outer, wide)] = got_outer[0:wide]
        cur[pl.ds(cur_mate, wide)] = got_mate[0:wide]
        old[own - RAD : own] = known[0]
        old[own + rows : own + rows + RAD] = known[1]
        low, high = own - narrow, own + rows + RAD
        more = narrow - RAD
        old[pl.ds(jnp.where(odd == 0, low, high), more)] = got_outer[wide:]
        old[pl.ds(jnp.where(odd == 0, high, low), more)] = got_mate[wide:]
    mask[...] = jnp.zeros(mask.shape, F32)
    for block in (-1, 0, 1):
        mark_source(mask, jnp.max(packs[block + 1, NT : 2 * NT]).astype(jnp.int32), block, rows)
    for step in range(steps):
        halo = RAD * (steps - 1 - step)
        amounts = [jnp.broadcast_to(packs[i, done + step : done + step + 1], (8, shape[1])) for i in range(3)]

        def extra(x, column):
            place = x - own + rows
            return mask[place, column] * amounts[place // rows]

        def keep(x, column, tile):
            if own <= x < own + rows:
                fields[step, x - own, column] = tile

        advance(cur, old, model, zmat, ymat, own - halo, own + rows + halo, HALO - own, extra, keep)
        if after_step:
            after_step(step, old[own : own + rows])
        cur, old = old, cur
    return cur, old, own


def gather_packs(pack_own, outer, mate, packs):
    odd = parity()
    packs[2 * odd] = outer[outer.shape[0] - 16 :]
    packs[1] = pack_own[...]
    packs[2 - 2 * odd] = mate[mate.shape[0] - 16 :]


def forward_kernel(index, *refs):
    take = 6 if index == 0 else 4
    refs_in, refs = refs[:take], refs[take:]
    zmat, ymat, model, pack, fields, known, send = refs[:7]
    if index == 0:
        packs, buf_a, buf_b, mask = refs[7:]
        gather_packs(pack, refs_in[4], refs_in[5], packs)
    else:
        packs, (buf_a, buf_b, mask) = pack, refs[7:]
    cur, old, own = forward_round(index, refs_in, zmat, ymat, model, packs, fields, buf_a, buf_b, mask)
    rows = 16
    known[0] = old[own - RAD : own]
    known[1] = old[own + rows : own + rows + RAD]
    send[0:rows] = cur[own : own + rows]
    send[rows:] = old[own + RAD : own + rows - RAD]


def split_exactly(values):
    high = values.astype(BF)
    rest = values - high.astype(F32)
    middle = rest.astype(BF)
    return high, middle, (rest - middle.astype(F32)).astype(BF)


def in_send_order(observed, count):
    owners = observed.shape[0]
    per_owner = count // owners
    slot = lax.broadcasted_iota(jnp.int32, (owners, count), 1)
    owner = lax.broadcasted_iota(jnp.int32, (owners, count), 0)
    owned = jnp.where(slot // per_owner == owner, 1.0, 0.0).astype(BF)
    spread = jnp.zeros((NT * per_owner, count), F32)
    for part in split_exactly(observed):
        spread = spread + dot(part, owned, (((0,), (0,)), ((), ())))
    line = lax.broadcasted_iota(jnp.int32, (per_owner, count), 0)
    slot = lax.broadcasted_iota(jnp.int32, (per_owner, count), 1)
    hit = slot % per_owner == line
    out = []
    for step in range(NT):
        part = spread[step * per_owner : (step + 1) * per_owner]
        out.append(jnp.sum(jnp.where(hit, part, 0.0), axis=0, keepdims=True))
    return jnp.concatenate(out, axis=0)


def tables_kernel(count, *refs):
    (cells, observed, *fields), (rows_out, lanes_out, traces) = refs[:-3], refs[-3:]
    rows_table, lane_table = pick_tables(cells[0:1].astype(jnp.int32), rows_out.shape[1])
    rows_out[...] = rows_table
    lanes_out[...] = lane_table
    total = jnp.zeros((16, count), F32)
    step = 0
    for group in fields:
        for i in range(group.shape[0]):
            total = total + extract(group[i], step, rows_table, lane_table)
            step += 1
    traces[...] = total[:NT] - in_send_order(observed[...], count)


def last_kernel(index, *refs):
    take = 6 if index == 0 else 4
    refs_in, refs = refs[:take], refs[take:]
    zmat, ymat, model, packs, cells, rows_table, lane_table, traces = refs[:8]
    fields, adj, buf_a, buf_b, mask = refs[8:]
    done = sum(ROUNDS[:index])
    total = [traces[...]]

    def pick(step, field):
        total[0] = total[0] + extract(field, done + step, rows_table[...], lane_table[...])[:NT]

    forward_round(index, refs_in, zmat, ymat, model, packs, fields, buf_a, buf_b, mask, pick)
    adj[0:NT] = total[0]
    adj[NT:] = cells[...]


def source_planes(rows_table, lane_table, amounts, span_z):
    tiles = split(jnp.broadcast_to(amounts, (16, amounts.shape[1])))
    both = jnp.concatenate(
        [lane_table[z : z + 16] * tile for tile in tiles for z in range(0, span_z, 16)], axis=0
    )
    added = dot(rows_table, both, (((1,), (1,)), ((), ())))
    return added[:, :span_z] + added[:, span_z:]


def injection_lanes(cells, span_z):
    sub = lax.broadcasted_iota(jnp.int32, (span_z, cells.shape[1]), 0)
    return jnp.where(sub == cells % span_z, 1.0, 0.0).astype(BF)


def injection_table(cells, table_rows, span_z):
    sub = lax.broadcasted_iota(jnp.int32, (table_rows, cells.shape[1]), 0)
    return jnp.where(sub == cells // span_z, 1.0, 0.0).astype(BF)


def own_sources_kernel(adj, out):
    rows, span_y, span_z = out.shape[1:]
    cells = adj[NT : NT + 1].astype(jnp.int32)
    table = injection_table(cells, rows * span_y, span_z)
    lanes = injection_lanes(cells, span_z)
    for step in range(NT):
        added = source_planes(table, lanes, adj[step : step + 1], span_z)
        out[step] = added.reshape(rows, span_y, span_z)


def pair_kernel(adj, mate, out):
    odd = parity()
    out[odd] = adj[...]
    out[1 - odd] = mate[...]


def adjoint_kernel(field_groups, slabs, *refs):
    fields = []
    for ref in refs[:field_groups]:
        fields += [ref.at[i] for i in range(ref.shape[0])]
    refs = refs[field_groups:]
    zmat, ymat, model, sources, own_pair, even_pair, odd_pair = refs[:7]
    outs = refs[7 : 7 + slabs]
    buf_a, buf_b, planes, image, rows_table, adjs, near = refs[7 + slabs :]
    odd = parity()
    odd_chip = lax.rem(lax.axis_index("shot") // 2, 2)
    near[2:4] = own_pair[...]
    near[pl.ds(4 - 4 * odd_chip, 2)] = even_pair[...]
    near[pl.ds(4 * odd_chip, 2)] = odd_pair[...]
    rows = 16
    own = HALO
    span_y, span_z = buf_a.shape[1:]
    table_rows = rows * span_y
    lanes = {}
    for block in (-2, -1, 1, 2):
        adjs[block + 2] = near[2 + odd + block]
        cells = adjs[block + 2, NT : NT + 1].astype(jnp.int32)
        rows_table[block + 2] = injection_table(cells, table_rows, span_z)
        lanes[block] = injection_lanes(cells, span_z)

    def place_sources(number, out):
        halo = RAD * (NT - number)
        step = NT - number
        for block in (-2, -1, 1, 2):
            begin = own + block * rows
            first = max(begin, own - halo)
            last = min(begin + rows, own + rows + halo)
            if first >= last:
                continue
            table = rows_table[block + 2, (first - begin) * span_y : (last - begin) * span_y, :]
            added = source_planes(table, lanes[block], adjs[block + 2, step : step + 1], span_z)
            out[first:last] = added.reshape(last - first, span_y, span_z)

    cur, old = buf_a, buf_b
    place_sources(1, cur)
    cur[own : own + rows] = sources[NT - 1]
    old[...] = jnp.zeros(old.shape, F32)
    image[...] = sources[NT - 1] * fields[NT - 1][...]
    for number in range(2, NT + 1):
        halo = RAD * (NT - number)
        step = NT - number
        place_sources(number, planes)

        def extra(x, column):
            return sources[step, x - own, column] if own <= x < own + rows else planes[x, column]

        def keep(x, column, tile):
            if own <= x < own + rows:
                image[x - own, column] = image[x - own, column] + tile * fields[step][x - own, column]

        advance(cur, old, model, zmat, ymat, own - halo, own + rows + halo, 0, extra, keep)
        cur, old = old, cur
    mine = lax.axis_index("shot") // PIECES
    thick = rows // slabs
    for i in range(slabs):
        outs[i][...] = image[pl.ds((mine ^ i) * thick, thick)]


def call(kernel, outs, ins, specs=None, scratch=(), cost=(1e6, 1e6), name=None):
    return pl.pallas_call(
        kernel,
        out_shape=outs,
        in_specs=specs or [VMEM] * len(ins),
        out_specs=jax.tree.map(lambda _: VMEM, outs),
        scratch_shapes=list(scratch),
        compiler_params=pltpu.CompilerParams(vmem_limit_bytes=48 * 1024 * 1024),
        cost_estimate=pl.CostEstimate(flops=int(cost[0]), bytes_accessed=int(cost[1]), transcendentals=0),
        name=name,
    )(*ins)


def swapped(value, partner):
    count = lax.axis_size("shot")
    return lax.ppermute(value, "shot", [(d, partner(d) % count) for d in range(count)])


def with_mate(value):
    return swapped(value, lambda d: d ^ 1)


def with_outer(value):
    return swapped(value, lambda d: d + 1 if d % 2 else d - 1)


def with_even_pair(value):
    return swapped(value, lambda d: d ^ 2)


def with_odd_pair(value):
    return swapped(value, lambda d: d + 2 if d % 4 >= 2 else d - 2)


def per_device(
    courant_sq, wave_now, wave_before, wavelet, source_cell, receiver_cell, send_order, observed
):
    devices = lax.axis_size("shot")
    rows, span_y, span_z = wave_now.shape
    count = receiver_cell.shape[0]
    table_rows = rows * span_y
    plane = (span_y, span_z)

    narrow = RAD * (ROUNDS[0] - 1)
    now_outer, now_mate = with_outer(wave_now), with_mate(wave_now)
    message = jax.ShapeDtypeStruct((narrow * span_y + 16, span_z), F32)
    to_outer, to_mate, pack, before = call(
        message_kernel,
        (message, message, jax.ShapeDtypeStruct((16, span_z), F32), jax.ShapeDtypeStruct(wave_before.shape, F32)),
        (wave_before, wavelet, source_cell),
        specs=[VMEM, SMEM, SMEM],
        name="message",
    )
    before_outer, before_mate = with_outer(to_outer), with_mate(to_mate)

    table = jnp.concatenate([receiver_cell, send_order]).reshape(1, 2 * count)
    model, cells, observed, now, ymat, zmat = call(
        prepare_kernel,
        (
            jax.ShapeDtypeStruct((rows + 2 * HALO,) + plane, F32),
            jax.ShapeDtypeStruct((8, count), F32),
            jax.ShapeDtypeStruct(observed.shape, F32),
            jax.ShapeDtypeStruct(wave_now.shape, F32),
            jax.ShapeDtypeStruct((GROUP * span_y, GROUP * span_y), BF),
            jax.ShapeDtypeStruct((2 * span_z, 2 * span_z), BF),
        ),
        (courant_sq, table, observed, pack, wave_now),
        name="prepare",
    )
    recorded = lax.all_to_all(observed, "shot", split_axis=0, concat_axis=0, tiled=True)

    common = (zmat, ymat, model)
    field_list = []
    ins = (now, before, now_outer, now_mate, before_outer, before_mate)
    for index in range(len(ROUNDS) - 1):
        window = rows + 2 * RAD * ROUNDS[index]
        sent = 2 * rows - 2 * RAD
        packs = (jax.ShapeDtypeStruct((3, 16, span_z), F32),) if index == 0 else ()
        fields, known, send, *made = call(
            functools.partial(forward_kernel, index),
            (
                jax.ShapeDtypeStruct((ROUNDS[index], rows) + plane, F32),
                jax.ShapeDtypeStruct((2, RAD) + plane, F32),
                jax.ShapeDtypeStruct((sent,) + plane, F32),
            )
            + packs,
            ins + common + (pack,),
            scratch=[pltpu.VMEM((window,) + plane, F32)] * 2 + [pltpu.VMEM((3 * rows,) + plane, F32)],
            name="forward",
        )
        field_list.append(fields)
        pack = made[0] if made else pack
        ins = (fields, known, with_outer(send), with_mate(send))

    rows_table, lane_table, traces = call(
        functools.partial(tables_kernel, count),
        (
            jax.ShapeDtypeStruct((count, table_rows), BF),
            jax.ShapeDtypeStruct((count, 256), F32),
            jax.ShapeDtypeStruct((NT, count), F32),
        ),
        (cells, recorded, *field_list),
        name="traces",
    )
    index = len(ROUNDS) - 1
    window = rows + 2 * RAD * ROUNDS[index]
    fields, adj = call(
        functools.partial(last_kernel, index),
        (
            jax.ShapeDtypeStruct((ROUNDS[index], rows) + plane, F32),
            jax.ShapeDtypeStruct((2 * NT, count), F32),
        ),
        ins + common + (pack, cells, rows_table, lane_table, traces),
        scratch=[pltpu.VMEM((window,) + plane, F32)] * 2 + [pltpu.VMEM((3 * rows,) + plane, F32)],
        name="forward_last",
    )
    field_list.append(fields)

    sources = call(
        own_sources_kernel, jax.ShapeDtypeStruct((NT, rows) + plane, F32), (adj,), name="own_sources"
    )
    pair = call(
        pair_kernel, jax.ShapeDtypeStruct((2, 2 * NT, count), F32), (adj, with_mate(adj)), name="pair"
    )
    adjs = [sources, pair, with_even_pair(pair), with_odd_pair(pair)]
    slabs = devices // PIECES
    thick = rows // slabs
    parts = call(
        functools.partial(adjoint_kernel, len(field_list), slabs),
        tuple(jax.ShapeDtypeStruct((thick,) + plane, F32) for _ in range(slabs)),
        (*field_list, zmat, ymat, model, *adjs),
        scratch=[pltpu.VMEM((rows + 2 * HALO,) + plane, F32)] * 3
        + [pltpu.VMEM((rows,) + plane, F32), pltpu.VMEM((5, table_rows, count), BF)]
        + [pltpu.VMEM((5, 2 * NT, count), F32), pltpu.VMEM((6, 2 * NT, count), F32)],
        name="adjoint",
    )
    total = parts[0]
    for i in [*range(2, slabs), 1]:
        total = total + swapped(parts[i], lambda d: d ^ (i * PIECES))
    return total


def solution(mesh):
    return jax.shard_map(
        per_device,
        mesh=mesh,
        in_specs=(
            P("groups", None, None),
            P(("groups", "shot"), None, None),
            P(("groups", "shot"), None, None),
            P(("groups", "shot"), None),
            P(("groups", "shot")),
            P(("groups", "shot")),
            P(("groups", "shot")),
            P(("groups", "shot"), None),
        ),
        out_specs=P(("groups", "shot"), None, None),
        check_vma=False,
    )
```

```python
import functools

import jax
import jax.numpy as jnp
from jax import lax
from jax.experimental import pallas as pl
from jax.experimental.pallas import tpu as pltpu
from jax.sharding import PartitionSpec as P

NT = 8
PIECES = 4
RAD = 4
ROUNDS = (4, 4)
SCALE = 5040.0
CENTER_Y = -43008.0
CENTER_Z = -42.0
WEIGHTS = (8064.0, -1008.0, 128.0, -9.0)
GROUP = 8
HALO = RAD * (NT - 1)
BF = jnp.bfloat16
F32 = jnp.float32

VMEM = pl.BlockSpec(memory_space=pltpu.VMEM)
SMEM = pl.BlockSpec(memory_space=pltpu.SMEM)


def band(distance, center):
    out = jnp.where(distance == 0, center, 0.0)
    for k, weight in enumerate(WEIGHTS, 1):
        out = jnp.where(jnp.abs(distance) == k, weight, out)
    return out


def build_bands(span_y, span_z, rows_out, fixed_out):
    size = GROUP * span_y
    row = lax.broadcasted_iota(jnp.int32, (size, size), 0)
    col = lax.broadcasted_iota(jnp.int32, (size, size), 1)
    tile = 8 * GROUP
    y_row = row // tile * 8 + row % 8
    y_col = col // tile * 8 + col % 8
    x_far = (row // 8) % GROUP - (col // 8) % GROUP
    y_far = y_row - y_col
    across = jnp.where(y_far == 0, band(x_far, 0.0), 0.0)
    rows_out[...] = jnp.where(x_far == 0, band(y_far, CENTER_Y), across).astype(BF)
    z = lax.broadcasted_iota(jnp.int32, (2 * span_z, 2 * span_z), 0) % span_z
    to = lax.broadcasted_iota(jnp.int32, (2 * span_z, 2 * span_z), 1)
    fixed_out[...] = jnp.where(to < span_z, band(z - to, CENTER_Z), 0.0).astype(BF)


def split(values):
    high = values.astype(BF)
    low = (values - high.astype(F32)).astype(BF)
    return high, low


def dot(a, b, dims=(((1,), (0,)), ((), ()))):
    return lax.dot_general(a, b, dims, preferred_element_type=F32)


def advance(cur, old, model, zmat, ymat, first, last, model_shift, extra, keep):
    span_y, span_z = cur.shape[1:]
    zmat, ymat = zmat[...], ymat[...]
    for base in range(first, last, GROUP):
        columns = [slice(j, j + 8) for j in range(0, span_y, 8)]
        order = [(i, column) for column in columns for i in range(GROUP)]
        group = jnp.concatenate([cur[base + i, column] for i, column in order], axis=0)
        pair = jnp.concatenate(split(group), axis=1)
        left = jnp.concatenate([ymat, pair], axis=1)
        right = jnp.concatenate([pair, zmat], axis=0)
        part = dot(left, right)
        for j, column in enumerate(columns):
            tiles = [cur[base - RAD + q, column] for q in range(GROUP + 2 * RAD)]
            for i in range(GROUP):
                x = base + i
                at = (j * GROUP + i) * 8
                rows = slice(at, at + 8)
                here = tiles[i + RAD]
                total = part[rows, :span_z] + part[rows, span_z:]
                for k, weight in enumerate(WEIGHTS, 1):
                    if i + k >= GROUP:
                        total = total + weight * tiles[i + RAD + k]
                    if i < k:
                        total = total + weight * tiles[i + RAD - k]
                tile = (here + here - old[x, column]) + model[x + model_shift, column] * total + extra(x, column)
                old[x, column] = tile
                keep(x, column, tile)


def mark_source(mask, cell, block, rows):
    span_y, span_z = mask.shape[1:]
    plane = (1 + block) * rows + cell // (span_y * span_z)
    y = (cell // span_z) % span_y
    tile = pl.ds(pl.multiple_of((y // 8) * 8, 8), 8)
    sub = lax.broadcasted_iota(jnp.int32, (8, span_z), 0)
    lane = lax.broadcasted_iota(jnp.int32, (8, span_z), 1)
    mask[plane, tile, :] = jnp.where((sub == y % 8) & (lane == cell % span_z), 1.0, 0.0)


def parity():
    return lax.rem(lax.axis_index("shot"), 2)


def message_kernel(before, wavelet, source, outer_out, mate_out, pack_out, before_out):
    rows, span_y, span_z = before.shape
    which = lax.broadcasted_iota(jnp.int32, (16, span_z), 0)
    pack = jnp.where(which >= NT, source[0].astype(F32), 0.0)
    for step in range(NT):
        pack = jnp.where(which == step, wavelet[0, step], pack)
    pack_out[...] = pack
    before_out[...] = before[...]
    narrow = RAD * (ROUNDS[0] - 1)
    size = narrow * span_y
    odd = parity()
    outer_out[:size] = before[pl.ds(odd * (rows - narrow), narrow)].reshape(size, span_z)
    mate_out[:size] = before[pl.ds((1 - odd) * (rows - narrow), narrow)].reshape(size, span_z)
    outer_out[size:] = pack
    mate_out[size:] = pack


def prepare_kernel(courant, table, observed, pack, now, model_out, cells_out, observed_out, now_out, ymat_out, zmat_out):
    rows, span_y, span_z = now.shape
    now_out[...] = now[...]
    build_bands(span_y, span_z, ymat_out, zmat_out)
    piece = lax.rem(lax.axis_index("shot"), PIECES)
    period = courant.shape[0]
    window = model_out.shape[0]
    for chunk in range(0, window, RAD):
        source = lax.rem(piece * rows - HALO + chunk + period, period)
        model_out[chunk : chunk + RAD] = courant[pl.ds(source, RAD)] * (1.0 / SCALE)
    count = cells_out.shape[1]
    cell = table[:, :count]
    wanted = table[:, count:]
    which = lax.broadcasted_iota(jnp.int32, (16, count), 0)
    digits = jnp.where(which == 0, cell // 256, jnp.where(which == 1, cell % 256, 0)).astype(F32).astype(BF)
    for j in range(0, count, 256):
        index = lax.broadcasted_iota(jnp.int32, (count, 256), 0)
        chosen = jnp.where(index == wanted[:, j : j + 256], 1.0, 0.0).astype(BF)
        found = dot(digits, chosen)
        ordered = found[0:1] * 256.0 + found[1:2]
        cells_out[:, j : j + 256] = jnp.broadcast_to(ordered, (8, 256))
    observed_out[...] = observed[...] + 0.0 * pack[0:1, :]


def pick_tables(cells, table_rows):
    count = cells.shape[1]
    column = jnp.transpose(jnp.broadcast_to(cells.astype(F32), (128, count)))
    column = column.astype(jnp.int32)
    row_of = jnp.concatenate([column // 128] * (table_rows // 128), axis=1)
    lane_of = jnp.concatenate([column % 128] * 2, axis=1)
    lanes = lax.broadcasted_iota(jnp.int32, (count, table_rows), 1)
    rows_table = jnp.where(row_of == lanes, 1.0, 0.0).astype(BF)
    lanes2 = lax.broadcasted_iota(jnp.int32, (count, 256), 1) % 128
    lane_table = jnp.where(lane_of == lanes2, 1.0, 0.0)
    return rows_table, lane_table


def extract(field, step, rows_table, lane_table):
    rows, span_y, span_z = field.shape
    pair = jnp.concatenate(split(field.reshape(rows * span_y, span_z)), axis=1)
    which = lax.broadcasted_iota(jnp.int32, (16, 2 * span_z), 0)
    ones = jnp.where(which == step, 1.0, 0.0).astype(BF)
    out = []
    for j in range(0, rows_table.shape[0], 256):
        found = dot(rows_table[j : j + 256], pair)
        kept = (found * lane_table[j : j + 256]).astype(BF)
        out.append(dot(ones, kept, (((1,), (1,)), ((), ()))))
    return jnp.concatenate(out, axis=1)


def forward_round(
    index, refs_in, zmat, ymat, model, packs, fields, buf_a, buf_b, mask, after_step=None
):
    steps = ROUNDS[index]
    done = sum(ROUNDS[:index])
    rows = 16
    own = RAD * steps
    cur, old = buf_a, buf_b
    wide, narrow = RAD * steps, RAD * (steps - 1)
    odd = parity()
    shape = cur.shape[1:]
    low, high = own - wide, own + rows
    cur_outer = jnp.where(odd == 0, low, high)
    cur_mate = jnp.where(odd == 0, high, low)
    if index == 0:
        now, before, now_mate, now_outer, before_outer, before_mate = refs_in
        cur[own : own + rows] = now[...]
        old[own : own + rows] = before[...]
        cur[pl.ds(cur_outer, wide)] = now_outer[...]
        cur[pl.ds(cur_mate, wide)] = now_mate[...]
        size = narrow * shape[0]
        low = own - narrow
        old[pl.ds(jnp.where(odd == 0, low, high), narrow)] = before_outer[:size].reshape((narrow,) + shape)
        old[pl.ds(jnp.where(odd == 0, high, low), narrow)] = before_mate[:size].reshape((narrow,) + shape)
    else:
        earlier, known, got_mate, got_outer = refs_in
        cur[own : own + rows] = earlier[earlier.shape[0] - 1]
        old[own : own + rows] = earlier[earlier.shape[0] - 2]
        cur[pl.ds(cur_outer, wide)] = got_outer[0:wide]
        cur[pl.ds(cur_mate, wide)] = got_mate[0:wide]
        old[own - RAD : own] = known[0]
        old[own + rows : own + rows + RAD] = known[1]
        low, high = own - narrow, own + rows + RAD
        more = narrow - RAD
        old[pl.ds(jnp.where(odd == 0, low, high), more)] = got_outer[wide:]
        old[pl.ds(jnp.where(odd == 0, high, low), more)] = got_mate[wide:]
    mask[...] = jnp.zeros(mask.shape, F32)
    for block in (-1, 0, 1):
        mark_source(mask, jnp.max(packs[block + 1, NT : 2 * NT]).astype(jnp.int32), block, rows)
    for step in range(steps):
        halo = RAD * (steps - 1 - step)
        amounts = [jnp.broadcast_to(packs[i, done + step : done + step + 1], (8, shape[1])) for i in range(3)]

        def extra(x, column):
            place = x - own + rows
            return mask[place, column] * amounts[place // rows]

        def keep(x, column, tile):
            if own <= x < own + rows:
                fields[step, x - own, column] = tile

        advance(cur, old, model, zmat, ymat, own - halo, own + rows + halo, HALO - own, extra, keep)
        if after_step:
            after_step(step, old[own : own + rows])
        cur, old = old, cur
    return cur, old, own


def gather_packs(pack_own, outer, mate, packs):
    odd = parity()
    packs[2 * odd] = outer[outer.shape[0] - 16 :]
    packs[1] = pack_own[...]
    packs[2 - 2 * odd] = mate[mate.shape[0] - 16 :]


def forward_kernel(index, *refs):
    take = 6 if index == 0 else 4
    refs_in, refs = refs[:take], refs[take:]
    zmat, ymat, model, pack, fields, known, send = refs[:7]
    if index == 0:
        packs, buf_a, buf_b, mask = refs[7:]
        gather_packs(pack, refs_in[4], refs_in[5], packs)
    else:
        packs, (buf_a, buf_b, mask) = pack, refs[7:]
    cur, old, own = forward_round(index, refs_in, zmat, ymat, model, packs, fields, buf_a, buf_b, mask)
    rows = 16
    known[0] = old[own - RAD : own]
    known[1] = old[own + rows : own + rows + RAD]
    send[0:rows] = cur[own : own + rows]
    send[rows:] = old[own + RAD : own + rows - RAD]


def split_exactly(values):
    high = values.astype(BF)
    rest = values - high.astype(F32)
    middle = rest.astype(BF)
    return high, middle, (rest - middle.astype(F32)).astype(BF)


def in_send_order(observed, count):
    owners = observed.shape[0]
    per_owner = count // owners
    slot = lax.broadcasted_iota(jnp.int32, (owners, count), 1)
    owner = lax.broadcasted_iota(jnp.int32, (owners, count), 0)
    owned = jnp.where(slot // per_owner == owner, 1.0, 0.0).astype(BF)
    spread = jnp.zeros((NT * per_owner, count), F32)
    for part in split_exactly(observed):
        spread = spread + dot(part, owned, (((0,), (0,)), ((), ())))
    line = lax.broadcasted_iota(jnp.int32, (per_owner, count), 0)
    slot = lax.broadcasted_iota(jnp.int32, (per_owner, count), 1)
    hit = slot % per_owner == line
    out = []
    for step in range(NT):
        part = spread[step * per_owner : (step + 1) * per_owner]
        out.append(jnp.sum(jnp.where(hit, part, 0.0), axis=0, keepdims=True))
    return jnp.concatenate(out, axis=0)


def tables_kernel(count, *refs):
    (cells, observed, *fields), (rows_out, lanes_out, traces) = refs[:-3], refs[-3:]
    rows_table, lane_table = pick_tables(cells[0:1].astype(jnp.int32), rows_out.shape[1])
    rows_out[...] = rows_table
    lanes_out[...] = lane_table
    total = jnp.zeros((16, count), F32)
    step = 0
    for group in fields:
        for i in range(group.shape[0]):
            total = total + extract(group[i], step, rows_table, lane_table)
            step += 1
    traces[...] = total[:NT] - in_send_order(observed[...], count)


def last_kernel(index, *refs):
    take = 6 if index == 0 else 4
    refs_in, refs = refs[:take], refs[take:]
    zmat, ymat, model, packs, cells, rows_table, lane_table, traces = refs[:8]
    fields, adj, buf_a, buf_b, mask = refs[8:]
    done = sum(ROUNDS[:index])
    total = [traces[...]]

    def pick(step, field):
        total[0] = total[0] + extract(field, done + step, rows_table[...], lane_table[...])[:NT]

    forward_round(index, refs_in, zmat, ymat, model, packs, fields, buf_a, buf_b, mask, pick)
    adj[0:NT] = total[0]
    adj[NT:] = cells[...]


def source_planes(rows_table, lane_table, amounts, span_z):
    tiles = split(jnp.broadcast_to(amounts, (16, amounts.shape[1])))
    both = jnp.concatenate(
        [lane_table[z : z + 16] * tile for tile in tiles for z in range(0, span_z, 16)], axis=0
    )
    added = dot(rows_table, both, (((1,), (1,)), ((), ())))
    return added[:, :span_z] + added[:, span_z:]


def injection_lanes(cells, span_z):
    sub = lax.broadcasted_iota(jnp.int32, (span_z, cells.shape[1]), 0)
    return jnp.where(sub == cells % span_z, 1.0, 0.0).astype(BF)


def injection_table(cells, table_rows, span_z):
    sub = lax.broadcasted_iota(jnp.int32, (table_rows, cells.shape[1]), 0)
    return jnp.where(sub == cells // span_z, 1.0, 0.0).astype(BF)


def own_sources_kernel(adj, out):
    rows, span_y, span_z = out.shape[1:]
    cells = adj[NT : NT + 1].astype(jnp.int32)
    table = injection_table(cells, rows * span_y, span_z)
    lanes = injection_lanes(cells, span_z)
    for step in range(NT):
        added = source_planes(table, lanes, adj[step : step + 1], span_z)
        out[step] = added.reshape(rows, span_y, span_z)


def pair_kernel(adj, mate, out):
    odd = parity()
    out[odd] = adj[...]
    out[1 - odd] = mate[...]


def adjoint_kernel(field_groups, slabs, *refs):
    fields = []
    for ref in refs[:field_groups]:
        fields += [ref.at[i] for i in range(ref.shape[0])]
    refs = refs[field_groups:]
    zmat, ymat, model, sources, own_pair, even_pair, odd_pair = refs[:7]
    outs = refs[7 : 7 + slabs]
    buf_a, buf_b, planes, image, rows_table, adjs, near = refs[7 + slabs :]
    odd = parity()
    odd_chip = lax.rem(lax.axis_index("shot") // 2, 2)
    near[2:4] = own_pair[...]
    near[pl.ds(4 - 4 * odd_chip, 2)] = even_pair[...]
    near[pl.ds(4 * odd_chip, 2)] = odd_pair[...]
    rows = 16
    own = HALO
    span_y, span_z = buf_a.shape[1:]
    table_rows = rows * span_y
    lanes = {}
    for block in (-2, -1, 1, 2):
        adjs[block + 2] = near[2 + odd + block]
        cells = adjs[block + 2, NT : NT + 1].astype(jnp.int32)
        rows_table[block + 2] = injection_table(cells, table_rows, span_z)
        lanes[block] = injection_lanes(cells, span_z)

    def place_sources(number, out):
        halo = RAD * (NT - number)
        step = NT - number
        for block in (-2, -1, 1, 2):
            begin = own + block * rows
            first = max(begin, own - halo)
            last = min(begin + rows, own + rows + halo)
            if first >= last:
                continue
            table = rows_table[block + 2, (first - begin) * span_y : (last - begin) * span_y, :]
            added = source_planes(table, lanes[block], adjs[block + 2, step : step + 1], span_z)
            out[first:last] = added.reshape(last - first, span_y, span_z)

    cur, old = buf_a, buf_b
    place_sources(1, cur)
    cur[own : own + rows] = sources[NT - 1]
    old[...] = jnp.zeros(old.shape, F32)
    image[...] = sources[NT - 1] * fields[NT - 1][...]
    for number in range(2, NT + 1):
        halo = RAD * (NT - number)
        step = NT - number
        place_sources(number, planes)

        def extra(x, column):
            return sources[step, x - own, column] if own <= x < own + rows else planes[x, column]

        def keep(x, column, tile):
            if own <= x < own + rows:
                image[x - own, column] = image[x - own, column] + tile * fields[step][x - own, column]

        advance(cur, old, model, zmat, ymat, own - halo, own + rows + halo, 0, extra, keep)
        cur, old = old, cur
    mine = lax.axis_index("shot") // PIECES
    thick = rows // slabs
    for i in range(slabs):
        outs[i][...] = image[pl.ds((mine ^ i) * thick, thick)]


def call(kernel, outs, ins, specs=None, scratch=(), cost=(1e6, 1e6), name=None):
    return pl.pallas_call(
        kernel,
        out_shape=outs,
        in_specs=specs or [VMEM] * len(ins),
        out_specs=jax.tree.map(lambda _: VMEM, outs),
        scratch_shapes=list(scratch),
        compiler_params=pltpu.CompilerParams(vmem_limit_bytes=48 * 1024 * 1024),
        cost_estimate=pl.CostEstimate(flops=int(cost[0]), bytes_accessed=int(cost[1]), transcendentals=0),
        name=name,
    )(*ins)


def swapped(value, partner):
    count = lax.axis_size("shot")
    return lax.ppermute(value, "shot", [(d, partner(d) % count) for d in range(count)])


def with_mate(value):
    return swapped(value, lambda d: d ^ 1)


def with_outer(value):
    return swapped(value, lambda d: d + 1 if d % 2 else d - 1)


def with_even_pair(value):
    return swapped(value, lambda d: d ^ 2)


def with_odd_pair(value):
    return swapped(value, lambda d: d + 2 if d % 4 >= 2 else d - 2)


def per_device(
    courant_sq, wave_now, wave_before, wavelet, source_cell, receiver_cell, send_order, observed
):
    devices = lax.axis_size("shot")
    rows, span_y, span_z = wave_now.shape
    count = receiver_cell.shape[0]
    table_rows = rows * span_y
    plane = (span_y, span_z)

    narrow = RAD * (ROUNDS[0] - 1)
    now_mate, now_outer = with_mate(wave_now), with_outer(wave_now)
    message = jax.ShapeDtypeStruct((narrow * span_y + 16, span_z), F32)
    to_outer, to_mate, pack, before = call(
        message_kernel,
        (message, message, jax.ShapeDtypeStruct((16, span_z), F32), jax.ShapeDtypeStruct(wave_before.shape, F32)),
        (wave_before, wavelet, source_cell),
        specs=[VMEM, SMEM, SMEM],
        name="message",
    )
    before_outer, before_mate = with_outer(to_outer), with_mate(to_mate)

    table = jnp.concatenate([receiver_cell, send_order]).reshape(1, 2 * count)
    model, cells, observed, now, ymat, zmat = call(
        prepare_kernel,
        (
            jax.ShapeDtypeStruct((rows + 2 * HALO,) + plane, F32),
            jax.ShapeDtypeStruct((8, count), F32),
            jax.ShapeDtypeStruct(observed.shape, F32),
            jax.ShapeDtypeStruct(wave_now.shape, F32),
            jax.ShapeDtypeStruct((GROUP * span_y, GROUP * span_y), BF),
            jax.ShapeDtypeStruct((2 * span_z, 2 * span_z), BF),
        ),
        (courant_sq, table, observed, pack, wave_now),
        name="prepare",
    )
    recorded = lax.all_to_all(observed, "shot", split_axis=0, concat_axis=0, tiled=True)

    common = (zmat, ymat, model)
    field_list = []
    ins = (now, before, now_mate, now_outer, before_outer, before_mate)
    for index in range(len(ROUNDS) - 1):
        window = rows + 2 * RAD * ROUNDS[index]
        sent = 2 * rows - 2 * RAD
        packs = (jax.ShapeDtypeStruct((3, 16, span_z), F32),) if index == 0 else ()
        fields, known, send, *made = call(
            functools.partial(forward_kernel, index),
            (
                jax.ShapeDtypeStruct((ROUNDS[index], rows) + plane, F32),
                jax.ShapeDtypeStruct((2, RAD) + plane, F32),
                jax.ShapeDtypeStruct((sent,) + plane, F32),
            )
            + packs,
            ins + common + (pack,),
            scratch=[pltpu.VMEM((window,) + plane, F32)] * 2 + [pltpu.VMEM((3 * rows,) + plane, F32)],
            name="forward",
        )
        field_list.append(fields)
        pack = made[0] if made else pack
        got_mate, got_outer = with_mate(send), with_outer(send)
        ins = (fields, known, got_mate, got_outer)

    rows_table, lane_table, traces = call(
        functools.partial(tables_kernel, count),
        (
            jax.ShapeDtypeStruct((count, table_rows), BF),
            jax.ShapeDtypeStruct((count, 256), F32),
            jax.ShapeDtypeStruct((NT, count), F32),
        ),
        (cells, recorded, *field_list),
        name="traces",
    )
    index = len(ROUNDS) - 1
    window = rows + 2 * RAD * ROUNDS[index]
    fields, adj = call(
        functools.partial(last_kernel, index),
        (
            jax.ShapeDtypeStruct((ROUNDS[index], rows) + plane, F32),
            jax.ShapeDtypeStruct((2 * NT, count), F32),
        ),
        ins + common + (pack, cells, rows_table, lane_table, traces),
        scratch=[pltpu.VMEM((window,) + plane, F32)] * 2 + [pltpu.VMEM((3 * rows,) + plane, F32)],
        name="forward_last",
    )
    field_list.append(fields)

    sources = call(
        own_sources_kernel, jax.ShapeDtypeStruct((NT, rows) + plane, F32), (adj,), name="own_sources"
    )
    pair = call(
        pair_kernel, jax.ShapeDtypeStruct((2, 2 * NT, count), F32), (adj, with_mate(adj)), name="pair"
    )
    adjs = [sources, pair, with_even_pair(pair), with_odd_pair(pair)]
    slabs = devices // PIECES
    thick = rows // slabs
    parts = call(
        functools.partial(adjoint_kernel, len(field_list), slabs),
        tuple(jax.ShapeDtypeStruct((thick,) + plane, F32) for _ in range(slabs)),
        (*field_list, zmat, ymat, model, *adjs),
        scratch=[pltpu.VMEM((rows + 2 * HALO,) + plane, F32)] * 3
        + [pltpu.VMEM((rows,) + plane, F32), pltpu.VMEM((5, table_rows, count), BF)]
        + [pltpu.VMEM((5, 2 * NT, count), F32), pltpu.VMEM((6, 2 * NT, count), F32)],
        name="adjoint",
    )
    total = parts[0]
    for i in [*range(2, slabs), 1]:
        total = total + swapped(parts[i], lambda d: d ^ (i * PIECES))
    return total


def solution(mesh):
    return jax.shard_map(
        per_device,
        mesh=mesh,
        in_specs=(
            P("groups", None, None),
            P(("groups", "shot"), None, None),
            P(("groups", "shot"), None, None),
            P(("groups", "shot"), None),
            P(("groups", "shot")),
            P(("groups", "shot")),
            P(("groups", "shot")),
            P(("groups", "shot"), None),
        ),
        out_specs=P(("groups", "shot"), None, None),
        check_vma=False,
    )
```

```python
import functools

import jax
import jax.numpy as jnp
from jax import lax
from jax.experimental import pallas as pl
from jax.experimental.pallas import tpu as pltpu
from jax.sharding import PartitionSpec as P

NT = 8
PIECES = 4
RAD = 4
ROUNDS = (4, 4)
SCALE = 5040.0
CENTER_Y = -43008.0
CENTER_Z = -42.0
WEIGHTS = (8064.0, -1008.0, 128.0, -9.0)
GROUP = 8
HALO = RAD * (NT - 1)
BF = jnp.bfloat16
F32 = jnp.float32

VMEM = pl.BlockSpec(memory_space=pltpu.VMEM)
SMEM = pl.BlockSpec(memory_space=pltpu.SMEM)


def band(distance, center):
    out = jnp.where(distance == 0, center, 0.0)
    for k, weight in enumerate(WEIGHTS, 1):
        out = jnp.where(jnp.abs(distance) == k, weight, out)
    return out


def build_bands(span_y, span_z, rows_out, fixed_out):
    size = GROUP * span_y
    row = lax.broadcasted_iota(jnp.int32, (size, size), 0)
    col = lax.broadcasted_iota(jnp.int32, (size, size), 1)
    tile = 8 * GROUP
    y_row = row // tile * 8 + row % 8
    y_col = col // tile * 8 + col % 8
    x_far = (row // 8) % GROUP - (col // 8) % GROUP
    y_far = y_row - y_col
    across = jnp.where(y_far == 0, band(x_far, 0.0), 0.0)
    rows_out[...] = jnp.where(x_far == 0, band(y_far, CENTER_Y), across).astype(BF)
    z = lax.broadcasted_iota(jnp.int32, (2 * span_z, 2 * span_z), 0) % span_z
    to = lax.broadcasted_iota(jnp.int32, (2 * span_z, 2 * span_z), 1)
    fixed_out[...] = jnp.where(to < span_z, band(z - to, CENTER_Z), 0.0).astype(BF)


def split(values):
    high = values.astype(BF)
    low = (values - high.astype(F32)).astype(BF)
    return high, low


def dot(a, b, dims=(((1,), (0,)), ((), ()))):
    return lax.dot_general(a, b, dims, preferred_element_type=F32)


def advance(cur, old, model, zmat, ymat, first, last, model_shift, extra, keep):
    span_y, span_z = cur.shape[1:]
    zmat, ymat = zmat[...], ymat[...]
    for base in range(first, last, GROUP):
        columns = [slice(j, j + 8) for j in range(0, span_y, 8)]
        order = [(i, column) for column in columns for i in range(GROUP)]
        group = jnp.concatenate([cur[base + i, column] for i, column in order], axis=0)
        pair = jnp.concatenate(split(group), axis=1)
        left = jnp.concatenate([ymat, pair], axis=1)
        right = jnp.concatenate([pair, zmat], axis=0)
        part = dot(left, right)
        for j, column in enumerate(columns):
            tiles = [cur[base - RAD + q, column] for q in range(GROUP + 2 * RAD)]
            for i in range(GROUP):
                x = base + i
                at = (j * GROUP + i) * 8
                rows = slice(at, at + 8)
                here = tiles[i + RAD]
                total = part[rows, :span_z] + part[rows, span_z:]
                for k, weight in enumerate(WEIGHTS, 1):
                    if i + k >= GROUP:
                        total = total + weight * tiles[i + RAD + k]
                    if i < k:
                        total = total + weight * tiles[i + RAD - k]
                tile = (here + here - old[x, column]) + model[x + model_shift, column] * total + extra(x, column)
                old[x, column] = tile
                keep(x, column, tile)


def mark_source(mask, cell, block, rows):
    span_y, span_z = mask.shape[1:]
    plane = (1 + block) * rows + cell // (span_y * span_z)
    y = (cell // span_z) % span_y
    tile = pl.ds(pl.multiple_of((y // 8) * 8, 8), 8)
    sub = lax.broadcasted_iota(jnp.int32, (8, span_z), 0)
    lane = lax.broadcasted_iota(jnp.int32, (8, span_z), 1)
    mask[plane, tile, :] = jnp.where((sub == y % 8) & (lane == cell % span_z), 1.0, 0.0)


def parity():
    return lax.rem(lax.axis_index("shot"), 2)


def message_kernel(before, wavelet, source, outer_out, mate_out, pack_out, before_out):
    rows, span_y, span_z = before.shape
    which = lax.broadcasted_iota(jnp.int32, (16, span_z), 0)
    pack = jnp.where(which >= NT, source[0].astype(F32), 0.0)
    for step in range(NT):
        pack = jnp.where(which == step, wavelet[0, step], pack)
    pack_out[...] = pack
    before_out[...] = before[...]
    narrow = RAD * (ROUNDS[0] - 1)
    size = narrow * span_y
    odd = parity()
    outer_out[:size] = before[pl.ds(odd * (rows - narrow), narrow)].reshape(size, span_z)
    mate_out[:size] = before[pl.ds((1 - odd) * (rows - narrow), narrow)].reshape(size, span_z)
    outer_out[size:] = pack
    mate_out[size:] = pack


def prepare_kernel(courant, table, pack, now, model_out, cells_out, now_out, ymat_out, zmat_out):
    rows, span_y, span_z = now.shape
    now_out[...] = now[...]
    build_bands(span_y, span_z, ymat_out, zmat_out)
    piece = lax.rem(lax.axis_index("shot"), PIECES)
    period = courant.shape[0]
    window = model_out.shape[0]
    for chunk in range(0, window, RAD):
        source = lax.rem(piece * rows - HALO + chunk + period, period)
        model_out[chunk : chunk + RAD] = courant[pl.ds(source, RAD)] * (1.0 / SCALE)
    count = cells_out.shape[1]
    cell = table[:, :count]
    wanted = table[:, count:]
    which = lax.broadcasted_iota(jnp.int32, (16, count), 0)
    digits = jnp.where(which == 0, cell // 256, jnp.where(which == 1, cell % 256, 0)).astype(F32).astype(BF)
    for j in range(0, count, 256):
        index = lax.broadcasted_iota(jnp.int32, (count, 256), 0)
        chosen = jnp.where(index == wanted[:, j : j + 256], 1.0, 0.0).astype(BF)
        found = dot(digits, chosen)
        ordered = found[0:1] * 256.0 + found[1:2]
        cells_out[:, j : j + 256] = jnp.broadcast_to(ordered, (8, 256))


def pick_tables(cells, table_rows):
    count = cells.shape[1]
    column = jnp.transpose(jnp.broadcast_to(cells.astype(F32), (128, count)))
    column = column.astype(jnp.int32)
    row_of = jnp.concatenate([column // 128] * (table_rows // 128), axis=1)
    lane_of = jnp.concatenate([column % 128] * 2, axis=1)
    lanes = lax.broadcasted_iota(jnp.int32, (count, table_rows), 1)
    rows_table = jnp.where(row_of == lanes, 1.0, 0.0).astype(BF)
    lanes2 = lax.broadcasted_iota(jnp.int32, (count, 256), 1) % 128
    lane_table = jnp.where(lane_of == lanes2, 1.0, 0.0)
    return rows_table, lane_table


def extract(field, step, rows_table, lane_table):
    rows, span_y, span_z = field.shape
    pair = jnp.concatenate(split(field.reshape(rows * span_y, span_z)), axis=1)
    which = lax.broadcasted_iota(jnp.int32, (16, 2 * span_z), 0)
    ones = jnp.where(which == step, 1.0, 0.0).astype(BF)
    out = []
    for j in range(0, rows_table.shape[0], 256):
        found = dot(rows_table[j : j + 256], pair)
        kept = (found * lane_table[j : j + 256]).astype(BF)
        out.append(dot(ones, kept, (((1,), (1,)), ((), ()))))
    return jnp.concatenate(out, axis=1)


def forward_round(
    index, refs_in, zmat, ymat, model, packs, fields, buf_a, buf_b, mask, after_step=None
):
    steps = ROUNDS[index]
    done = sum(ROUNDS[:index])
    rows = 16
    own = RAD * steps
    cur, old = buf_a, buf_b
    wide, narrow = RAD * steps, RAD * (steps - 1)
    odd = parity()
    shape = cur.shape[1:]
    low, high = own - wide, own + rows
    cur_outer = jnp.where(odd == 0, low, high)
    cur_mate = jnp.where(odd == 0, high, low)
    if index == 0:
        now, before, now_mate, now_outer, before_outer, before_mate = refs_in
        cur[own : own + rows] = now[...]
        old[own : own + rows] = before[...]
        cur[pl.ds(cur_outer, wide)] = now_outer[...]
        cur[pl.ds(cur_mate, wide)] = now_mate[...]
        size = narrow * shape[0]
        low = own - narrow
        old[pl.ds(jnp.where(odd == 0, low, high), narrow)] = before_outer[:size].reshape((narrow,) + shape)
        old[pl.ds(jnp.where(odd == 0, high, low), narrow)] = before_mate[:size].reshape((narrow,) + shape)
    else:
        earlier, known, got_mate, got_outer = refs_in
        cur[own : own + rows] = earlier[earlier.shape[0] - 1]
        old[own : own + rows] = earlier[earlier.shape[0] - 2]
        cur[pl.ds(cur_outer, wide)] = got_outer[0:wide]
        cur[pl.ds(cur_mate, wide)] = got_mate[0:wide]
        old[own - RAD : own] = known[0]
        old[own + rows : own + rows + RAD] = known[1]
        low, high = own - narrow, own + rows + RAD
        more = narrow - RAD
        old[pl.ds(jnp.where(odd == 0, low, high), more)] = got_outer[wide:]
        old[pl.ds(jnp.where(odd == 0, high, low), more)] = got_mate[wide:]
    mask[...] = jnp.zeros(mask.shape, F32)
    for block in (-1, 0, 1):
        mark_source(mask, jnp.max(packs[block + 1, NT : 2 * NT]).astype(jnp.int32), block, rows)
    for step in range(steps):
        halo = RAD * (steps - 1 - step)
        amounts = [jnp.broadcast_to(packs[i, done + step : done + step + 1], (8, shape[1])) for i in range(3)]

        def extra(x, column):
            place = x - own + rows
            return mask[place, column] * amounts[place // rows]

        def keep(x, column, tile):
            if own <= x < own + rows:
                fields[step, x - own, column] = tile

        advance(cur, old, model, zmat, ymat, own - halo, own + rows + halo, HALO - own, extra, keep)
        if after_step:
            after_step(step, old[own : own + rows])
        cur, old = old, cur
    return cur, old, own


def gather_packs(pack_own, outer, mate, packs):
    odd = parity()
    packs[2 * odd] = outer[outer.shape[0] - 16 :]
    packs[1] = pack_own[...]
    packs[2 - 2 * odd] = mate[mate.shape[0] - 16 :]


def forward_kernel(index, *refs):
    take = 6 if index == 0 else 4
    refs_in, refs = refs[:take], refs[take:]
    zmat, ymat, model, pack, fields, known, send = refs[:7]
    if index == 0:
        packs, buf_a, buf_b, mask = refs[7:]
        gather_packs(pack, refs_in[4], refs_in[5], packs)
    else:
        packs, (buf_a, buf_b, mask) = pack, refs[7:]
    cur, old, own = forward_round(index, refs_in, zmat, ymat, model, packs, fields, buf_a, buf_b, mask)
    rows = 16
    known[0] = old[own - RAD : own]
    known[1] = old[own + rows : own + rows + RAD]
    send[0:rows] = cur[own : own + rows]
    send[rows:] = old[own + RAD : own + rows - RAD]


def split_exactly(values):
    high = values.astype(BF)
    rest = values - high.astype(F32)
    middle = rest.astype(BF)
    return high, middle, (rest - middle.astype(F32)).astype(BF)


def in_send_order(observed, count):
    owners = observed.shape[0]
    per_owner = count // owners
    slot = lax.broadcasted_iota(jnp.int32, (owners, count), 1)
    owner = lax.broadcasted_iota(jnp.int32, (owners, count), 0)
    owned = jnp.where(slot // per_owner == owner, 1.0, 0.0).astype(BF)
    spread = jnp.zeros((NT * per_owner, count), F32)
    for part in split_exactly(observed):
        spread = spread + dot(part, owned, (((0,), (0,)), ((), ())))
    line = lax.broadcasted_iota(jnp.int32, (per_owner, count), 0)
    slot = lax.broadcasted_iota(jnp.int32, (per_owner, count), 1)
    hit = slot % per_owner == line
    out = []
    for step in range(NT):
        part = spread[step * per_owner : (step + 1) * per_owner]
        out.append(jnp.sum(jnp.where(hit, part, 0.0), axis=0, keepdims=True))
    return jnp.concatenate(out, axis=0)


def tables_kernel(count, *refs):
    (cells, observed, *fields), (rows_out, lanes_out, traces) = refs[:-3], refs[-3:]
    rows_table, lane_table = pick_tables(cells[0:1].astype(jnp.int32), rows_out.shape[1])
    rows_out[...] = rows_table
    lanes_out[...] = lane_table
    total = jnp.zeros((16, count), F32)
    step = 0
    for group in fields:
        for i in range(group.shape[0]):
            total = total + extract(group[i], step, rows_table, lane_table)
            step += 1
    traces[...] = total[:NT] - in_send_order(observed[...], count)


def last_kernel(index, *refs):
    take = 6 if index == 0 else 4
    refs_in, refs = refs[:take], refs[take:]
    zmat, ymat, model, packs, cells, rows_table, lane_table, traces = refs[:8]
    fields, adj, buf_a, buf_b, mask = refs[8:]
    done = sum(ROUNDS[:index])
    total = [traces[...]]

    def pick(step, field):
        total[0] = total[0] + extract(field, done + step, rows_table[...], lane_table[...])[:NT]

    forward_round(index, refs_in, zmat, ymat, model, packs, fields, buf_a, buf_b, mask, pick)
    adj[0:NT] = total[0]
    adj[NT:] = cells[...]


def source_planes(rows_table, lane_table, amounts, span_z):
    tiles = split(jnp.broadcast_to(amounts, (16, amounts.shape[1])))
    both = jnp.concatenate(
        [lane_table[z : z + 16] * tile for tile in tiles for z in range(0, span_z, 16)], axis=0
    )
    added = dot(rows_table, both, (((1,), (1,)), ((), ())))
    return added[:, :span_z] + added[:, span_z:]


def injection_lanes(cells, span_z):
    sub = lax.broadcasted_iota(jnp.int32, (span_z, cells.shape[1]), 0)
    return jnp.where(sub == cells % span_z, 1.0, 0.0).astype(BF)


def injection_table(cells, table_rows, span_z):
    sub = lax.broadcasted_iota(jnp.int32, (table_rows, cells.shape[1]), 0)
    return jnp.where(sub == cells // span_z, 1.0, 0.0).astype(BF)


def own_sources_kernel(adj, out):
    rows, span_y, span_z = out.shape[1:]
    cells = adj[NT : NT + 1].astype(jnp.int32)
    table = injection_table(cells, rows * span_y, span_z)
    lanes = injection_lanes(cells, span_z)
    for step in range(NT):
        added = source_planes(table, lanes, adj[step : step + 1], span_z)
        out[step] = added.reshape(rows, span_y, span_z)


def pair_kernel(adj, mate, out):
    odd = parity()
    out[odd] = adj[...]
    out[1 - odd] = mate[...]


def adjoint_kernel(field_groups, slabs, *refs):
    fields = []
    for ref in refs[:field_groups]:
        fields += [ref.at[i] for i in range(ref.shape[0])]
    refs = refs[field_groups:]
    zmat, ymat, model, sources, own_pair, even_pair, odd_pair = refs[:7]
    outs = refs[7 : 7 + slabs]
    buf_a, buf_b, planes, image, rows_table, adjs, near = refs[7 + slabs :]
    odd = parity()
    odd_chip = lax.rem(lax.axis_index("shot") // 2, 2)
    near[2:4] = own_pair[...]
    near[pl.ds(4 - 4 * odd_chip, 2)] = even_pair[...]
    near[pl.ds(4 * odd_chip, 2)] = odd_pair[...]
    rows = 16
    own = HALO
    span_y, span_z = buf_a.shape[1:]
    table_rows = rows * span_y
    lanes = {}
    for block in (-2, -1, 1, 2):
        adjs[block + 2] = near[2 + odd + block]
        cells = adjs[block + 2, NT : NT + 1].astype(jnp.int32)
        rows_table[block + 2] = injection_table(cells, table_rows, span_z)
        lanes[block] = injection_lanes(cells, span_z)

    def place_sources(number, out):
        halo = RAD * (NT - number)
        step = NT - number
        for block in (-2, -1, 1, 2):
            begin = own + block * rows
            first = max(begin, own - halo)
            last = min(begin + rows, own + rows + halo)
            if first >= last:
                continue
            table = rows_table[block + 2, (first - begin) * span_y : (last - begin) * span_y, :]
            added = source_planes(table, lanes[block], adjs[block + 2, step : step + 1], span_z)
            out[first:last] = added.reshape(last - first, span_y, span_z)

    cur, old = buf_a, buf_b
    place_sources(1, cur)
    cur[own : own + rows] = sources[NT - 1]
    old[...] = jnp.zeros(old.shape, F32)
    image[...] = sources[NT - 1] * fields[NT - 1][...]
    for number in range(2, NT + 1):
        halo = RAD * (NT - number)
        step = NT - number
        place_sources(number, planes)

        def extra(x, column):
            return sources[step, x - own, column] if own <= x < own + rows else planes[x, column]

        def keep(x, column, tile):
            if own <= x < own + rows:
                image[x - own, column] = image[x - own, column] + tile * fields[step][x - own, column]

        advance(cur, old, model, zmat, ymat, own - halo, own + rows + halo, 0, extra, keep)
        cur, old = old, cur
    mine = lax.axis_index("shot") // PIECES
    thick = rows // slabs
    for i in range(slabs):
        outs[i][...] = image[pl.ds((mine ^ i) * thick, thick)]


def call(kernel, outs, ins, specs=None, scratch=(), cost=(1e6, 1e6), name=None):
    return pl.pallas_call(
        kernel,
        out_shape=outs,
        in_specs=specs or [VMEM] * len(ins),
        out_specs=jax.tree.map(lambda _: VMEM, outs),
        scratch_shapes=list(scratch),
        compiler_params=pltpu.CompilerParams(vmem_limit_bytes=48 * 1024 * 1024),
        cost_estimate=pl.CostEstimate(flops=int(cost[0]), bytes_accessed=int(cost[1]), transcendentals=0),
        name=name,
    )(*ins)


def swapped(value, partner):
    count = lax.axis_size("shot")
    return lax.ppermute(value, "shot", [(d, partner(d) % count) for d in range(count)])


def with_mate(value):
    return swapped(value, lambda d: d ^ 1)


def with_outer(value):
    return swapped(value, lambda d: d + 1 if d % 2 else d - 1)


def with_even_pair(value):
    return swapped(value, lambda d: d ^ 2)


def with_odd_pair(value):
    return swapped(value, lambda d: d + 2 if d % 4 >= 2 else d - 2)


def per_device(
    courant_sq, wave_now, wave_before, wavelet, source_cell, receiver_cell, send_order, observed
):
    devices = lax.axis_size("shot")
    rows, span_y, span_z = wave_now.shape
    count = receiver_cell.shape[0]
    table_rows = rows * span_y
    plane = (span_y, span_z)

    narrow = RAD * (ROUNDS[0] - 1)
    now_mate, now_outer = with_mate(wave_now), with_outer(wave_now)
    message = jax.ShapeDtypeStruct((narrow * span_y + 16, span_z), F32)
    to_outer, to_mate, pack, before = call(
        message_kernel,
        (message, message, jax.ShapeDtypeStruct((16, span_z), F32), jax.ShapeDtypeStruct(wave_before.shape, F32)),
        (wave_before, wavelet, source_cell),
        specs=[VMEM, SMEM, SMEM],
        name="message",
    )
    before_outer, before_mate = with_outer(to_outer), with_mate(to_mate)

    table = jnp.concatenate([receiver_cell, send_order]).reshape(1, 2 * count)
    model, cells, now, ymat, zmat = call(
        prepare_kernel,
        (
            jax.ShapeDtypeStruct((rows + 2 * HALO,) + plane, F32),
            jax.ShapeDtypeStruct((8, count), F32),
            jax.ShapeDtypeStruct(wave_now.shape, F32),
            jax.ShapeDtypeStruct((GROUP * span_y, GROUP * span_y), BF),
            jax.ShapeDtypeStruct((2 * span_z, 2 * span_z), BF),
        ),
        (courant_sq, table, pack, wave_now),
        name="prepare",
    )
    recorded = lax.all_to_all(observed, "shot", split_axis=0, concat_axis=0, tiled=True)

    common = (zmat, ymat, model)
    field_list = []
    ins = (now, before, now_mate, now_outer, before_outer, before_mate)
    for index in range(len(ROUNDS) - 1):
        window = rows + 2 * RAD * ROUNDS[index]
        sent = 2 * rows - 2 * RAD
        packs = (jax.ShapeDtypeStruct((3, 16, span_z), F32),) if index == 0 else ()
        fields, known, send, *made = call(
            functools.partial(forward_kernel, index),
            (
                jax.ShapeDtypeStruct((ROUNDS[index], rows) + plane, F32),
                jax.ShapeDtypeStruct((2, RAD) + plane, F32),
                jax.ShapeDtypeStruct((sent,) + plane, F32),
            )
            + packs,
            ins + common + (pack,),
            scratch=[pltpu.VMEM((window,) + plane, F32)] * 2 + [pltpu.VMEM((3 * rows,) + plane, F32)],
            name="forward",
        )
        field_list.append(fields)
        pack = made[0] if made else pack
        got_mate, got_outer = with_mate(send), with_outer(send)
        ins = (fields, known, got_mate, got_outer)

    rows_table, lane_table, traces = call(
        functools.partial(tables_kernel, count),
        (
            jax.ShapeDtypeStruct((count, table_rows), BF),
            jax.ShapeDtypeStruct((count, 256), F32),
            jax.ShapeDtypeStruct((NT, count), F32),
        ),
        (cells, recorded, *field_list),
        name="traces",
    )
    index = len(ROUNDS) - 1
    window = rows + 2 * RAD * ROUNDS[index]
    fields, adj = call(
        functools.partial(last_kernel, index),
        (
            jax.ShapeDtypeStruct((ROUNDS[index], rows) + plane, F32),
            jax.ShapeDtypeStruct((2 * NT, count), F32),
        ),
        ins + common + (pack, cells, rows_table, lane_table, traces),
        scratch=[pltpu.VMEM((window,) + plane, F32)] * 2 + [pltpu.VMEM((3 * rows,) + plane, F32)],
        name="forward_last",
    )
    field_list.append(fields)

    sources = call(
        own_sources_kernel, jax.ShapeDtypeStruct((NT, rows) + plane, F32), (adj,), name="own_sources"
    )
    pair = call(
        pair_kernel, jax.ShapeDtypeStruct((2, 2 * NT, count), F32), (adj, with_mate(adj)), name="pair"
    )
    adjs = [sources, pair, with_even_pair(pair), with_odd_pair(pair)]
    slabs = devices // PIECES
    thick = rows // slabs
    parts = call(
        functools.partial(adjoint_kernel, len(field_list), slabs),
        tuple(jax.ShapeDtypeStruct((thick,) + plane, F32) for _ in range(slabs)),
        (*field_list, zmat, ymat, model, *adjs),
        scratch=[pltpu.VMEM((rows + 2 * HALO,) + plane, F32)] * 3
        + [pltpu.VMEM((rows,) + plane, F32), pltpu.VMEM((5, table_rows, count), BF)]
        + [pltpu.VMEM((5, 2 * NT, count), F32), pltpu.VMEM((6, 2 * NT, count), F32)],
        name="adjoint",
    )
    total = parts[0]
    for i in [*range(2, slabs), 1]:
        total = total + swapped(parts[i], lambda d: d ^ (i * PIECES))
    return total


def solution(mesh):
    return jax.shard_map(
        per_device,
        mesh=mesh,
        in_specs=(
            P("groups", None, None),
            P(("groups", "shot"), None, None),
            P(("groups", "shot"), None, None),
            P(("groups", "shot"), None),
            P(("groups", "shot")),
            P(("groups", "shot")),
            P(("groups", "shot")),
            P(("groups", "shot"), None),
        ),
        out_specs=P(("groups", "shot"), None, None),
        check_vma=False,
    )
```

```python
import functools

import jax
import jax.numpy as jnp
from jax import lax
from jax.experimental import pallas as pl
from jax.experimental.pallas import tpu as pltpu
from jax.sharding import PartitionSpec as P

NT = 8
PIECES = 4
RAD = 4
ROUNDS = (4, 4)
SCALE = 5040.0
CENTER_Y = -43008.0
CENTER_Z = -42.0
WEIGHTS = (8064.0, -1008.0, 128.0, -9.0)
GROUP = 8
HALO = RAD * (NT - 1)
BF = jnp.bfloat16
F32 = jnp.float32

VMEM = pl.BlockSpec(memory_space=pltpu.VMEM)
SMEM = pl.BlockSpec(memory_space=pltpu.SMEM)


def band(distance, center):
    out = jnp.where(distance == 0, center, 0.0)
    for k, weight in enumerate(WEIGHTS, 1):
        out = jnp.where(jnp.abs(distance) == k, weight, out)
    return out


def build_bands(span_y, span_z, rows_out, fixed_out):
    size = GROUP * span_y
    row = lax.broadcasted_iota(jnp.int32, (size, size), 0)
    col = lax.broadcasted_iota(jnp.int32, (size, size), 1)
    tile = 8 * GROUP
    y_row = row // tile * 8 + row % 8
    y_col = col // tile * 8 + col % 8
    x_far = (row // 8) % GROUP - (col // 8) % GROUP
    y_far = y_row - y_col
    across = jnp.where(y_far == 0, band(x_far, 0.0), 0.0)
    rows_out[...] = jnp.where(x_far == 0, band(y_far, CENTER_Y), across).astype(BF)
    z = lax.broadcasted_iota(jnp.int32, (2 * span_z, 2 * span_z), 0) % span_z
    to = lax.broadcasted_iota(jnp.int32, (2 * span_z, 2 * span_z), 1)
    fixed_out[...] = jnp.where(to < span_z, band(z - to, CENTER_Z), 0.0).astype(BF)


def split(values):
    high = values.astype(BF)
    low = (values - high.astype(F32)).astype(BF)
    return high, low


def dot(a, b, dims=(((1,), (0,)), ((), ()))):
    return lax.dot_general(a, b, dims, preferred_element_type=F32)


def advance(cur, old, model, zmat, ymat, first, last, model_shift, extra, keep):
    span_y, span_z = cur.shape[1:]
    zmat, ymat = zmat[...], ymat[...]
    for base in range(first, last, GROUP):
        columns = [slice(j, j + 8) for j in range(0, span_y, 8)]
        order = [(i, column) for column in columns for i in range(GROUP)]
        group = jnp.concatenate([cur[base + i, column] for i, column in order], axis=0)
        pair = jnp.concatenate(split(group), axis=1)
        left = jnp.concatenate([ymat, pair], axis=1)
        right = jnp.concatenate([pair, zmat], axis=0)
        part = dot(left, right)
        for j, column in enumerate(columns):
            tiles = [cur[base - RAD + q, column] for q in range(GROUP + 2 * RAD)]
            for i in range(GROUP):
                x = base + i
                at = (j * GROUP + i) * 8
                rows = slice(at, at + 8)
                here = tiles[i + RAD]
                total = part[rows, :span_z] + part[rows, span_z:]
                for k, weight in enumerate(WEIGHTS, 1):
                    if i + k >= GROUP:
                        total = total + weight * tiles[i + RAD + k]
                    if i < k:
                        total = total + weight * tiles[i + RAD - k]
                tile = (here + here - old[x, column]) + model[x + model_shift, column] * total + extra(x, column)
                old[x, column] = tile
                keep(x, column, tile)


def mark_source(mask, cell, block, rows):
    span_y, span_z = mask.shape[1:]
    plane = (1 + block) * rows + cell // (span_y * span_z)
    y = (cell // span_z) % span_y
    tile = pl.ds(pl.multiple_of((y // 8) * 8, 8), 8)
    sub = lax.broadcasted_iota(jnp.int32, (8, span_z), 0)
    lane = lax.broadcasted_iota(jnp.int32, (8, span_z), 1)
    mask[plane, tile, :] = jnp.where((sub == y % 8) & (lane == cell % span_z), 1.0, 0.0)


def parity():
    return lax.rem(lax.axis_index("shot"), 2)


def message_kernel(before, wavelet, source, outer_out, mate_out, pack_out, before_out):
    rows, span_y, span_z = before.shape
    which = lax.broadcasted_iota(jnp.int32, (16, span_z), 0)
    pack = jnp.where(which >= NT, source[0].astype(F32), 0.0)
    for step in range(NT):
        pack = jnp.where(which == step, wavelet[0, step], pack)
    pack_out[...] = pack
    before_out[...] = before[...]
    narrow = RAD * (ROUNDS[0] - 1)
    size = narrow * span_y
    odd = parity()
    outer_out[:size] = before[pl.ds(odd * (rows - narrow), narrow)].reshape(size, span_z)
    mate_out[:size] = before[pl.ds((1 - odd) * (rows - narrow), narrow)].reshape(size, span_z)
    outer_out[size:] = pack
    mate_out[size:] = pack


def prepare_kernel(courant, table, pack, now, model_out, cells_out, now_out, ymat_out, zmat_out):
    rows, span_y, span_z = now.shape
    now_out[...] = now[...]
    build_bands(span_y, span_z, ymat_out, zmat_out)
    piece = lax.rem(lax.axis_index("shot"), PIECES)
    period = courant.shape[0]
    window = model_out.shape[0]
    for chunk in range(0, window, RAD):
        source = lax.rem(piece * rows - HALO + chunk + period, period)
        model_out[chunk : chunk + RAD] = courant[pl.ds(source, RAD)] * (1.0 / SCALE)
    count = cells_out.shape[1]
    cell = table[:, :count]
    wanted = table[:, count:]
    which = lax.broadcasted_iota(jnp.int32, (16, count), 0)
    digits = jnp.where(which == 0, cell // 256, jnp.where(which == 1, cell % 256, 0)).astype(F32).astype(BF)
    for j in range(0, count, 256):
        index = lax.broadcasted_iota(jnp.int32, (count, 256), 0)
        chosen = jnp.where(index == wanted[:, j : j + 256], 1.0, 0.0).astype(BF)
        found = dot(digits, chosen)
        ordered = found[0:1] * 256.0 + found[1:2]
        cells_out[:, j : j + 256] = jnp.broadcast_to(ordered, (8, 256))


def pick_tables(cells, table_rows):
    count = cells.shape[1]
    column = jnp.transpose(jnp.broadcast_to(cells.astype(F32), (128, count)))
    column = column.astype(jnp.int32)
    row_of = jnp.concatenate([column // 128] * (table_rows // 128), axis=1)
    lane_of = jnp.concatenate([column % 128] * 2, axis=1)
    lanes = lax.broadcasted_iota(jnp.int32, (count, table_rows), 1)
    rows_table = jnp.where(row_of == lanes, 1.0, 0.0).astype(BF)
    lanes2 = lax.broadcasted_iota(jnp.int32, (count, 256), 1) % 128
    lane_table = jnp.where(lane_of == lanes2, 1.0, 0.0).astype(BF)
    return rows_table, lane_table


def extract(field, step, rows_table, lane_table):
    rows, span_y, span_z = field.shape
    pair = jnp.concatenate(split(field.reshape(rows * span_y, span_z)), axis=1)
    which = lax.broadcasted_iota(jnp.int32, (16, 2 * span_z), 0)
    ones = jnp.where(which == step, 1.0, 0.0).astype(BF)
    out = []
    for j in range(0, rows_table.shape[0], 256):
        found = dot(rows_table[j : j + 256], pair)
        kept = found.astype(BF) * lane_table[j : j + 256]
        out.append(dot(ones, kept, (((1,), (1,)), ((), ()))))
    return jnp.concatenate(out, axis=1)


def forward_round(
    index, refs_in, zmat, ymat, model, packs, fields, buf_a, buf_b, mask, after_step=None
):
    steps = ROUNDS[index]
    done = sum(ROUNDS[:index])
    rows = 16
    own = RAD * steps
    cur, old = buf_a, buf_b
    wide, narrow = RAD * steps, RAD * (steps - 1)
    odd = parity()
    shape = cur.shape[1:]
    low, high = own - wide, own + rows
    cur_outer = jnp.where(odd == 0, low, high)
    cur_mate = jnp.where(odd == 0, high, low)
    if index == 0:
        now, before, now_mate, now_outer, before_outer, before_mate = refs_in
        cur[own : own + rows] = now[...]
        old[own : own + rows] = before[...]
        cur[pl.ds(cur_outer, wide)] = now_outer[...]
        cur[pl.ds(cur_mate, wide)] = now_mate[...]
        size = narrow * shape[0]
        low = own - narrow
        old[pl.ds(jnp.where(odd == 0, low, high), narrow)] = before_outer[:size].reshape((narrow,) + shape)
        old[pl.ds(jnp.where(odd == 0, high, low), narrow)] = before_mate[:size].reshape((narrow,) + shape)
    else:
        earlier, known, got_mate, got_outer = refs_in
        cur[own : own + rows] = earlier[earlier.shape[0] - 1]
        old[own : own + rows] = earlier[earlier.shape[0] - 2]
        cur[pl.ds(cur_outer, wide)] = got_outer[0:wide]
        cur[pl.ds(cur_mate, wide)] = got_mate[0:wide]
        old[own - RAD : own] = known[0]
        old[own + rows : own + rows + RAD] = known[1]
        low, high = own - narrow, own + rows + RAD
        more = narrow - RAD
        old[pl.ds(jnp.where(odd == 0, low, high), more)] = got_outer[wide:]
        old[pl.ds(jnp.where(odd == 0, high, low), more)] = got_mate[wide:]
    mask[...] = jnp.zeros(mask.shape, F32)
    for block in (-1, 0, 1):
        mark_source(mask, jnp.max(packs[block + 1, NT : 2 * NT]).astype(jnp.int32), block, rows)
    for step in range(steps):
        halo = RAD * (steps - 1 - step)
        amounts = [jnp.broadcast_to(packs[i, done + step : done + step + 1], (8, shape[1])) for i in range(3)]

        def extra(x, column):
            place = x - own + rows
            return mask[place, column] * amounts[place // rows]

        def keep(x, column, tile):
            if own <= x < own + rows:
                fields[step, x - own, column] = tile

        advance(cur, old, model, zmat, ymat, own - halo, own + rows + halo, HALO - own, extra, keep)
        if after_step:
            after_step(step, old[own : own + rows])
        cur, old = old, cur
    return cur, old, own


def gather_packs(pack_own, outer, mate, packs):
    odd = parity()
    packs[2 * odd] = outer[outer.shape[0] - 16 :]
    packs[1] = pack_own[...]
    packs[2 - 2 * odd] = mate[mate.shape[0] - 16 :]


def forward_kernel(index, *refs):
    take = 6 if index == 0 else 4
    refs_in, refs = refs[:take], refs[take:]
    zmat, ymat, model, pack, fields, known, send = refs[:7]
    if index == 0:
        packs, buf_a, buf_b, mask = refs[7:]
        gather_packs(pack, refs_in[4], refs_in[5], packs)
    else:
        packs, (buf_a, buf_b, mask) = pack, refs[7:]
    cur, old, own = forward_round(index, refs_in, zmat, ymat, model, packs, fields, buf_a, buf_b, mask)
    rows = 16
    known[0] = old[own - RAD : own]
    known[1] = old[own + rows : own + rows + RAD]
    send[0:rows] = cur[own : own + rows]
    send[rows:] = old[own + RAD : own + rows - RAD]


def split_exactly(values):
    high = values.astype(BF)
    rest = values - high.astype(F32)
    middle = rest.astype(BF)
    return high, middle, (rest - middle.astype(F32)).astype(BF)


def in_send_order(observed, count):
    owners = observed.shape[0]
    per_owner = count // owners
    slot = lax.broadcasted_iota(jnp.int32, (owners, count), 1)
    owner = lax.broadcasted_iota(jnp.int32, (owners, count), 0)
    owned = jnp.where(slot // per_owner == owner, 1.0, 0.0).astype(BF)
    spread = jnp.zeros((NT * per_owner, count), F32)
    for part in split_exactly(observed):
        spread = spread + dot(part, owned, (((0,), (0,)), ((), ())))
    line = lax.broadcasted_iota(jnp.int32, (per_owner, count), 0)
    slot = lax.broadcasted_iota(jnp.int32, (per_owner, count), 1)
    hit = slot % per_owner == line
    out = []
    for step in range(NT):
        part = spread[step * per_owner : (step + 1) * per_owner]
        out.append(jnp.sum(jnp.where(hit, part, 0.0), axis=0, keepdims=True))
    return jnp.concatenate(out, axis=0)


def tables_kernel(count, *refs):
    (cells, observed, *fields), (rows_out, lanes_out, traces) = refs[:-3], refs[-3:]
    rows_table, lane_table = pick_tables(cells[0:1].astype(jnp.int32), rows_out.shape[1])
    rows_out[...] = rows_table
    lanes_out[...] = lane_table
    total = jnp.zeros((16, count), F32)
    step = 0
    for group in fields:
        for i in range(group.shape[0]):
            total = total + extract(group[i], step, rows_table, lane_table)
            step += 1
    traces[...] = total[:NT] - in_send_order(observed[...], count)


def last_kernel(index, *refs):
    take = 6 if index == 0 else 4
    refs_in, refs = refs[:take], refs[take:]
    zmat, ymat, model, packs, cells, rows_table, lane_table, traces = refs[:8]
    fields, adj, buf_a, buf_b, mask = refs[8:]
    done = sum(ROUNDS[:index])
    total = [traces[...]]

    def pick(step, field):
        total[0] = total[0] + extract(field, done + step, rows_table[...], lane_table[...])[:NT]

    forward_round(index, refs_in, zmat, ymat, model, packs, fields, buf_a, buf_b, mask, pick)
    adj[0:NT] = total[0]
    adj[NT:] = cells[...]


def source_planes(rows_table, lane_table, amounts, span_z):
    tiles = split(jnp.broadcast_to(amounts, (16, amounts.shape[1])))
    both = jnp.concatenate(
        [lane_table[z : z + 16] * tile for tile in tiles for z in range(0, span_z, 16)], axis=0
    )
    added = dot(rows_table, both, (((1,), (1,)), ((), ())))
    return added[:, :span_z] + added[:, span_z:]


def injection_lanes(cells, span_z):
    sub = lax.broadcasted_iota(jnp.int32, (span_z, cells.shape[1]), 0)
    return jnp.where(sub == cells % span_z, 1.0, 0.0).astype(BF)


def injection_table(cells, table_rows, span_z):
    sub = lax.broadcasted_iota(jnp.int32, (table_rows, cells.shape[1]), 0)
    return jnp.where(sub == cells // span_z, 1.0, 0.0).astype(BF)


def own_sources_kernel(adj, out):
    rows, span_y, span_z = out.shape[1:]
    cells = adj[NT : NT + 1].astype(jnp.int32)
    table = injection_table(cells, rows * span_y, span_z)
    lanes = injection_lanes(cells, span_z)
    for step in range(NT):
        added = source_planes(table, lanes, adj[step : step + 1], span_z)
        out[step] = added.reshape(rows, span_y, span_z)


def pair_kernel(adj, mate, out):
    odd = parity()
    out[odd] = adj[...]
    out[1 - odd] = mate[...]


def adjoint_kernel(field_groups, slabs, *refs):
    fields = []
    for ref in refs[:field_groups]:
        fields += [ref.at[i] for i in range(ref.shape[0])]
    refs = refs[field_groups:]
    zmat, ymat, model, sources, own_pair, even_pair, odd_pair = refs[:7]
    outs = refs[7 : 7 + slabs]
    buf_a, buf_b, planes, image, rows_table, adjs, near = refs[7 + slabs :]
    odd = parity()
    odd_chip = lax.rem(lax.axis_index("shot") // 2, 2)
    near[2:4] = own_pair[...]
    near[pl.ds(4 - 4 * odd_chip, 2)] = even_pair[...]
    near[pl.ds(4 * odd_chip, 2)] = odd_pair[...]
    rows = 16
    own = HALO
    span_y, span_z = buf_a.shape[1:]
    table_rows = rows * span_y
    lanes = {}
    for block in (-2, -1, 1, 2):
        adjs[block + 2] = near[2 + odd + block]
        cells = adjs[block + 2, NT : NT + 1].astype(jnp.int32)
        rows_table[block + 2] = injection_table(cells, table_rows, span_z)
        lanes[block] = injection_lanes(cells, span_z)

    def place_sources(number, out):
        halo = RAD * (NT - number)
        step = NT - number
        for block in (-2, -1, 1, 2):
            begin = own + block * rows
            first = max(begin, own - halo)
            last = min(begin + rows, own + rows + halo)
            if first >= last:
                continue
            table = rows_table[block + 2, (first - begin) * span_y : (last - begin) * span_y, :]
            added = source_planes(table, lanes[block], adjs[block + 2, step : step + 1], span_z)
            out[first:last] = added.reshape(last - first, span_y, span_z)

    cur, old = buf_a, buf_b
    place_sources(1, cur)
    cur[own : own + rows] = sources[NT - 1]
    old[...] = jnp.zeros(old.shape, F32)
    image[...] = sources[NT - 1] * fields[NT - 1][...]
    for number in range(2, NT + 1):
        halo = RAD * (NT - number)
        step = NT - number
        place_sources(number, planes)

        def extra(x, column):
            return sources[step, x - own, column] if own <= x < own + rows else planes[x, column]

        def keep(x, column, tile):
            if own <= x < own + rows:
                image[x - own, column] = image[x - own, column] + tile * fields[step][x - own, column]

        advance(cur, old, model, zmat, ymat, own - halo, own + rows + halo, 0, extra, keep)
        cur, old = old, cur
    mine = lax.axis_index("shot") // PIECES
    thick = rows // slabs
    for i in range(slabs):
        outs[i][...] = image[pl.ds((mine ^ i) * thick, thick)]


def call(kernel, outs, ins, specs=None, scratch=(), cost=(1e6, 1e6), name=None):
    return pl.pallas_call(
        kernel,
        out_shape=outs,
        in_specs=specs or [VMEM] * len(ins),
        out_specs=jax.tree.map(lambda _: VMEM, outs),
        scratch_shapes=list(scratch),
        compiler_params=pltpu.CompilerParams(vmem_limit_bytes=48 * 1024 * 1024),
        cost_estimate=pl.CostEstimate(flops=int(cost[0]), bytes_accessed=int(cost[1]), transcendentals=0),
        name=name,
    )(*ins)


def swapped(value, partner):
    count = lax.axis_size("shot")
    return lax.ppermute(value, "shot", [(d, partner(d) % count) for d in range(count)])


def with_mate(value):
    return swapped(value, lambda d: d ^ 1)


def with_outer(value):
    return swapped(value, lambda d: d + 1 if d % 2 else d - 1)


def with_even_pair(value):
    return swapped(value, lambda d: d ^ 2)


def with_odd_pair(value):
    return swapped(value, lambda d: d + 2 if d % 4 >= 2 else d - 2)


def per_device(
    courant_sq, wave_now, wave_before, wavelet, source_cell, receiver_cell, send_order, observed
):
    devices = lax.axis_size("shot")
    rows, span_y, span_z = wave_now.shape
    count = receiver_cell.shape[0]
    table_rows = rows * span_y
    plane = (span_y, span_z)

    narrow = RAD * (ROUNDS[0] - 1)
    now_mate, now_outer = with_mate(wave_now), with_outer(wave_now)
    message = jax.ShapeDtypeStruct((narrow * span_y + 16, span_z), F32)
    to_outer, to_mate, pack, before = call(
        message_kernel,
        (message, message, jax.ShapeDtypeStruct((16, span_z), F32), jax.ShapeDtypeStruct(wave_before.shape, F32)),
        (wave_before, wavelet, source_cell),
        specs=[VMEM, SMEM, SMEM],
        name="message",
    )
    before_outer, before_mate = with_outer(to_outer), with_mate(to_mate)

    table = jnp.concatenate([receiver_cell, send_order]).reshape(1, 2 * count)
    model, cells, now, ymat, zmat = call(
        prepare_kernel,
        (
            jax.ShapeDtypeStruct((rows + 2 * HALO,) + plane, F32),
            jax.ShapeDtypeStruct((8, count), F32),
            jax.ShapeDtypeStruct(wave_now.shape, F32),
            jax.ShapeDtypeStruct((GROUP * span_y, GROUP * span_y), BF),
            jax.ShapeDtypeStruct((2 * span_z, 2 * span_z), BF),
        ),
        (courant_sq, table, pack, wave_now),
        name="prepare",
    )
    recorded = lax.all_to_all(observed, "shot", split_axis=0, concat_axis=0, tiled=True)

    common = (zmat, ymat, model)
    field_list = []
    ins = (now, before, now_mate, now_outer, before_outer, before_mate)
    for index in range(len(ROUNDS) - 1):
        window = rows + 2 * RAD * ROUNDS[index]
        sent = 2 * rows - 2 * RAD
        packs = (jax.ShapeDtypeStruct((3, 16, span_z), F32),) if index == 0 else ()
        fields, known, send, *made = call(
            functools.partial(forward_kernel, index),
            (
                jax.ShapeDtypeStruct((ROUNDS[index], rows) + plane, F32),
                jax.ShapeDtypeStruct((2, RAD) + plane, F32),
                jax.ShapeDtypeStruct((sent,) + plane, F32),
            )
            + packs,
            ins + common + (pack,),
            scratch=[pltpu.VMEM((window,) + plane, F32)] * 2 + [pltpu.VMEM((3 * rows,) + plane, F32)],
            name="forward",
        )
        field_list.append(fields)
        pack = made[0] if made else pack
        got_mate, got_outer = with_mate(send), with_outer(send)
        ins = (fields, known, got_mate, got_outer)

    rows_table, lane_table, traces = call(
        functools.partial(tables_kernel, count),
        (
            jax.ShapeDtypeStruct((count, table_rows), BF),
            jax.ShapeDtypeStruct((count, 256), BF),
            jax.ShapeDtypeStruct((NT, count), F32),
        ),
        (cells, recorded, *field_list),
        name="traces",
    )
    index = len(ROUNDS) - 1
    window = rows + 2 * RAD * ROUNDS[index]
    fields, adj = call(
        functools.partial(last_kernel, index),
        (
            jax.ShapeDtypeStruct((ROUNDS[index], rows) + plane, F32),
            jax.ShapeDtypeStruct((2 * NT, count), F32),
        ),
        ins + common + (pack, cells, rows_table, lane_table, traces),
        scratch=[pltpu.VMEM((window,) + plane, F32)] * 2 + [pltpu.VMEM((3 * rows,) + plane, F32)],
        name="forward_last",
    )
    field_list.append(fields)

    sources = call(
        own_sources_kernel, jax.ShapeDtypeStruct((NT, rows) + plane, F32), (adj,), name="own_sources"
    )
    pair = call(
        pair_kernel, jax.ShapeDtypeStruct((2, 2 * NT, count), F32), (adj, with_mate(adj)), name="pair"
    )
    adjs = [sources, pair, with_even_pair(pair), with_odd_pair(pair)]
    slabs = devices // PIECES
    thick = rows // slabs
    parts = call(
        functools.partial(adjoint_kernel, len(field_list), slabs),
        tuple(jax.ShapeDtypeStruct((thick,) + plane, F32) for _ in range(slabs)),
        (*field_list, zmat, ymat, model, *adjs),
        scratch=[pltpu.VMEM((rows + 2 * HALO,) + plane, F32)] * 3
        + [pltpu.VMEM((rows,) + plane, F32), pltpu.VMEM((5, table_rows, count), BF)]
        + [pltpu.VMEM((5, 2 * NT, count), F32), pltpu.VMEM((6, 2 * NT, count), F32)],
        name="adjoint",
    )
    total = parts[0]
    for i in [*range(2, slabs), 1]:
        total = total + swapped(parts[i], lambda d: d ^ (i * PIECES))
    return total


def solution(mesh):
    return jax.shard_map(
        per_device,
        mesh=mesh,
        in_specs=(
            P("groups", None, None),
            P(("groups", "shot"), None, None),
            P(("groups", "shot"), None, None),
            P(("groups", "shot"), None),
            P(("groups", "shot")),
            P(("groups", "shot")),
            P(("groups", "shot")),
            P(("groups", "shot"), None),
        ),
        out_specs=P(("groups", "shot"), None, None),
        check_vma=False,
    )
```
